128 devices in a mesh: ctx: 8 (over x_lo, y), exp: 16 (over x_hi, z, core).
Axes of the slice: x: 4 (x_hi: 2, x_lo: 2; x = x_hi * 2 + x_lo), y: 4, z: 4, core: 2. Of those that a mesh axis runs over, the one named last changes fastest.
Arguments:
- q_heads: bfloat16 [8192, 2048], P('ctx', 'exp'), may hold values from -5 to 5
- k_heads: bfloat16 [8192, 2048], P('ctx', 'exp'), may hold values from -5 to 5
- v_heads: bfloat16 [8192, 2048], P('ctx', 'exp'), may hold values from -6 to 6
- doc_ids: int32 [8192], P('ctx'), may hold values from 0 to 3, never falling along the last dimension, each value on 1 to 4096 neighbouring positions
- w_out: bfloat16 [2048, 2048], P('exp'), may hold values from -0.125 to 0.125
- hidden_rows: bfloat16 [8192, 2048], P(('ctx', 'exp')), may hold values from -6 to 6
- out_grad: bfloat16 [8192, 2048], P(('ctx', 'exp')), may hold values from -6 to 6
- picks: int32 [128, 16, 6], P(('ctx', 'exp')), may hold values from 0 to 63, as said below
- gates: bfloat16 [128, 16, 6], P(('ctx', 'exp')), may hold values from 0.099609375 to 1
- w_gate: bfloat16 [16, 2048, 1408], P('exp'), may hold values from -0.125 to 0.125
- w_up: bfloat16 [16, 2048, 1408], P('exp'), may hold values from -0.125 to 0.125
- w_down: bfloat16 [16, 1408, 2048], P('exp'), may hold values from -0.15625 to 0.15625
Outputs:
- d_queries: bfloat16 [8192, 2048], P('ctx', 'exp')
- d_keys: bfloat16 [8192, 2048], P('ctx', 'exp')
- d_values: bfloat16 [8192, 2048], P('ctx', 'exp')
- d_hidden: bfloat16 [8192, 2048], P(('ctx', 'exp'))
- d_gates: bfloat16 [128, 16, 6], P(('ctx', 'exp'))
The draws below stay inside these ranges and needn't reach their ends.
Inputs may be any that keep to these rules, and one draw needn't show every extreme that they name: `picks`: for each row block and expert the 6 offsets are distinct.
All inputs are finite; a program needn't handle non-finite values.
Results may differ from the reference program's by a relative error of at most 0.017.
Values may be sent and summed in bfloat16 or wider, within the bound.
A program may use at most 192 MiB of HBM per device.

```python
import math
import jax
import jax.numpy as jnp
import numpy as np
from jax import lax

D = 2048
FF = 1408
HD = 128
HEADS = 16
EXPERTS = 16
TOKENS = 8192
ROWS = 64
SLOT = 6
SOURCES = 128


def draw_q_heads(key, part):
    key = jax.random.fold_in(key, 11)
    shape = (TOKENS, HEADS * HD)
    return jnp.clip(1.2 * jax.random.normal(key, shape), -5.0, 5.0).astype(jnp.bfloat16)


def draw_k_heads(key, part):
    key = jax.random.fold_in(key, 23)
    shape = (TOKENS, HEADS * HD)
    return jnp.clip(1.2 * jax.random.normal(key, shape), -5.0, 5.0).astype(jnp.bfloat16)


def draw_picks(key, part):
    key = jax.random.fold_in(key, 5)
    scores = jax.random.randint(key, (SOURCES, EXPERTS, ROWS), 0, 1 << 20) * ROWS + jnp.arange(ROWS, dtype=jnp.int32)
    order = jnp.argsort(scores, axis=-1, stable=True)
    return order[..., :SLOT].astype(jnp.int32)


def shard_levels(stream_key, extent, pieces, low, top_value):
    loudness, own = 1.0, jax.random.fold_in(stream_key, 6)
    for axis_at, parts in pieces:
        draws = jnp.exp(jax.random.uniform(jax.random.fold_in(own, axis_at), (parts,), jnp.float32, low / len(pieces), top_value / len(pieces)))
        loudness = loudness * jnp.repeat(draws, extent[axis_at] // parts).reshape([-1 if axis == axis_at else 1 for axis in range(len(extent))])
    return loudness


def split_up(amount, total, bound, lean):
    portions = [(1 << 20) // math.isqrt(rank ** lean) + 1 for rank in range(2, amount + 1)]
    surplus, counts = total - bound - (amount - 1), [1] * (amount - 1)
    while surplus > 0:
        candidates = [i for i in range(amount - 1) if counts[i] < bound]
        mass, remaining = sum([portions[i] for i in candidates]), surplus
        for i in candidates:
            extra = min(bound - counts[i], max(1, remaining * portions[i] // mass), surplus)
            counts[i] = counts[i] + extra
            surplus = surplus - extra
    return np.array([bound] + counts)


def uneven_parts(key, number_of, total, limit, lean):
    if number_of == 2:
        one = jax.random.randint(key, (), max(1, total - limit), min(limit, total - 1) + 1)
        return jnp.stack([one, total - one])
    sizes = jnp.asarray(split_up(number_of, total, limit, lean), jnp.int32)
    couples = (number_of - 1) // 2
    source_of, taker = sizes[1:1 + 2 * couples:2], sizes[2:2 + 2 * couples:2]
    room = jnp.minimum(source_of - 1, limit - taker)
    passed = jax.random.randint(jax.random.fold_in(key, 1), (couples,), 0, 1 << 20) % (room + 1)
    sizes = sizes.at[1:1 + 2 * couples:2].set(source_of - passed).at[2:2 + 2 * couples:2].set(taker + passed)
    return sizes[jax.random.permutation(jax.random.fold_in(key, 2), number_of)]


def bell_draw(rng, dims, scale, most, cuts=(), held_as=jnp.bfloat16):
    values = scale * jax.random.normal(rng, dims, jnp.float32)
    if cuts:
        values = values * shard_levels(rng, dims, cuts, -0.22, 0.18)
    return jnp.clip(values, -most, most).astype(held_as)


def setup_inputs(seed: int = 0) -> dict:
    key_of = jax.random.split(jax.random.key(seed), 13)
    q_heads = draw_q_heads(jax.random.fold_in(key_of[12], 71), 0)
    k_heads = draw_k_heads(jax.random.fold_in(key_of[12], 71), 0)
    v_heads = bell_draw(key_of[2], (TOKENS, HEADS * HD), 1.0, 6.0, ((0, 8), (1, 16)))
    doc_ids = jnp.searchsorted(jnp.cumsum(uneven_parts(key_of[3], 4, TOKENS, TOKENS // 2, 0)), jnp.arange(TOKENS), side="right").astype(jnp.int32)
    w_out = bell_draw(key_of[4], (HEADS * HD, D), (HEADS * HD) ** -0.5, 0.125, ((0, 16),))
    hidden_rows = bell_draw(key_of[5], (TOKENS, D), 1.0, 6.0, ((0, 128),))
    out_grad = bell_draw(key_of[6], (TOKENS, D), 1.0, 6.0, ((0, 128),))
    picks = draw_picks(jax.random.fold_in(key_of[12], 71), 0)
    gates = jnp.clip(0.099609375 + 0.9003906 * jax.random.uniform(key_of[8], (SOURCES, EXPERTS, SLOT), jnp.float32) ** shard_levels(key_of[8], (SOURCES, EXPERTS, SLOT), ((0, 128),), -0.2, 0.2), 0.099609375, 1.0).astype(jnp.bfloat16)
    w_gate = bell_draw(key_of[9], (EXPERTS, D, FF), D ** -0.5, 0.125, ((0, 16),))
    w_up = bell_draw(key_of[10], (EXPERTS, D, FF), D ** -0.5, 0.125, ((0, 16),))
    w_down = bell_draw(key_of[11], (EXPERTS, FF, D), FF ** -0.5, 0.15625, ((0, 16),))
    return dict(q_heads=q_heads, k_heads=k_heads, v_heads=v_heads, doc_ids=doc_ids, w_out=w_out, hidden_rows=hidden_rows, out_grad=out_grad, picks=picks, gates=gates, w_gate=w_gate, w_up=w_up, w_down=w_down)


NEG = -1e+30

def head_grads(args):
    queries, keys, values, d_out, doc_ids = args
    scale = 1.0 / math.sqrt(HD)
    place = jnp.arange(TOKENS)
    scores = jnp.dot(queries, keys.T, preferred_element_type=jnp.float32) * scale
    allowed = (place[None, :] <= place[:, None]) & (doc_ids[None, :] == doc_ids[:, None])
    top = lax.optimization_barrier(jnp.max(jnp.where(allowed, scores, NEG), axis=1))
    total = lax.optimization_barrier(jnp.sum(jnp.where(allowed, jnp.exp(scores - top[:, None]), 0.0), axis=1))
    lse = top + jnp.log(total)
    probs = jnp.where(allowed, jnp.exp(scores - lse[:, None]), 0.0)
    d_probs = jnp.dot(d_out, values.T, preferred_element_type=jnp.float32)
    delta = lax.optimization_barrier(jnp.sum(probs * d_probs, axis=1))
    probs_low = probs.astype(jnp.bfloat16)
    d_values = jnp.dot(probs_low.T, d_out, preferred_element_type=jnp.float32)
    d_scores = (probs * (d_probs - delta[:, None])).astype(jnp.bfloat16)
    d_queries = jnp.dot(d_scores, keys, preferred_element_type=jnp.float32) * scale
    d_keys = jnp.dot(d_scores.T, queries, preferred_element_type=jnp.float32) * scale
    return (d_queries.astype(jnp.bfloat16), d_keys.astype(jnp.bfloat16), d_values.astype(jnp.bfloat16))

def reference(q_heads, k_heads, v_heads, doc_ids, w_out, hidden_rows, out_grad, picks, gates, w_gate, w_up, w_down):
    offsets = (jnp.arange(SOURCES) * ROWS).astype(jnp.int32)[:, None, None]
    global_rows = (picks + offsets).astype(jnp.int32)
    by_expert = jnp.transpose(global_rows, (1, 0, 2)).reshape(EXPERTS, SOURCES * SLOT)
    gate_rows = jnp.transpose(gates, (1, 0, 2)).reshape(EXPERTS, SOURCES * SLOT)

    def expert(args):
        index, weight, gate_w, up_w, down_w = args
        x = hidden_rows[index]
        g = out_grad[index]
        a = jnp.dot(x, gate_w, preferred_element_type=jnp.float32)
        b = jnp.dot(x, up_w, preferred_element_type=jnp.float32)
        u = jnp.dot(g, down_w.T, preferred_element_type=jnp.float32)
        sig = jax.nn.sigmoid(a)
        act_gate = a * sig
        d_gate = lax.optimization_barrier(jnp.sum(act_gate * b * u, axis=1)).astype(jnp.bfloat16)
        d_act = weight.astype(jnp.float32)[:, None] * u
        da = (d_act * b * sig * (1.0 + a * (1.0 - sig))).astype(jnp.bfloat16)
        db = (d_act * act_gate).astype(jnp.bfloat16)
        dx = jnp.dot(da, gate_w.T, preferred_element_type=jnp.float32) + jnp.dot(db, up_w.T, preferred_element_type=jnp.float32)
        return (dx.astype(jnp.bfloat16), d_gate)
    d_rows, d_gate_rows = lax.map(expert, (by_expert, gate_rows, w_gate, w_up, w_down))
    summed = jnp.zeros((TOKENS, D), jnp.float32).at[by_expert.reshape(-1)].add(d_rows.reshape(-1, D).astype(jnp.float32))
    d_hidden = (out_grad.astype(jnp.float32) + summed).astype(jnp.bfloat16)
    d_gates = jnp.transpose(d_gate_rows.reshape(EXPERTS, SOURCES, SLOT), (1, 0, 2))
    d_out = jnp.dot(d_hidden, w_out.T, preferred_element_type=jnp.float32).astype(jnp.bfloat16)

    def split_heads(array):
        return jnp.transpose(array.reshape(TOKENS, HEADS, HD), (1, 0, 2))
    docs = jnp.broadcast_to(doc_ids, (HEADS, TOKENS))
    d_queries, d_keys, d_values = lax.map(head_grads, (split_heads(q_heads), split_heads(k_heads), split_heads(v_heads), split_heads(d_out), docs))

    def join_heads(array):
        return jnp.transpose(array, (1, 0, 2)).reshape(TOKENS, HEADS * HD)
    return (join_heads(d_queries), join_heads(d_keys), join_heads(d_values), d_hidden, d_gates)
```

```python
import math

import jax
import jax.numpy as jnp
from jax import lax
from jax.experimental import pallas as pl
from jax.experimental.pallas import tpu as pltpu
from jax.sharding import PartitionSpec as P

NEG = -1e30
SCALE = 1.0 / math.sqrt(128)
KT = 512
QT = 256


def doc_start(place, scal):
    start = jnp.zeros_like(place)
    for d in range(1, 4):
        start = jnp.maximum(start, jnp.where(scal[d] <= place, scal[d], 0))
    return start


def doc_end(place, scal, tokens):
    end = jnp.full_like(place, tokens)
    for d in range(1, 4):
        end = jnp.minimum(end, jnp.where(scal[d] > place, scal[d], tokens))
    return end


def nt(a, b):
    return lax.dot_general(a, b, (((1,), (1,)), ((), ())), preferred_element_type=jnp.float32)


def fold(x, op):
    parts = [x[:, i * 128:(i + 1) * 128] for i in range(x.shape[1] // 128)]
    while len(parts) > 1:
        parts = [op(parts[i], parts[i + 1]) for i in range(0, len(parts), 2)]
    return parts[0]


def query_kernel(scal, qkv, d_out, dq_out, stats, s_buf, dp_buf):
    tok = d_out.shape[0]
    per = tok // KT
    me = scal[0]

    def one(qi, _):
        rows = pl.ds(pl.multiple_of(qi * QT, QT), QT)
        row0 = me * tok + qi * QT
        first = doc_start(row0, scal) // KT
        last = (row0 + QT - 1) // KT
        count = last - first + 1
        q = qkv[me, 0, rows, :]
        do = d_out[rows, :]
        place = row0 + lax.broadcasted_iota(jnp.int32, (QT, KT), 0)
        start = doc_start(place, scal)
        lane = lax.broadcasted_iota(jnp.int32, (QT, KT), 1)

        def tile(t, which):
            at = first + t
            return qkv[at // per, which, pl.ds(pl.multiple_of((at % per) * KT, KT), KT), :]

        def scores(t, top):
            s = nt(q, tile(t, 1)) * SCALE
            key = (first + t) * KT + lane
            s = jnp.where((key >= start) & (key <= place), s, NEG)
            s_buf[t] = s
            return jnp.maximum(top, fold(s, jnp.maximum))

        top = lax.fori_loop(0, count, scores, jnp.full((QT, 128), NEG, jnp.float32))
        top = jnp.max(top, axis=1, keepdims=True)

        def probs(t, carry):
            total, weighted = carry
            p = jnp.exp(s_buf[t] - top)
            dp = nt(do, tile(t, 2))
            s_buf[t] = p
            dp_buf[t] = dp
            return total + fold(p, jnp.add), weighted + fold(p * dp, jnp.add)

        zero = jnp.zeros((QT, 128), jnp.float32)
        total, weighted = lax.fori_loop(0, count, probs, (zero, zero))
        total = jnp.sum(total, axis=1, keepdims=True)
        inv = 1.0 / total
        delta = jnp.sum(weighted, axis=1, keepdims=True) * inv
        lse = top + jnp.log(total)

        def grads(t, dq):
            ds = (s_buf[t] * inv) * (dp_buf[t] - delta)
            return dq + jnp.dot(ds.astype(jnp.bfloat16), tile(t, 1), preferred_element_type=jnp.float32)

        dq = lax.fori_loop(0, count, grads, zero)
        dq_out[rows, :] = (dq * SCALE).astype(jnp.bfloat16)
        stats[0:1, rows] = jnp.transpose(jnp.broadcast_to(lse, (QT, 128)))[0:1, :]
        stats[1:2, rows] = jnp.transpose(jnp.broadcast_to(delta, (QT, 128)))[0:1, :]
        return 0

    lax.fori_loop(0, tok // QT, one, 0)


def key_kernel(scal, qkv, d_out, stats, dk_out, dv_out):
    tok = dk_out.shape[0]
    per = tok // KT
    me = scal[0]
    tokens = tok * qkv.shape[0]

    def one(ki, _):
        rows = pl.ds(pl.multiple_of(ki * QT, QT), QT)
        row0 = me * tok + ki * QT
        first = row0 // KT
        last = (doc_end(row0 + QT - 1, scal, tokens) - 1) // KT
        k = qkv[me, 1, rows, :]
        v = qkv[me, 2, rows, :]
        key = row0 + lax.broadcasted_iota(jnp.int32, (QT, KT), 0)
        lane = lax.broadcasted_iota(jnp.int32, (1, KT), 1)

        def step(at, carry):
            dk, dv = carry
            block = at // per
            cols = pl.ds(pl.multiple_of((at % per) * KT, KT), KT)
            q = qkv[block, 0, cols, :]
            do = d_out[block, cols, :]
            place = at * KT + lane
            start = doc_start(place, scal)
            allowed = (key >= start) & (key <= place)
            s = nt(k, q) * SCALE
            p = jnp.where(allowed, jnp.exp(s - stats[block, 0:1, cols]), 0.0)
            dp = nt(v, do)
            dv = dv + jnp.dot(p.astype(jnp.bfloat16), do, preferred_element_type=jnp.float32)
            ds = (p * (dp - stats[block, 1:2, cols])).astype(jnp.bfloat16)
            dk = dk + jnp.dot(ds, q, preferred_element_type=jnp.float32)
            return dk, dv

        zero = jnp.zeros((QT, 128), jnp.float32)
        dk, dv = lax.fori_loop(first, last + 1, step, (zero, zero))
        dk_out[rows, :] = (dk * SCALE).astype(jnp.bfloat16)
        dv_out[rows, :] = dv.astype(jnp.bfloat16)
        return 0

    lax.fori_loop(0, tok // QT, one, 0)


def attention(q_heads, k_heads, v_heads, doc_ids, d_out):
    tok, width = q_heads.shape
    ncx = lax.axis_size("ctx")
    me = lax.axis_index("ctx")
    qkv = lax.all_gather(jnp.stack([q_heads, k_heads, v_heads]), "ctx", axis=0)
    doc_all = lax.all_gather(doc_ids, "ctx", axis=0, tiled=True)
    starts = jnp.sum((doc_all[None, :] < jnp.arange(1, 4)[:, None]).astype(jnp.int32), axis=1)
    scal = jnp.concatenate([me[None].astype(jnp.int32), starts])
    d_out_all = lax.all_gather(d_out, "ctx", axis=0)
    vmem = pl.BlockSpec(memory_space=pltpu.VMEM)
    smem = pl.BlockSpec(memory_space=pltpu.SMEM)
    params = pltpu.CompilerParams(vmem_limit_bytes=48 * 2**20)
    low = jax.ShapeDtypeStruct((tok, width), jnp.bfloat16)
    pairs = 3 * tok * tok * 2 * width
    cost = pl.CostEstimate(flops=4 * pairs, bytes_accessed=8 * 2**20, transcendentals=3 * tok * tok)
    d_queries, stats = pl.pallas_call(
        query_kernel,
        out_shape=(low, jax.ShapeDtypeStruct((2, tok), jnp.float32)),
        in_specs=[smem, vmem, vmem],
        out_specs=(vmem, vmem),
        scratch_shapes=[pltpu.VMEM((9, QT, KT), jnp.float32), pltpu.VMEM((9, QT, KT), jnp.float32)],
        compiler_params=params,
        cost_estimate=cost,
        name="query_grads",
    )(scal, qkv, d_out)
    stats_all = lax.all_gather(stats, "ctx", axis=0)
    d_keys, d_values = pl.pallas_call(
        key_kernel,
        out_shape=(low, low),
        in_specs=[smem, vmem, vmem, vmem],
        out_specs=(vmem, vmem),
        compiler_params=params,
        cost_estimate=cost,
        name="key_grads",
    )(scal, qkv, d_out_all, stats_all)
    return d_queries, d_keys, d_values


def per_device(
    q_heads,
    k_heads,
    v_heads,
    doc_ids,
    w_out,
    hidden_rows,
    out_grad,
    picks,
    gates,
    w_gate,
    w_up,
    w_down,
):
    rows = hidden_rows.shape[0]
    model = hidden_rows.shape[1]
    experts = picks.shape[1]
    slots = picks.shape[2]
    index = picks[0].reshape(-1)
    chosen_h = jnp.take(hidden_rows, index, axis=0).reshape(experts, 1, slots, model)
    chosen_g = jnp.take(out_grad, index, axis=0).reshape(experts, 1, slots, model)
    chosen_w = gates.reshape(experts, 1, slots)
    xs = lax.all_to_all(chosen_h, "exp", split_axis=0, concat_axis=1, tiled=True)
    gs = lax.all_to_all(chosen_g, "exp", split_axis=0, concat_axis=1, tiled=True)
    ws = lax.all_to_all(chosen_w, "exp", split_axis=0, concat_axis=1, tiled=True)
    local = xs.shape[0]
    x_rows = xs.reshape(local, -1, model)
    g_rows = gs.reshape(local, -1, model)
    weight = ws.reshape(local, -1).astype(jnp.float32)
    a = jnp.einsum("erd,edf->erf", x_rows, w_gate, preferred_element_type=jnp.float32)
    b = jnp.einsum("erd,edf->erf", x_rows, w_up, preferred_element_type=jnp.float32)
    u = jnp.einsum("erd,efd->erf", g_rows, w_down, preferred_element_type=jnp.float32)
    sig = jax.nn.sigmoid(a)
    act_gate = a * sig
    d_gate = jnp.sum(act_gate * b * u, axis=2).astype(jnp.bfloat16)
    d_act = weight[..., None] * u
    da = (d_act * b * sig * (1.0 + a * (1.0 - sig))).astype(jnp.bfloat16)
    db = (d_act * act_gate).astype(jnp.bfloat16)
    d_x = jnp.einsum("erf,edf->erd", da, w_gate, preferred_element_type=jnp.float32)
    d_x = d_x + jnp.einsum("erf,edf->erd", db, w_up, preferred_element_type=jnp.float32)
    d_x = d_x.astype(jnp.bfloat16).reshape(xs.shape)
    d_gate = d_gate.reshape(ws.shape)
    back_rows = lax.all_to_all(d_x, "exp", split_axis=1, concat_axis=0, tiled=True)
    back_gates = lax.all_to_all(d_gate, "exp", split_axis=1, concat_axis=0, tiled=True)
    flat_rows = back_rows.reshape(experts * slots, model)
    one_hot = (index[:, None] == jnp.arange(rows)[None, :]).astype(jnp.bfloat16)
    summed = lax.dot_general(
        one_hot, flat_rows, (((0,), (0,)), ((), ())), preferred_element_type=jnp.float32
    )
    d_hidden = (out_grad.astype(jnp.float32) + summed).astype(jnp.bfloat16)
    d_gates = back_gates.reshape(1, experts, slots)
    d_out = lax.dot_general(
        lax.all_gather(d_hidden, "exp", axis=0, tiled=True),
        w_out,
        (((1,), (1,)), ((), ())),
        preferred_element_type=jnp.float32,
    ).astype(jnp.bfloat16)
    d_queries, d_keys, d_values = attention(q_heads, k_heads, v_heads, doc_ids, d_out)
    return (d_queries, d_keys, d_values, d_hidden, d_gates)


def solution(mesh):
    return jax.shard_map(
        per_device,
        mesh=mesh,
        in_specs=(
            P("ctx", "exp"),
            P("ctx", "exp"),
            P("ctx", "exp"),
            P("ctx"),
            P("exp", None),
            P(("ctx", "exp"), None),
            P(("ctx", "exp"), None),
            P(("ctx", "exp"), None, None),
            P(("ctx", "exp"), None, None),
            P("exp", None, None),
            P("exp", None, None),
            P("exp", None, None),
        ),
        out_specs=(
            P("ctx", "exp"),
            P("ctx", "exp"),
            P("ctx", "exp"),
            P(("ctx", "exp"), None),
            P(("ctx", "exp"), None, None),
        ),
        check_vma=False,
    )
```

```python
import math

import jax
import jax.numpy as jnp
from jax import lax
from jax.experimental import pallas as pl
from jax.experimental.pallas import tpu as pltpu
from jax.sharding import PartitionSpec as P

NEG = -1e30
SCALE = 1.0 / math.sqrt(128)
KT = 512
QT = 256


def doc_start(place, scal):
    start = jnp.zeros_like(place)
    for d in range(1, 4):
        start = jnp.maximum(start, jnp.where(scal[d] <= place, scal[d], 0))
    return start


def doc_end(place, scal, tokens):
    end = jnp.full_like(place, tokens)
    for d in range(1, 4):
        end = jnp.minimum(end, jnp.where(scal[d] > place, scal[d], tokens))
    return end


def nt(a, b):
    return lax.dot_general(a, b, (((1,), (1,)), ((), ())), preferred_element_type=jnp.float32)


def fold(x, op):
    parts = [x[:, i * 128:(i + 1) * 128] for i in range(x.shape[1] // 128)]
    while len(parts) > 1:
        parts = [op(parts[i], parts[i + 1]) for i in range(0, len(parts), 2)]
    return parts[0]


BF = jnp.bfloat16
F32 = jnp.float32
MESH = pl.DeviceIdType.MESH
FC = 256


def iota(shape, dim):
    return lax.broadcasted_iota(jnp.int32, shape, dim)


def mm(a, b):
    return jnp.dot(a, b, preferred_element_type=F32)


def place_in_message(r, j):
    tail = (r - 12, jnp.where(r < 14, r - 8, r - 14), r - 10)[j]
    slot = jnp.where(r < 6, r, jnp.where(r < 12, r - 6, tail))
    block = jnp.where(r < 6, 0, jnp.where(r < 12, 1, 2))
    if j == 1:
        block = jnp.where(r >= 14, 3, block)
    return slot, block


BLOCKS = ((0, 3, 6), (1, 4, 6, 7), (2, 5, 7))


def stacked(array, j, width=256):
    return jnp.concatenate([array[:, c * width:(c + 1) * width] for c in BLOCKS[j]], axis=0)


def pack_weights(j, rows_in_block):
    wide = len(BLOCKS[j]) * rows_in_block
    row = iota((256, wide), 0)
    slot, block = place_in_message(row % 16, j)
    return (iota((256, wide), 1) == block * rows_in_block + (row // 16) * 6 + slot).astype(BF)


def unpack(buf, c):
    lane, i = iota((96, 256), 1), iota((96, 256), 0)
    r, src = lane % 16, lane // 16
    out = None
    for j in range(3):
        if c not in BLOCKS[j]:
            continue
        slot, block = place_in_message(r, j)
        pick = ((i == src * 6 + slot) & (block == BLOCKS[j].index(c))).astype(BF)
        part = mm(pick, buf[:, j * 256:(j + 1) * 256])
        out = part if out is None else out + part
    return out.astype(BF)


def remote(src, dst, ss, rs, device):
    return pltpu.make_async_remote_copy(
        src_ref=src, dst_ref=dst, send_sem=ss, recv_sem=rs, device_id=device, device_id_type=MESH)


def start(copy):
    copy.start()


def sent(copy):
    copy.wait_send()


def received(copy):
    copy.wait_recv()


def q_own(src, win, ss, rs, slot, device):
    return remote(src, win.at[slot], ss.at[slot], rs.at[slot], device)


def backward(src, win, ss, rs, act):
    c, e = lax.axis_index("ctx"), lax.axis_index("exp")
    xl, y = c // 4, c % 4

    @pl.when(xl == 1)
    def _():
        act(q_own(src, win, ss, rs, 4, ((c + 4) % 8, e)))
    for o in range(1, 4):
        yo = (y + o) % 4

        @pl.when(yo < y)
        def _():
            act(q_own(src, win, ss, rs, y - yo, (xl * 4 + yo, e)))


def backward_first(src, win, ss, rs, act):
    c, e = lax.axis_index("ctx"), lax.axis_index("exp")

    @pl.when(c // 4 == 0)
    def _():
        act(q_own(src, win, ss, rs, 4, ((c + 4) % 8, e)))


def backward_relay(win, ss, rs, act):
    c, e = lax.axis_index("ctx"), lax.axis_index("exp")
    xl, y = c // 4, c % 4
    for o in range(1, 4):
        yo = (y + o) % 4

        @pl.when((xl == 0) & (yo > y))
        def _():
            act(q_own(win.at[4], win, ss, rs, 4 + y - yo, (xl * 4 + yo, e)))


def backward_rest(src, win, ss, rs, act):
    c, e = lax.axis_index("ctx"), lax.axis_index("exp")
    for slot in range(1, 5):
        @pl.when((c + slot <= 7) & ((c >= 4) | (slot < 4)))
        def _():
            act(q_own(src, win, ss, rs, slot, (c, e)))


def rows16(ref, i):
    return ref.at[pl.ds(pl.multiple_of(i * 16, 16), 16), :]


def moe_kernel(hidden, grad, picks, gates, docs, wg, wu, wd, wo, qh, kh, vh,
               d_hidden, d_gates, kv_win, q_win, do_win, counts,
               wg_v, wu_v, wd_v, w4, sx, sg, rx, rg, x_v, g_v, a_v, b_v, da_v, db_v, dx_v,
               px, rr, dgs, dgr, selw, ag, d4, d_out, cnt,
               local_sem, x_ss, x_rs, g_ss, g_rs, r_ss, r_rs, t_ss, t_rs, c_ss, c_rs,
               w_ss, w_rs, ag_ss, ag_rs, ex_ss, ex_rs, kv_ss, kv_rs, q_ss, q_rs, do_ss, do_rs):
    c = lax.axis_index("ctx")
    e = lax.axis_index("exp")
    xl, y = c // 4, c % 4
    xh, z, k = e // 8, (e // 2) % 4, e % 2
    across = (c + 4) % 8

    def exp_at(xh_, z_, k_):
        return (xh_ * 4 + z_) * 2 + k_

    def peer(d):
        p = (e + d) % 16
        return p, ((c + 4 * ((p // 8 + xh) % 2)) % 8, p)

    loads = [
        pltpu.make_async_copy(wg, wg_v, local_sem.at[0]),
        pltpu.make_async_copy(wu, wu_v, local_sem.at[1]),
        pltpu.make_async_copy(wd, wd_v, local_sem.at[2]),
        pltpu.make_async_copy(wo, w4.at[xh * 2 + k], local_sem.at[3]),
        pltpu.make_async_copy(qh, q_win.at[0], local_sem.at[4]),
        pltpu.make_async_copy(kh, kv_win.at[0, 0], local_sem.at[5]),
        pltpu.make_async_copy(vh, kv_win.at[0, 1], local_sem.at[6]),
    ]
    for load in loads:
        load.start()

    barrier = pltpu.get_barrier_semaphore()

    def greet(d, _):
        pl.semaphore_signal(barrier, inc=1, device_id=peer(d)[1], device_id_type=MESH)
        return 0

    lax.fori_loop(1, 16, greet, 0)
    for k_ in range(2):
        pl.semaphore_signal(barrier, inc=1, device_id=(c, exp_at(1 - xh, z, k_)), device_id_type=MESH)

    def greet_ctx(o, _):
        pl.semaphore_signal(barrier, inc=1, device_id=((c + o) % 8, e), device_id_type=MESH)
        return 0

    lax.fori_loop(1, 8, greet_ctx, 0)

    row = iota((256, 16), 0)
    spread = (row // 16 == iota((256, 16), 1)).astype(BF)
    pick_rows = mm(spread, picks[0].astype(F32).astype(BF))
    gate_rows = mm(spread, gates[0])
    r = iota((256, 6), 0) % 16
    lane6 = iota((256, 6), 1)
    hid, gra = hidden[...], grad[...]
    for j in range(3):
        slot, block = place_in_message(r, j)
        mine = lane6 == slot
        pick = jnp.sum(jnp.where(mine, pick_rows, 0.0), axis=1, keepdims=True)
        gate = jnp.sum(jnp.where(mine, gate_rows, 0.0), axis=1, keepdims=True)
        wide = 64 * len(BLOCKS[j])
        target = block[:, 0:1].astype(F32) * 64.0 + pick
        hit = iota((256, wide), 1).astype(F32) == target
        sel = hit.astype(BF)
        sx[:, j * 256:(j + 1) * 256] = mm(sel, stacked(hid, j)).astype(BF)
        sg[:, j * 256:(j + 1) * 256] = mm(sel, stacked(gra, j)).astype(BF)
        if wide == 256:
            hit_w = hit
        else:
            hit_w = iota((256, 256), 1).astype(F32) == target
        selw[j] = jnp.transpose(jnp.where(hit_w, gate, 0.0)).astype(BF)
    sizes = []
    for d in range(8):
        under_d = jnp.sum((docs[...] < d).astype(F32), axis=1, keepdims=True)
        sizes.append(jnp.broadcast_to(jnp.sum(under_d, axis=0, keepdims=True), (1, 128)))
    below = jnp.concatenate(sizes, axis=0).astype(jnp.int32)
    cnt[...] = below
    counts[c] = below

    pl.semaphore_wait(barrier, 15 + 2 + 7)

    def x_copy(d):
        p, device = peer(d)
        return remote(rows16(sx, p), rows16(rx, e), x_ss.at[p], x_rs.at[e], device)

    def g_copy(d):
        p, device = peer(d)
        return remote(rows16(sg, p), rows16(rg, e), g_ss.at[p], g_rs.at[e], device)

    def r_copy(d):
        p, device = peer(d)
        return remote(rows16(px, p), rows16(rr, e), r_ss.at[p], r_rs.at[e], device)

    def t_copy(d):
        p, device = peer(d)
        return remote(rows16(dgs, p), rows16(dgr, e), t_ss.at[p], t_rs.at[e], device)

    def c_copy(o):
        return remote(cnt, counts.at[c], c_ss.at[o], c_rs.at[c], ((c + o) % 8, e))

    def recv(buf, rs):
        def one(d, _):
            p, device = peer(d)
            remote(rows16(buf, p), rows16(buf, p), rs.at[p], rs.at[p], device).wait_recv()
            return 0
        lax.fori_loop(1, 16, one, 0)

    def each(n0, n1, act):
        def one(d, _):
            act(d)
            return 0
        lax.fori_loop(n0, n1, one, 0)

    each(1, 16, lambda d: x_copy(d).start())
    each(1, 16, lambda d: g_copy(d).start())
    own16 = pl.ds(pl.multiple_of(e * 16, 16), 16)
    rx[own16, :] = sx[own16, :]
    rg[own16, :] = sg[own16, :]

    mate = (c, exp_at(xh, z, 1 - k))
    facing = (across, exp_at(1 - xh, z, k))
    own_q, mate_q = xh * 2 + k, xh * 2 + 1 - k
    far_q, far_mate_q = (1 - xh) * 2 + k, (1 - xh) * 2 + 1 - k
    w_mate = remote(wo, w4.at[own_q], w_ss.at[0], w_rs.at[0], mate)
    w_facing = remote(wo, w4.at[own_q], w_ss.at[1], w_rs.at[1], facing)
    w_relay = remote(w4.at[far_q], w4.at[far_q], w_ss.at[2], w_rs.at[2], mate)
    w_mate.start()
    w_facing.start()
    each(1, 8, lambda o: c_copy(o).start())

    def kv_own(slot, device):
        return [remote(src, kv_win.at[slot, i], kv_ss.at[slot, i], kv_rs.at[slot, i], device)
                for i, src in enumerate((kh, vh))]

    def forward(act):
        @pl.when(xl == 0)
        def _():
            for copy in kv_own(4, (across, e)):
                act(copy)
        for o in range(1, 4):
            yo = (y + o) % 4

            @pl.when(yo > y)
            def _():
                for copy in kv_own(yo - y, (xl * 4 + yo, e)):
                    act(copy)

    def forward_relay(act):
        for o in range(1, 4):
            yo = (y + o) % 4

            @pl.when((xl == 1) & (yo < y))
            def _():
                slot = 4 + yo - y
                act(remote(kv_win.at[4], kv_win.at[slot], kv_ss.at[slot, 0], kv_rs.at[slot, 0], (xl * 4 + yo, e)))

    forward(start)
    backward(qh, q_win, q_ss, q_rs, start)

    recv(rx, x_rs)
    for col in range(8):
        x_v[:, col * 256:(col + 1) * 256] = unpack(rx[...], col)
    loads[0].wait()
    loads[1].wait()

    def up(f0, n):
        cols = pl.ds(f0, n)
        a_v[:, cols] = mm(x_v[...], wg_v[:, cols])
        b_v[:, cols] = mm(x_v[...], wu_v[:, cols])

    def up_step(i, _):
        up(pl.multiple_of(i * FC, FC), FC)
        return 0

    ff = wg.shape[1]
    whole = ff // FC
    lax.fori_loop(0, whole, up_step, 0)
    if ff % FC:
        up(whole * FC, ff % FC)
    recv(rg, g_rs)
    for col in range(8):
        g_v[:, col * 256:(col + 1) * 256] = unpack(rg[...], col)
    loads[2].wait()

    def down(f0, n, acc):
        cols = pl.ds(f0, n)
        u = nt(g_v[...], wd_v[cols, :])
        a, b = a_v[:, cols], b_v[:, cols]
        sig = 1.0 / (1.0 + jnp.exp(-a))
        act = a * sig
        da_v[:, cols] = (u * b * sig * (1.0 + a * (1.0 - sig))).astype(BF)
        db_v[:, cols] = (u * act).astype(BF)
        return acc + fold(act * b * u, jnp.add)

    def down_step(i, acc):
        return down(pl.multiple_of(i * FC, FC), FC, acc)

    acc = lax.fori_loop(0, whole, down_step, jnp.zeros((96, 128), F32))
    if ff % FC:
        acc = down(whole * FC, ff % FC, acc)

    def back_step(i, _):
        cols = pl.ds(pl.multiple_of(i * FC, FC), FC)
        dx_v[:, cols] = (nt(da_v[...], wg_v[cols, :]) + nt(db_v[...], wu_v[cols, :])).astype(BF)
        return 0

    lax.fori_loop(0, wg.shape[0] // FC, back_step, 0)
    for j in range(3):
        px[:, j * 256:(j + 1) * 256] = mm(pack_weights(j, 96), stacked(dx_v[...], j)).astype(BF)
    each(1, 16, lambda d: r_copy(d).start())
    rr[own16, :] = px[own16, :]
    d_gate = jnp.broadcast_to(jnp.sum(acc, axis=1, keepdims=True), (96, 128)).astype(BF)
    row = iota((256, 96), 0)
    pack6 = ((iota((256, 96), 1) == (row // 16) * 6 + row % 16) & (row % 16 < 6)).astype(BF)
    dgs[...] = mm(pack6, d_gate).astype(BF)
    each(1, 16, lambda d: t_copy(d).start())
    dgr[own16, :] = dgs[own16, :]

    w_facing.wait_recv()
    w_relay.start()

    @pl.when(xl == 1)
    def _():
        for copy in kv_own(4, (across, e)):
            copy.wait_recv()
    forward_relay(start)

    backward_first(qh, q_win, q_ss, q_rs, received)
    backward_relay(q_win, q_ss, q_rs, start)

    recv(rr, r_rs)
    sums = [mm(selw[j], rr[:, j * 256:(j + 1) * 256]) for j in range(3)]
    parts = [sums[c_ % 3][(c_ // 3) * 64:(c_ // 3) * 64 + 64] for c_ in range(6)]
    parts.append(sums[0][128:192] + sums[1][128:192])
    parts.append(sums[1][192:256] + sums[2][128:192])
    for col in range(8):
        cols = slice(col * 256, (col + 1) * 256)
        low = (grad[:, cols].astype(F32) + parts[col]).astype(BF)
        ag[z, :, cols] = low
        d_hidden[:, cols] = low

    above, under = (c, exp_at(xh, (z + 1) % 4, k)), (c, exp_at(xh, (z + 3) % 4, k))
    z_up, z_down = (z + 1) % 4, (z + 3) % 4
    first, second = pl.ds(0, 32), pl.ds(32, 32)
    g_up = remote(ag.at[z], ag.at[z], ag_ss.at[0], ag_rs.at[0], above)
    g_down = remote(ag.at[z], ag.at[z], ag_ss.at[1], ag_rs.at[1], under)
    g_up2 = remote(ag.at[z_down, first], ag.at[z_down, first], ag_ss.at[2], ag_rs.at[2], above)
    g_down2 = remote(ag.at[z_up, second], ag.at[z_up, second], ag_ss.at[3], ag_rs.at[3], under)
    g_up.start()
    g_down.start()
    g_up.wait_recv()
    g_up2.start()
    g_down.wait_recv()
    g_down2.start()
    loads[3].wait()
    w_mate.wait_recv()
    w_relay.wait_recv()
    g_up2.wait_recv()
    g_down2.wait_recv()

    tokens = ag[...].reshape(256, ag.shape[2])
    for q_ in range(4):
        d4[q_] = nt(tokens, w4[q_]).astype(BF).reshape(4, 64, 128)
    others = [(mate_q, mate), (far_q, (c, exp_at(1 - xh, z, k))), (far_mate_q, (c, exp_at(1 - xh, z, 1 - k)))]
    sends = [remote(d4.at[q_], d_out.at[xh, :, k], ex_ss.at[i], ex_rs.at[i], device)
             for i, (q_, device) in enumerate(others)]
    for copy in sends:
        copy.start()
    d_out[xh, :, k] = d4[own_q]
    for copy in sends:
        copy.wait_recv()

    flat = d_out
    keep = pltpu.make_async_copy(flat, do_win.at[0], local_sem.at[7])
    keep.start()
    backward(flat, do_win, do_ss, do_rs, start)

    backward_first(flat, do_win, do_ss, do_rs, received)
    backward_relay(do_win, do_ss, do_rs, start)

    recv(dgr, t_rs)
    row, lane = iota((256, 128), 0), iota((256, 128), 1)
    diag = jnp.where(row % 16 == lane, dgr[...].astype(F32), 0.0).astype(BF)
    gather = (iota((16, 256), 1) // 16 == iota((16, 256), 0)).astype(BF)
    d_gates[...] = mm(gather, diag)[:, 0:6].astype(BF)

    def c_recv(o):
        src = (c + o) % 8
        remote(cnt, counts.at[src], c_ss.at[o], c_rs.at[src], (src, e)).wait_recv()

    each(1, 8, c_recv)
    for slot in range(1, 5):
        @pl.when((c >= slot) & (slot < 4))
        def _():
            @pl.when(c - slot >= xl * 4)
            def _():
                for copy in kv_own(slot, (c, e)):
                    copy.wait_recv()

            @pl.when(c - slot < xl * 4)
            def _():
                remote(kv_win.at[slot], kv_win.at[slot], kv_ss.at[slot, 0], kv_rs.at[slot, 0], (c, e)).wait_recv()

    backward_rest(qh, q_win, q_ss, q_rs, received)
    backward_rest(flat, do_win, do_ss, do_rs, received)
    each(1, 16, lambda d: x_copy(d).wait_send())
    each(1, 16, lambda d: g_copy(d).wait_send())
    each(1, 16, lambda d: r_copy(d).wait_send())
    each(1, 16, lambda d: t_copy(d).wait_send())
    each(1, 8, lambda o: c_copy(o).wait_send())
    for copy in [w_mate, w_facing, w_relay, g_up, g_down, g_up2, g_down2] + sends:
        copy.wait_send()
    forward(sent)
    forward_relay(sent)
    backward(qh, q_win, q_ss, q_rs, sent)
    backward_relay(q_win, q_ss, q_rs, sent)
    backward(flat, do_win, do_ss, do_rs, sent)
    backward_relay(do_win, do_ss, do_rs, sent)
    for load in loads[4:] + [keep]:
        load.wait()


def moe(q_heads, k_heads, v_heads, doc_ids, w_out, hidden_rows, out_grad, picks, gates, w_gate, w_up, w_down):
    vm, hbm = pl.BlockSpec(memory_space=pltpu.VMEM), pl.BlockSpec(memory_space=pl.ANY)
    tok, width = q_heads.shape
    rows, model = hidden_rows.shape
    ff = w_gate.shape[2]
    dma = pltpu.SemaphoreType.DMA

    def low(*shape):
        return pltpu.VMEM(shape, BF)

    def out(*shape, dtype=BF):
        return jax.ShapeDtypeStruct(shape, dtype)

    return pl.pallas_call(
        moe_kernel,
        out_shape=(out(rows, model), out(16, 6), out(5, 2, tok, width), out(5, tok, width),
                   out(5, 2, 4, 2, rows, width), out(8, 8, 128, dtype=jnp.int32)),
        in_specs=[vm] * 5 + [hbm] * 7,
        out_specs=(vm, vm, hbm, hbm, hbm, vm),
        scratch_shapes=[
            low(model, ff), low(model, ff), low(ff, model), low(4, 128, model),
            low(256, 768), low(256, 768), low(256, 768), low(256, 768),
            low(96, model), low(96, model), pltpu.VMEM((96, ff), F32), pltpu.VMEM((96, ff), F32),
            low(96, ff), low(96, ff), low(96, model),
            low(256, 768), low(256, 768), low(256, 128), low(256, 128),
            low(3, 256, 256), low(4, rows, model), low(4, 4, rows, width), low(2, 4, 2, rows, width),
            pltpu.VMEM((8, 128), jnp.int32),
            dma((8,)), dma((16,)), dma((16,)), dma((16,)), dma((16,)), dma((16,)), dma((16,)), dma((16,)), dma((16,)),
            dma((8,)), dma((8,)), dma((3,)), dma((3,)), dma((4,)), dma((4,)), dma((3,)), dma((3,)),
            dma((5, 2)), dma((5, 2)), dma((5,)), dma((5,)), dma((5,)), dma((5,)),
        ],
        compiler_params=pltpu.CompilerParams(
            collective_id=0, has_side_effects=True, vmem_limit_bytes=48 * 2**20),
        name="experts",
    )(hidden_rows, out_grad, picks, gates, doc_ids.reshape(8, 128), w_gate[0], w_up[0], w_down[0], w_out,
      q_heads, k_heads, v_heads)


def query_kernel(scal, q_ref, kv_win, d_out, dq_out, stats, s_buf, dp_buf):
    tok = q_ref.shape[0]
    per = tok // KT
    me = scal[0]

    def one(qi, _):
        rows = pl.ds(pl.multiple_of(qi * QT, QT), QT)
        row0 = me * tok + qi * QT
        first = doc_start(row0, scal) // KT
        last = (row0 + QT - 1) // KT
        count = last - first + 1
        q = q_ref[rows, :]
        do = d_out[0, rows, :]
        place = row0 + lax.broadcasted_iota(jnp.int32, (QT, KT), 0)
        start = doc_start(place, scal)
        lane = lax.broadcasted_iota(jnp.int32, (QT, KT), 1)

        def tile(t, which):
            at = first + t
            return kv_win[me - at // per, which, pl.ds(pl.multiple_of((at % per) * KT, KT), KT), :]

        def scores(t, top):
            s = nt(q, tile(t, 0)) * SCALE
            key = (first + t) * KT + lane
            s = jnp.where((key >= start) & (key <= place), s, NEG)
            s_buf[t] = s
            return jnp.maximum(top, fold(s, jnp.maximum))

        top = lax.fori_loop(0, count, scores, jnp.full((QT, 128), NEG, jnp.float32))
        top = jnp.max(top, axis=1, keepdims=True)

        def probs(t, carry):
            total, weighted = carry
            p = jnp.exp(s_buf[t] - top)
            dp = nt(do, tile(t, 1))
            s_buf[t] = p
            dp_buf[t] = dp
            return total + fold(p, jnp.add), weighted + fold(p * dp, jnp.add)

        zero = jnp.zeros((QT, 128), jnp.float32)
        total, weighted = lax.fori_loop(0, count, probs, (zero, zero))
        total = jnp.sum(total, axis=1, keepdims=True)
        inv = 1.0 / total
        delta = jnp.sum(weighted, axis=1, keepdims=True) * inv
        lse = top + jnp.log(total)

        def grads(t, dq):
            ds = (s_buf[t] * inv) * (dp_buf[t] - delta)
            return dq + jnp.dot(ds.astype(jnp.bfloat16), tile(t, 0), preferred_element_type=jnp.float32)

        dq = lax.fori_loop(0, count, grads, zero)
        dq_out[rows, :] = (dq * SCALE).astype(jnp.bfloat16)
        stats[0:1, rows] = jnp.transpose(jnp.broadcast_to(lse, (QT, 128)))[0:1, :]
        stats[1:2, rows] = jnp.transpose(jnp.broadcast_to(delta, (QT, 128)))[0:1, :]
        return 0

    lax.fori_loop(0, tok // QT, one, 0)


def key_kernel(scal, k_ref, v_ref, q_win, do_win, stats, dk_out, dv_out):
    tok = dk_out.shape[0]
    per = tok // KT
    me = scal[0]
    tokens = tok * 8

    def one(ki, _):
        rows = pl.ds(pl.multiple_of(ki * QT, QT), QT)
        row0 = me * tok + ki * QT
        first = row0 // KT
        last = (doc_end(row0 + QT - 1, scal, tokens) - 1) // KT
        k = k_ref[rows, :]
        v = v_ref[rows, :]
        key = row0 + lax.broadcasted_iota(jnp.int32, (QT, KT), 0)
        lane = lax.broadcasted_iota(jnp.int32, (1, KT), 1)

        def step(at, carry):
            dk, dv = carry
            block = at // per - me
            cols = pl.ds(pl.multiple_of((at % per) * KT, KT), KT)
            q = q_win[block, cols, :]
            do = do_win[block, cols, :]
            place = at * KT + lane
            start = doc_start(place, scal)
            allowed = (key >= start) & (key <= place)
            s = nt(k, q) * SCALE
            p = jnp.where(allowed, jnp.exp(s - stats[block, 0:1, cols]), 0.0)
            dp = nt(v, do)
            dv = dv + jnp.dot(p.astype(jnp.bfloat16), do, preferred_element_type=jnp.float32)
            ds = (p * (dp - stats[block, 1:2, cols])).astype(jnp.bfloat16)
            dk = dk + jnp.dot(ds, q, preferred_element_type=jnp.float32)
            return dk, dv

        zero = jnp.zeros((QT, 128), jnp.float32)
        dk, dv = lax.fori_loop(first, last + 1, step, (zero, zero))
        dk_out[rows, :] = (dk * SCALE).astype(jnp.bfloat16)
        dv_out[rows, :] = dv.astype(jnp.bfloat16)
        return 0

    lax.fori_loop(0, tok // QT, one, 0)


def stats_kernel(stats, win, local_sem, ss, rs):
    c, e = lax.axis_index("ctx"), lax.axis_index("exp")
    barrier = pltpu.get_barrier_semaphore()
    peers = [((c + 4) % 8, e)] + [((c // 4) * 4 + (c + o) % 4, e) for o in range(1, 4)]
    for device in peers:
        pl.semaphore_signal(barrier, inc=1, device_id=device, device_id_type=MESH)
    win[0] = stats[...]
    pl.semaphore_wait(barrier, 4)
    backward(stats, win, ss, rs, start)
    backward_first(stats, win, ss, rs, received)
    backward_relay(win, ss, rs, start)
    backward_rest(stats, win, ss, rs, received)
    backward(stats, win, ss, rs, sent)
    backward_relay(win, ss, rs, sent)


def attention(q_heads, k_heads, v_heads, kv_win, q_win, do_win, counts):
    tok, width = q_heads.shape
    me = lax.axis_index("ctx")
    starts = jnp.sum(counts[:, 1:4, 0], axis=0)
    scal = jnp.concatenate([me[None].astype(jnp.int32), starts])
    vmem = pl.BlockSpec(memory_space=pltpu.VMEM)
    smem = pl.BlockSpec(memory_space=pltpu.SMEM)
    params = pltpu.CompilerParams(vmem_limit_bytes=48 * 2**20)
    low = jax.ShapeDtypeStruct((tok, width), jnp.bfloat16)
    d_queries, stats = pl.pallas_call(
        query_kernel,
        grid=(1,),
        out_shape=(low, jax.ShapeDtypeStruct((8, tok), jnp.float32)),
        in_specs=[smem, vmem, vmem, pl.BlockSpec((1, tok, width), lambda *_: (0, 0, 0))],
        out_specs=(vmem, vmem),
        scratch_shapes=[pltpu.VMEM((9, QT, KT), jnp.float32), pltpu.VMEM((9, QT, KT), jnp.float32)],
        compiler_params=params,
        name="query_grads",
    )(scal, q_heads, kv_win, do_win)
    dma = pltpu.SemaphoreType.DMA
    stats_win = pl.pallas_call(
        stats_kernel,
        out_shape=jax.ShapeDtypeStruct((5, 8, tok), jnp.float32),
        in_specs=[vmem],
        out_specs=vmem,
        scratch_shapes=[dma((1,)), dma((5,)), dma((5,))],
        compiler_params=pltpu.CompilerParams(collective_id=1, has_side_effects=True),
        name="row_stats",
    )(stats)
    d_keys, d_values = pl.pallas_call(
        key_kernel,
        out_shape=(low, low),
        in_specs=[smem] + [vmem] * 5,
        out_specs=(vmem, vmem),
        compiler_params=params,
        name="key_grads",
    )(scal, k_heads, v_heads, q_win, do_win, stats_win)
    return d_queries, d_keys, d_values


def per_device(q_heads, k_heads, v_heads, doc_ids, w_out, hidden_rows, out_grad, picks, gates, w_gate, w_up, w_down):
    tok, width = q_heads.shape
    d_hidden, d_gates, kv_win, q_win, do_win, counts = moe(
        q_heads, k_heads, v_heads, doc_ids, w_out, hidden_rows, out_grad, picks, gates, w_gate, w_up, w_down)
    do_win = do_win.reshape(5, tok, width)
    d_queries, d_keys, d_values = attention(q_heads, k_heads, v_heads, kv_win, q_win, do_win, counts)
    return (d_queries, d_keys, d_values, d_hidden, d_gates[None])


def solution(mesh):
    return jax.shard_map(
        per_device,
        mesh=mesh,
        in_specs=(
            P("ctx", "exp"),
            P("ctx", "exp"),
            P("ctx", "exp"),
            P("ctx"),
            P("exp", None),
            P(("ctx", "exp"), None),
            P(("ctx", "exp"), None),
            P(("ctx", "exp"), None, None),
            P(("ctx", "exp"), None, None),
            P("exp", None, None),
            P("exp", None, None),
            P("exp", None, None),
        ),
        out_specs=(
            P("ctx", "exp"),
            P("ctx", "exp"),
            P("ctx", "exp"),
            P(("ctx", "exp"), None),
            P(("ctx", "exp"), None, None),
        ),
        check_vma=False,
    )
```

```python
import math

import jax
import jax.numpy as jnp
from jax import lax
from jax.experimental import pallas as pl
from jax.experimental.pallas import tpu as pltpu
from jax.sharding import PartitionSpec as P

NEG = -1e30
SCALE = 1.0 / math.sqrt(128)


def nt(a, b):
    return lax.dot_general(a, b, (((1,), (1,)), ((), ())), preferred_element_type=jnp.float32)


def fold(x, op):
    parts = [x[:, i * 128:(i + 1) * 128] for i in range(x.shape[1] // 128)]
    while len(parts) > 1:
        parts = [op(parts[i], parts[i + 1]) for i in range(0, len(parts), 2)]
    return parts[0]


BF = jnp.bfloat16
F32 = jnp.float32
MESH = pl.DeviceIdType.MESH
FC = 256


def iota(shape, dim):
    return lax.broadcasted_iota(jnp.int32, shape, dim)


def mm(a, b):
    return jnp.dot(a, b, preferred_element_type=F32)


def place_in_message(r, j):
    tail = (r - 12, jnp.where(r < 14, r - 8, r - 14), r - 10)[j]
    slot = jnp.where(r < 6, r, jnp.where(r < 12, r - 6, tail))
    block = jnp.where(r < 6, 0, jnp.where(r < 12, 1, 2))
    if j == 1:
        block = jnp.where(r >= 14, 3, block)
    return slot, block


BLOCKS = ((0, 3, 6), (1, 4, 6, 7), (2, 5, 7))


def stacked(array, j, width=256):
    return jnp.concatenate([array[:, c * width:(c + 1) * width] for c in BLOCKS[j]], axis=0)


def pack_weights(j, rows_in_block):
    wide = len(BLOCKS[j]) * rows_in_block
    row = iota((256, wide), 0)
    slot, block = place_in_message(row % 16, j)
    return (iota((256, wide), 1) == block * rows_in_block + (row // 16) * 6 + slot).astype(BF)


def unpack(buf, c):
    lane, i = iota((96, 256), 1), iota((96, 256), 0)
    r, src = lane % 16, lane // 16
    out = None
    for j in range(3):
        if c not in BLOCKS[j]:
            continue
        slot, block = place_in_message(r, j)
        pick = ((i == src * 6 + slot) & (block == BLOCKS[j].index(c))).astype(BF)
        part = mm(pick, buf[:, j * 256:(j + 1) * 256])
        out = part if out is None else out + part
    return out.astype(BF)


def remote(src, dst, ss, rs, device):
    return pltpu.make_async_remote_copy(
        src_ref=src, dst_ref=dst, send_sem=ss, recv_sem=rs, device_id=device, device_id_type=MESH)


def rows16(ref, i):
    return ref.at[pl.ds(pl.multiple_of(i * 16, 16), 16), :]


def kernel(hidden, grad, picks, gates, docs, wg, wu, wd, wo, qh, kh, vh,
           d_hidden, d_gates, dq_out, dk_out, dv_out,
           wg_v, wu_v, wd_v, w4, sx, sg, rx, rg, x_v, g_v, a_v, b_v, da_v, db_v, dx_v,
           px, rr, dgs, dgr, selw, ag, d4, cnt, counts,
           q_win, k_win, v_win, do_win, lse_win, delta_win, top_v, sum_v, o_v, lse_v, delta_v, start_v,
           pt_v, dq_v, dk_v, dv_v,
           local_sem, x_ss, x_rs, g_ss, g_rs, r_ss, r_rs, t_ss, t_rs, c_ss, c_rs,
           w_ss, w_rs, ag_ss, ag_rs, ex_ss, ex_rs, xs_ss, kv_ss, kv_rs, q_ss, q_rs, do_ss, do_rs,
           lse_ss, lse_rs, dl_ss, dl_rs):
    c = lax.axis_index("ctx")
    e = lax.axis_index("exp")
    xl, y = c // 4, c % 4
    xh, z, k = e // 8, (e // 2) % 4, e % 2
    across = (c + 4) % 8

    def exp_at(xh_, z_, k_):
        return (xh_ * 4 + z_) * 2 + k_

    def peer(d):
        p = (e + d) % 16
        return p, ((c + 4 * ((p // 8 + xh) % 2)) % 8, p)

    loads = [
        pltpu.make_async_copy(wg, wg_v, local_sem.at[0]),
        pltpu.make_async_copy(wu, wu_v, local_sem.at[1]),
        pltpu.make_async_copy(wd, wd_v, local_sem.at[2]),
        pltpu.make_async_copy(wo, w4.at[xh * 2 + k], local_sem.at[3]),
        pltpu.make_async_copy(qh, q_win.at[0], local_sem.at[4]),
        pltpu.make_async_copy(kh, k_win.at[0], local_sem.at[5]),
        pltpu.make_async_copy(vh, v_win.at[0], local_sem.at[6]),
    ]
    for load in loads:
        load.start()

    barrier = pltpu.get_barrier_semaphore()

    def greet(d, _):
        pl.semaphore_signal(barrier, inc=1, device_id=peer(d)[1], device_id_type=MESH)
        return 0

    lax.fori_loop(1, 16, greet, 0)
    for k_ in range(2):
        pl.semaphore_signal(barrier, inc=1, device_id=(c, exp_at(1 - xh, z, k_)), device_id_type=MESH)

    pl.semaphore_signal(barrier, inc=1, device_id=(across, exp_at(xh, z, 1 - k)), device_id_type=MESH)

    def greet_ctx(o, _):
        pl.semaphore_signal(barrier, inc=1, device_id=((c + o) % 8, e), device_id_type=MESH)
        return 0

    lax.fori_loop(1, 8, greet_ctx, 0)

    row = iota((256, 16), 0)
    spread = (row // 16 == iota((256, 16), 1)).astype(BF)
    pick_rows = nt(spread, jnp.concatenate([picks[i] for i in range(6)], axis=0).astype(F32).astype(BF))
    gate_rows = nt(spread, gates[0])
    r = iota((256, 6), 0) % 16
    lane6 = iota((256, 6), 1)
    hid, gra = hidden[...], grad[...]
    for j in range(3):
        slot, block = place_in_message(r, j)
        mine = lane6 == slot
        pick = jnp.sum(jnp.where(mine, pick_rows, 0.0), axis=1, keepdims=True)
        gate = jnp.sum(jnp.where(mine, gate_rows, 0.0), axis=1, keepdims=True)
        wide = 64 * len(BLOCKS[j])
        target = block[:, 0:1].astype(F32) * 64.0 + pick
        hit = iota((256, wide), 1).astype(F32) == target
        sel = hit.astype(BF)
        sx[:, j * 256:(j + 1) * 256] = mm(sel, stacked(hid, j)).astype(BF)
        sg[:, j * 256:(j + 1) * 256] = mm(sel, stacked(gra, j)).astype(BF)
        if wide == 256:
            hit_w = hit
        else:
            hit_w = iota((256, 256), 1).astype(F32) == target
        selw[j] = jnp.transpose(jnp.where(hit_w, gate, 0.0)).astype(BF)
    sizes = []
    for d in range(8):
        under_d = jnp.sum((docs[...] < d).astype(F32), axis=1, keepdims=True)
        sizes.append(jnp.broadcast_to(jnp.sum(under_d, axis=0, keepdims=True), (1, 128)))
    below = jnp.concatenate(sizes, axis=0).astype(jnp.int32)
    cnt[...] = below
    counts[c] = below

    pl.semaphore_wait(barrier, 15 + 3 + 7)

    def x_copy(d):
        p, device = peer(d)
        return remote(rows16(sx, p), rows16(rx, e), x_ss.at[p], x_rs.at[e], device)

    def g_copy(d):
        p, device = peer(d)
        return remote(rows16(sg, p), rows16(rg, e), g_ss.at[p], g_rs.at[e], device)

    def r_copy(d):
        p, device = peer(d)
        return remote(rows16(px, p), rows16(rr, e), r_ss.at[p], r_rs.at[e], device)

    def t_copy(d):
        p, device = peer(d)
        return remote(rows16(dgs, p), rows16(dgr, e), t_ss.at[p], t_rs.at[e], device)

    def c_copy(o):
        return remote(cnt, counts.at[c], c_ss.at[o], c_rs.at[c], ((c + o) % 8, e))

    def c_recv(o):
        src = (c + o) % 8
        remote(cnt, counts.at[src], c_ss.at[o], c_rs.at[src], (src, e)).wait_recv()

    def recv(buf, rs):
        def one(d, _):
            p, device = peer(d)
            remote(rows16(buf, p), rows16(buf, p), rs.at[p], rs.at[p], device).wait_recv()
            return 0
        lax.fori_loop(1, 16, one, 0)

    def each(n0, n1, act):
        def one(d, _):
            act(d)
            return 0
        lax.fori_loop(n0, n1, one, 0)

    each(1, 16, lambda d: x_copy(d).start())
    each(1, 16, lambda d: g_copy(d).start())
    own16 = pl.ds(pl.multiple_of(e * 16, 16), 16)
    rx[own16, :] = sx[own16, :]
    rg[own16, :] = sg[own16, :]

    mate = (c, exp_at(xh, z, 1 - k))
    facing = (across, exp_at(1 - xh, z, k))
    own_q, mate_q = xh * 2 + k, xh * 2 + 1 - k
    far_q, far_mate_q = (1 - xh) * 2 + k, (1 - xh) * 2 + 1 - k
    w_mate = remote(wo, w4.at[own_q], w_ss.at[0], w_rs.at[0], mate)
    w_facing = remote(wo, w4.at[own_q], w_ss.at[1], w_rs.at[1], facing)
    w_relay = remote(w4.at[far_q], w4.at[far_q], w_ss.at[2], w_rs.at[2], mate)
    w_mate.start()
    w_facing.start()
    each(1, 8, lambda o: c_copy(o).start())

    def kv_copy(slot, device, relay=False):
        return [remote(win.at[4] if relay else src, win.at[slot], kv_ss.at[slot, i], kv_rs.at[slot, i], device)
                for i, (src, win) in enumerate(((kh, k_win), (vh, v_win)))]

    def q_copy(slot, device, relay=False):
        return [remote(q_win.at[4] if relay else qh, q_win.at[slot], q_ss.at[slot], q_rs.at[slot], device)]

    def to_row(act):
        @pl.when(xl == 0)
        def _():
            act(kv_copy(4, (across, e)))

        @pl.when(xl == 1)
        def _():
            act(q_copy(4, (across, e)))
        for o in range(1, 4):
            yo = (y + o) % 4

            @pl.when(yo > y)
            def _():
                act(kv_copy(yo - y, (xl * 4 + yo, e)))

            @pl.when(yo < y)
            def _():
                act(q_copy(y - yo, (xl * 4 + yo, e)))

    def relay_row(act):
        for o in range(1, 4):
            yo = (y + o) % 4

            @pl.when((xl == 1) & (yo < y))
            def _():
                act(kv_copy(4 + yo - y, (xl * 4 + yo, e), True))

            @pl.when((xl == 0) & (yo > y))
            def _():
                act(q_copy(4 + y - yo, (xl * 4 + yo, e), True))

    def start(copies):
        for copy in copies:
            copy.start()

    def sent(copies):
        for copy in copies:
            copy.wait_send()

    def received(copies):
        for copy in copies:
            copy.wait_recv()

    to_row(start)

    recv(rx, x_rs)
    for col in range(8):
        x_v[:, col * 256:(col + 1) * 256] = unpack(rx[...], col)
    loads[0].wait()
    loads[1].wait()

    def up(f0, n):
        cols = pl.ds(f0, n)
        a_v[:, cols] = mm(x_v[...], wg_v[:, cols])
        b_v[:, cols] = mm(x_v[...], wu_v[:, cols])

    def up_step(i, _):
        up(pl.multiple_of(i * FC, FC), FC)
        return 0

    ff = wg.shape[1]
    whole = ff // FC
    lax.fori_loop(0, whole, up_step, 0)
    if ff % FC:
        up(whole * FC, ff % FC)
    recv(rg, g_rs)
    for col in range(8):
        g_v[:, col * 256:(col + 1) * 256] = unpack(rg[...], col)
    loads[2].wait()

    def down(f0, n, acc):
        cols = pl.ds(f0, n)
        u = nt(g_v[...], wd_v[cols, :])
        a, b = a_v[:, cols], b_v[:, cols]
        sig = 1.0 / (1.0 + jnp.exp(-a))
        act = a * sig
        da_v[:, cols] = (u * b * sig * (1.0 + a * (1.0 - sig))).astype(BF)
        db_v[:, cols] = (u * act).astype(BF)
        return acc + fold(act * b * u, jnp.add)

    def down_step(i, acc):
        return down(pl.multiple_of(i * FC, FC), FC, acc)

    acc = lax.fori_loop(0, whole, down_step, jnp.zeros((96, 128), F32))
    if ff % FC:
        acc = down(whole * FC, ff % FC, acc)

    def back_step(i, _):
        cols = pl.ds(pl.multiple_of(i * FC, FC), FC)
        dx_v[:, cols] = (nt(da_v[...], wg_v[cols, :]) + nt(db_v[...], wu_v[cols, :])).astype(BF)
        return 0

    lax.fori_loop(0, wg.shape[0] // FC, back_step, 0)
    for j in range(3):
        px[:, j * 256:(j + 1) * 256] = mm(pack_weights(j, 96), stacked(dx_v[...], j)).astype(BF)
    each(1, 16, lambda d: r_copy(d).start())
    rr[own16, :] = px[own16, :]
    d_gate = jnp.broadcast_to(jnp.sum(acc, axis=1, keepdims=True), (96, 128)).astype(BF)
    row = iota((256, 96), 0)
    pack6 = ((iota((256, 96), 1) == (row // 16) * 6 + row % 16) & (row % 16 < 6)).astype(BF)
    dgs[...] = mm(pack6, d_gate).astype(BF)
    each(1, 16, lambda d: t_copy(d).start())
    dgr[own16, :] = dgs[own16, :]

    w_facing.wait_recv()
    w_relay.start()

    @pl.when(xl == 1)
    def _():
        received(kv_copy(4, (across, e)))

    @pl.when(xl == 0)
    def _():
        received(q_copy(4, (across, e)))
    relay_row(start)

    recv(rr, r_rs)
    sums = [mm(selw[j], rr[:, j * 256:(j + 1) * 256]) for j in range(3)]
    parts = [sums[c_ % 3][(c_ // 3) * 64:(c_ // 3) * 64 + 64] for c_ in range(6)]
    parts.append(sums[0][128:192] + sums[1][128:192])
    parts.append(sums[1][192:256] + sums[2][128:192])
    for col in range(8):
        cols = slice(col * 256, (col + 1) * 256)
        low = (grad[:, cols].astype(F32) + parts[col]).astype(BF)
        ag[z, :, cols] = low
        d_hidden[:, cols] = low

    above, under = (c, exp_at(xh, (z + 1) % 4, k)), (c, exp_at(xh, (z + 3) % 4, k))
    z_up, z_down = (z + 1) % 4, (z + 3) % 4
    first, second = pl.ds(0, 32), pl.ds(32, 32)
    g_up = remote(ag.at[z], ag.at[z], ag_ss.at[0], ag_rs.at[0], above)
    g_down = remote(ag.at[z], ag.at[z], ag_ss.at[1], ag_rs.at[1], under)
    g_up2 = remote(ag.at[z_down, first], ag.at[z_down, first], ag_ss.at[2], ag_rs.at[2], above)
    g_down2 = remote(ag.at[z_up, second], ag.at[z_up, second], ag_ss.at[3], ag_rs.at[3], under)
    g_up.start()
    g_down.start()

    each(1, 8, lambda o: c_recv(o))
    total = counts[0]
    for src in range(1, 8):
        total = total + counts[src]

    def doc_start(place):
        start_at = jnp.zeros_like(place)
        for d in range(1, 4):
            first_of = jnp.concatenate([total[d:d + 1]] * (place.shape[1] // 128), axis=1)
            start_at = jnp.maximum(start_at, jnp.where(first_of <= place, first_of, 0))
        return start_at

    for i in (4, 5, 6):
        loads[i].wait()

    def half(i):
        return slice(i * 512, (i + 1) * 512)

    def row_mask(t, d, h):
        key = (c - d) * 1024 + h * 512 + iota((512, 512), 1)
        allowed = key >= start_v[half(t), 0:1]
        if isinstance(d, int) and d == 0:
            allowed = allowed & (key <= c * 1024 + t * 512 + iota((512, 512), 0))
        return allowed

    def key_tiles(t, act):
        act(0, range(t + 1))

        def step(d, _):
            act(d, range(2))
            return 0

        lax.fori_loop(1, jnp.minimum(c, 3) + 1, step, 0)

        @pl.when(xl == 1)
        def _():
            act(4, range(t, 2))

    def statistics(t):
        rows = half(t)
        start_v[rows, :] = doc_start(c * 1024 + t * 512 + iota((512, 128), 0))
        top_v[...] = jnp.full((512, 128), NEG, F32)
        sum_v[...] = jnp.zeros((512, 128), F32)
        o_v[rows, :] = jnp.zeros((512, 128), F32)
        q = q_win[0, rows, :]

        def act(d, halves):
            for h in halves:
                keys = half(h)
                s = jnp.where(row_mask(t, d, h), nt(q, k_win[d, keys, :]) * SCALE, NEG)
                old = top_v[...]
                new = jnp.maximum(old, jnp.max(fold(s, jnp.maximum), axis=1, keepdims=True))
                p = jnp.exp(s - new[:, 0:1])
                fade = jnp.exp(old - new)
                top_v[...] = new
                sum_v[...] = sum_v[...] * fade + fold(p, jnp.add)
                o_v[rows, :] = o_v[rows, :] * fade + mm(p.astype(BF), v_win[d, keys, :])

        key_tiles(t, act)
        norm = jnp.broadcast_to(jnp.sum(sum_v[...], axis=1, keepdims=True), (512, 128))
        o_v[rows, :] = o_v[rows, :] / norm
        lse = top_v[...] + jnp.log(norm)
        lse_v[rows, :] = lse
        lse_win[0, :, rows] = jnp.transpose(lse)[0:8, :]

    def row_copy(win, ss, rs, d):
        return remote(win.at[0], win.at[d], ss.at[d], rs.at[d], ((c + 8 - d) % 8, e))

    def before(act):
        for d in range(1, 5):
            @pl.when(c >= d)
            def _():
                act(d)

    def later(act):
        for d in range(1, 5):
            @pl.when(c + d <= 7)
            def _():
                act(d)

    for slot in range(1, 4):
        @pl.when(c >= slot)
        def _():
            received(kv_copy(slot, (c, e)))
    statistics(0)
    g_up.wait_recv()
    g_up2.start()
    g_down.wait_recv()
    g_down2.start()
    statistics(1)
    before(lambda d: row_copy(lse_win, lse_ss, lse_rs, d).start())
    loads[3].wait()
    w_mate.wait_recv()
    w_relay.wait_recv()
    g_up2.wait_recv()
    g_down2.wait_recv()

    tokens = ag[...].reshape(256, ag.shape[2])
    for q_ in range(4):
        d4[q_] = nt(tokens, w4[q_]).astype(BF).reshape(4, 64, 128)
    pieces = [
        (own_q, e, (xh, k)),
        (mate_q, exp_at(xh, z, 1 - k), (xh, 1 - k)),
        (far_q, exp_at(1 - xh, z, k), (1 - xh, k)),
        (far_mate_q, exp_at(1 - xh, z, 1 - k), (1 - xh, 1 - k)),
    ]

    def piece_copy(i):
        q_, head, _ = pieces[i]
        return remote(d4.at[q_], do_win.at[0, xh, :, k], ex_ss.at[i], ex_rs.at[i], (c, head))

    def piece_across(i):
        q_, head, _ = pieces[i]
        return remote(d4.at[q_], do_win.at[4, xh, :, k], xs_ss.at[i], do_rs.at[4, i], (across, head))

    def piece_along(i, slot, yo, src):
        _, _, (xs, ks) = pieces[i]
        return remote(do_win.at[src, xs, :, ks], do_win.at[slot, xs, :, ks], do_ss.at[slot, i], do_rs.at[slot, i],
                      (xl * 4 + yo, e))

    def along(i, act):
        for o in range(1, 4):
            yo = (y + o) % 4

            @pl.when(yo < y)
            def _():
                act(piece_along(i, y - yo, yo, 0))

    def along_relay(i, act):
        for o in range(1, 4):
            yo = (y + o) % 4

            @pl.when((xl == 0) & (yo > y))
            def _():
                act(piece_along(i, 4 + y - yo, yo, 4))

    for i in (2, 3, 1):
        piece_copy(i).start()

    @pl.when(xl == 1)
    def _():
        for i in (2, 3, 1, 0):
            piece_across(i).start()
    do_win[0, xh, :, k] = d4[own_q]
    along(0, lambda copy: copy.start())

    later(lambda d: received(q_copy(d, (c, e))) if d < 4 else None)

    def key_probs(t, d, halves, masked):
        key = c * 1024 + t * 512 + iota((512, 512), 0)
        for h in halves:
            cols = half(h)
            place = (c + d) * 1024 + h * 512 + iota((1, 512), 1)
            allowed = key >= doc_start(place)
            if masked:
                allowed = allowed & (key <= place)
            s = nt(k_win[0, half(t), :], q_win[d, cols, :]) * SCALE
            p = jnp.where(allowed, jnp.exp(s - lse_win[d, 0:1, cols]), 0.0)
            pt_v[t, d, :, cols] = p.astype(BF)

    def query_tiles(d, act):
        if d == 0:
            act(0, 0, range(2))
            act(1, 0, range(1, 2))
        elif d == 4:
            act(0, 4, range(1))
            act(1, 4, range(2))
        else:
            act(0, d, range(2))
            act(1, d, range(2))

    query_tiles(0, lambda t, d, halves: key_probs(t, d, halves, True))
    for i in (1, 2, 3):
        piece_copy(i).wait_recv()
        along(i, lambda copy: copy.start())

    @pl.when(xl == 0)
    def _():
        for i in range(4):
            piece_across(i).wait_recv()
    for i in range(4):
        along_relay(i, lambda copy: copy.start())

    d_own = do_win[0].reshape(1024, 128)
    prod = d_own.astype(F32) * o_v[...]
    delta_v[...] = jnp.broadcast_to(jnp.sum(prod, axis=1, keepdims=True), (1024, 128))
    high = prod.astype(BF)
    low_part = (prod - high.astype(F32)).astype(BF)
    ones = jnp.ones((8, 128), BF)
    delta_win[0] = nt(ones, high) + nt(ones, low_part)
    before(lambda d: row_copy(delta_win, dl_ss, dl_rs, d).start())
    later(lambda d: row_copy(lse_win, lse_ss, lse_rs, d).wait_recv())

    def probs_step(d, _):
        query_tiles(1, lambda t, _, halves: key_probs(t, d, halves, False))
        return 0

    lax.fori_loop(1, jnp.minimum(7 - c, 3) + 1, probs_step, 0)

    @pl.when(xl == 0)
    def _():
        query_tiles(4, lambda t, d, halves: key_probs(t, d, halves, False))

    for t in range(2):
        rows = half(t)
        dq_v[...] = jnp.zeros((512, 128), F32)
        q = q_win[0, rows, :]
        do = d_own[rows, :]

        def act(d, halves, t=t, rows=rows, q=q, do=do):
            for h in halves:
                keys = half(h)
                k_ = k_win[d, keys, :]
                p = jnp.where(row_mask(t, d, h), jnp.exp(nt(q, k_) * SCALE - lse_v[rows, 0:1]), 0.0)
                ds = p * (nt(do, v_win[d, keys, :]) - delta_v[rows, 0:1])
                dq_v[...] += mm(ds.astype(BF), k_)

        key_tiles(t, act)
        dq_out[rows, :] = (dq_v[...] * SCALE).astype(BF)

    dk_v[...] = jnp.zeros((1024, 128), F32)
    dv_v[...] = jnp.zeros((1024, 128), F32)

    def key_grads(t, d, halves):
        rows = half(t)
        do_all = do_win[d].reshape(1024, 128)
        for h in halves:
            cols = half(h)
            do = do_all[cols, :]
            p = pt_v[t, d, :, cols]
            dv_v[rows, :] += mm(p, do)
            ds = p.astype(F32) * (nt(v_win[0, rows, :], do) - delta_win[d, 0:1, cols])
            dk_v[rows, :] += mm(ds.astype(BF), q_win[d, cols, :])

    query_tiles(0, key_grads)
    later(lambda d: row_copy(delta_win, dl_ss, dl_rs, d).wait_recv())

    def grads_step(d, _):
        for i in range(4):
            piece_along(i, d, y, 0).wait_recv()
        query_tiles(1, lambda t, _, halves: key_grads(t, d, halves))
        return 0

    lax.fori_loop(1, jnp.minimum(7 - c, 3) + 1, grads_step, 0)

    @pl.when(xl == 0)
    def _():
        query_tiles(4, key_grads)
    dk_out[...] = (dk_v[...] * SCALE).astype(BF)
    dv_out[...] = dv_v[...].astype(BF)

    recv(dgr, t_rs)
    row, lane = iota((256, 128), 0), iota((256, 128), 1)
    diag = jnp.where(row % 16 == lane, dgr[...].astype(F32), 0.0).astype(BF)
    gather = (iota((16, 256), 1) // 16 == iota((16, 256), 0)).astype(BF)
    d_gates[...] = mm(gather, diag)[:, 0:6].astype(BF)

    each(1, 16, lambda d: x_copy(d).wait_send())
    each(1, 16, lambda d: g_copy(d).wait_send())
    each(1, 16, lambda d: r_copy(d).wait_send())
    each(1, 16, lambda d: t_copy(d).wait_send())
    each(1, 8, lambda o: c_copy(o).wait_send())
    for copy in [w_mate, w_facing, w_relay, g_up, g_down, g_up2, g_down2]:
        copy.wait_send()
    to_row(sent)
    relay_row(sent)
    before(lambda d: row_copy(lse_win, lse_ss, lse_rs, d).wait_send())
    before(lambda d: row_copy(delta_win, dl_ss, dl_rs, d).wait_send())
    for i in range(1, 4):
        piece_copy(i).wait_send()

    @pl.when(xl == 1)
    def _():
        for i in range(4):
            piece_across(i).wait_send()
    for i in range(4):
        along(i, lambda copy: copy.wait_send())
        along_relay(i, lambda copy: copy.wait_send())


def per_device(q_heads, k_heads, v_heads, doc_ids, w_out, hidden_rows, out_grad, picks, gates, w_gate, w_up, w_down):
    vm, hbm = pl.BlockSpec(memory_space=pltpu.VMEM), pl.BlockSpec(memory_space=pl.ANY)
    tok, width = q_heads.shape
    rows, model = hidden_rows.shape
    ff = w_gate.shape[2]
    dma = pltpu.SemaphoreType.DMA

    def low(*shape):
        return pltpu.VMEM(shape, BF)

    def full(*shape):
        return pltpu.VMEM(shape, F32)

    def out(*shape):
        return jax.ShapeDtypeStruct(shape, BF)

    d_hidden, d_gates, d_queries, d_keys, d_values = pl.pallas_call(
        kernel,
        out_shape=(out(rows, model), out(16, 6), out(tok, width), out(tok, width), out(tok, width)),
        in_specs=[vm] * 5 + [hbm] * 7,
        out_specs=[vm] * 5,
        scratch_shapes=[
            low(model, ff), low(model, ff), low(ff, model), low(4, 128, model),
            low(256, 768), low(256, 768), low(256, 768), low(256, 768),
            low(96, model), low(96, model), full(96, ff), full(96, ff),
            low(96, ff), low(96, ff), low(96, model),
            low(256, 768), low(256, 768), low(256, 128), low(256, 128),
            low(3, 256, 256), low(4, rows, model), low(4, 4, rows, width),
            pltpu.VMEM((8, 128), jnp.int32), pltpu.VMEM((8, 8, 128), jnp.int32),
            low(5, tok, width), low(5, tok, width), low(5, tok, width), low(5, 2, 4, 2, rows, width),
            full(5, 8, tok), full(5, 8, tok), full(512, 128), full(512, 128), full(tok, 128), full(tok, 128),
            full(tok, 128), pltpu.VMEM((tok, 128), jnp.int32),
            low(2, 5, 512, tok), full(512, 128), full(tok, 128), full(tok, 128),
            dma((8,)), dma((16,)), dma((16,)), dma((16,)), dma((16,)), dma((16,)), dma((16,)), dma((16,)), dma((16,)),
            dma((8,)), dma((8,)), dma((3,)), dma((3,)), dma((4,)), dma((4,)), dma((4,)), dma((4,)), dma((4,)),
            dma((5, 2)), dma((5, 2)), dma((5,)), dma((5,)), dma((5, 4)), dma((5, 4)),
            dma((5,)), dma((5,)), dma((5,)), dma((5,)),
        ],
        compiler_params=pltpu.CompilerParams(
            collective_id=0, has_side_effects=True, vmem_limit_bytes=60 * 2**20),
        name="backward",
    )(hidden_rows, out_grad, jnp.transpose(picks, (2, 0, 1)), jnp.transpose(gates, (0, 2, 1)), doc_ids.reshape(8, 128),
      w_gate[0], w_up[0], w_down[0], w_out, q_heads, k_heads, v_heads)
    return (d_queries, d_keys, d_values, d_hidden, d_gates[None])


def solution(mesh):
    return jax.shard_map(
        per_device,
        mesh=mesh,
        in_specs=(
            P("ctx", "exp"),
            P("ctx", "exp"),
            P("ctx", "exp"),
            P("ctx"),
            P("exp", None),
            P(("ctx", "exp"), None),
            P(("ctx", "exp"), None),
            P(("ctx", "exp"), None, None),
            P(("ctx", "exp"), None, None),
            P("exp", None, None),
            P("exp", None, None),
            P("exp", None, None),
        ),
        out_specs=(
            P("ctx", "exp"),
            P("ctx", "exp"),
            P("ctx", "exp"),
            P(("ctx", "exp"), None),
            P(("ctx", "exp"), None, None),
        ),
        check_vma=False,
    )
```

```python
import functools
import math

import jax
import jax.numpy as jnp
from jax import lax
from jax.experimental import pallas as pl
from jax.experimental.pallas import tpu as pltpu
from jax.sharding import PartitionSpec as P

NEG = -1e30
SCALE = 1.0 / math.sqrt(128)
SCALE2 = SCALE * math.log2(math.e)


def nt(a, b):
    return lax.dot_general(a, b, (((1,), (1,)), ((), ())), preferred_element_type=jnp.float32)


def fold(x, op):
    parts = [x[:, i * 128:(i + 1) * 128] for i in range(x.shape[1] // 128)]
    while len(parts) > 1:
        parts = [op(parts[i], parts[i + 1]) for i in range(0, len(parts), 2)]
    return parts[0]


BF = jnp.bfloat16
F32 = jnp.float32
MESH = pl.DeviceIdType.MESH
FC = 256


def iota(shape, dim):
    return lax.broadcasted_iota(jnp.int32, shape, dim)


def mm(a, b):
    return jnp.dot(a, b, preferred_element_type=F32)


def place_in_message(r, j):
    tail = (r - 12, jnp.where(r < 14, r - 8, r - 14), r - 10)[j]
    slot = jnp.where(r < 6, r, jnp.where(r < 12, r - 6, tail))
    block = jnp.where(r < 6, 0, jnp.where(r < 12, 1, 2))
    if j == 1:
        block = jnp.where(r >= 14, 3, block)
    return slot, block


BLOCKS = ((0, 3, 6), (1, 4, 6, 7), (2, 5, 7))


def stacked(array, j, width=256):
    return jnp.concatenate([array[:, c * width:(c + 1) * width] for c in BLOCKS[j]], axis=0)


def pack_weights(j, rows_in_block):
    wide = len(BLOCKS[j]) * rows_in_block
    row = iota((256, wide), 0)
    slot, block = place_in_message(row % 16, j)
    return (iota((256, wide), 1) == block * rows_in_block + (row // 16) * 6 + slot).astype(BF)


def unpack(buf, c):
    lane, i = iota((96, 256), 1), iota((96, 256), 0)
    r, src = lane % 16, lane // 16
    out = None
    for j in range(3):
        if c not in BLOCKS[j]:
            continue
        slot, block = place_in_message(r, j)
        pick = ((i == src * 6 + slot) & (block == BLOCKS[j].index(c))).astype(BF)
        part = mm(pick, buf[:, j * 256:(j + 1) * 256])
        out = part if out is None else out + part
    return out.astype(BF)


def remote(src, dst, ss, rs, device):
    return pltpu.make_async_remote_copy(
        src_ref=src, dst_ref=dst, send_sem=ss, recv_sem=rs, device_id=device, device_id_type=MESH)


def over_rows(x, op):
    parts = [x[i * 8:(i + 1) * 8] for i in range(x.shape[0] // 8)]
    while len(parts) > 1:
        parts = [op(parts[i], parts[i + 1]) for i in range(0, len(parts), 2)]
    return parts[0]


def rows16(ref, i):
    return ref.at[pl.ds(pl.multiple_of(i * 16, 16), 16), :]


def kernel(hidden, grad, picks, gates, docs, wg, wu, wd, wo, qh, kh, vh,
           d_hidden, d_gates, dq_out, dk_out, dv_out,
           wg_v, wu_v, wd_v, w4, sx, sg, rx, rg, x_v, g_v, a_v, b_v, da_v, db_v, dx_v,
           px, rr, dgs, dgr, selw, ag, d4, cnt, counts,
           q_win, k_win, v_win, do_win, lse_win, delta_win, top_v, sum_v, o_v,
           pt_v, dq_v, dk_v, dv_v,
           local_sem, x_ss, x_rs, g_ss, g_rs, r_ss, r_rs, t_ss, t_rs, c_ss, c_rs,
           w_ss, w_rs, ag_ss, ag_rs, ex_ss, ex_rs, xs_ss, kv_ss, kv_rs, q_ss, q_rs, do_ss, do_rs,
           lse_ss, lse_rs, dl_ss, dl_rs):
    c = lax.axis_index("ctx")
    e = lax.axis_index("exp")
    xl, y = c // 4, c % 4
    xh, z, k = e // 8, (e // 2) % 4, e % 2
    across = (c + 4) % 8

    def exp_at(xh_, z_, k_):
        return (xh_ * 4 + z_) * 2 + k_

    def peer(d):
        p = (e + d) % 16
        return p, ((c + 4 * ((p // 8 + xh) % 2)) % 8, p)

    loads = [
        pltpu.make_async_copy(wg, wg_v, local_sem.at[0]),
        pltpu.make_async_copy(wu, wu_v, local_sem.at[1]),
        pltpu.make_async_copy(wd, wd_v, local_sem.at[2]),
        pltpu.make_async_copy(wo, w4.at[xh * 2 + k], local_sem.at[3]),
        pltpu.make_async_copy(qh, q_win.at[0], local_sem.at[4]),
        pltpu.make_async_copy(kh, k_win.at[0], local_sem.at[5]),
        pltpu.make_async_copy(vh, v_win.at[0], local_sem.at[6]),
    ]
    for load in loads:
        load.start()

    barrier = pltpu.get_barrier_semaphore()

    def greet(d, _):
        pl.semaphore_signal(barrier, inc=1, device_id=peer(d)[1], device_id_type=MESH)
        return 0

    lax.fori_loop(1, 16, greet, 0)
    for k_ in range(2):
        pl.semaphore_signal(barrier, inc=1, device_id=(c, exp_at(1 - xh, z, k_)), device_id_type=MESH)

    pl.semaphore_signal(barrier, inc=1, device_id=(across, exp_at(xh, z, 1 - k)), device_id_type=MESH)

    def greet_ctx(o, _):
        pl.semaphore_signal(barrier, inc=1, device_id=((c + o) % 8, e), device_id_type=MESH)
        return 0

    lax.fori_loop(1, 8, greet_ctx, 0)

    row = iota((256, 16), 0)
    spread = (row // 16 == iota((256, 16), 1)).astype(BF)
    pick_rows = nt(spread, jnp.concatenate([picks[i] for i in range(6)], axis=0).astype(F32).astype(BF))
    gate_rows = nt(spread, gates[0])
    r = iota((256, 6), 0) % 16
    lane6 = iota((256, 6), 1)
    hid, gra = hidden[...], grad[...]
    for j in range(3):
        slot, block = place_in_message(r, j)
        mine = lane6 == slot
        pick = jnp.sum(jnp.where(mine, pick_rows, 0.0), axis=1, keepdims=True)
        gate = jnp.sum(jnp.where(mine, gate_rows, 0.0), axis=1, keepdims=True)
        wide = 64 * len(BLOCKS[j])
        target = block[:, 0:1].astype(F32) * 64.0 + pick
        hit = iota((256, wide), 1).astype(F32) == target
        sel = hit.astype(BF)
        sx[:, j * 256:(j + 1) * 256] = mm(sel, stacked(hid, j)).astype(BF)
        sg[:, j * 256:(j + 1) * 256] = mm(sel, stacked(gra, j)).astype(BF)
        if wide == 256:
            hit_w = hit
        else:
            hit_w = iota((256, 256), 1).astype(F32) == target
        selw[j] = jnp.transpose(jnp.where(hit_w, gate, 0.0)).astype(BF)
    sizes = []
    for d in range(8):
        under_d = jnp.sum((docs[...] < d).astype(F32), axis=1, keepdims=True)
        sizes.append(jnp.broadcast_to(jnp.sum(under_d, axis=0, keepdims=True), (1, 128)))
    below = jnp.concatenate(sizes, axis=0).astype(jnp.int32)
    cnt[...] = below
    counts[c] = below

    pl.semaphore_wait(barrier, 15 + 3 + 7)

    def x_copy(d):
        p, device = peer(d)
        return remote(rows16(sx, p), rows16(rx, e), x_ss.at[p], x_rs.at[e], device)

    def g_copy(d):
        p, device = peer(d)
        return remote(rows16(sg, p), rows16(rg, e), g_ss.at[p], g_rs.at[e], device)

    def r_copy(d):
        p, device = peer(d)
        return remote(rows16(px, p), rows16(rr, e), r_ss.at[p], r_rs.at[e], device)

    def t_copy(d):
        p, device = peer(d)
        return remote(rows16(dgs, p), rows16(dgr, e), t_ss.at[p], t_rs.at[e], device)

    def c_copy(o):
        return remote(cnt, counts.at[c], c_ss.at[o], c_rs.at[c], ((c + o) % 8, e))

    def c_recv(o):
        src = (c + o) % 8
        remote(cnt, counts.at[src], c_ss.at[o], c_rs.at[src], (src, e)).wait_recv()

    def recv(buf, rs):
        def one(d, _):
            p, device = peer(d)
            remote(rows16(buf, p), rows16(buf, p), rs.at[p], rs.at[p], device).wait_recv()
            return 0
        lax.fori_loop(1, 16, one, 0)

    def each(n0, n1, act):
        def one(d, _):
            act(d)
            return 0
        lax.fori_loop(n0, n1, one, 0)

    each(1, 16, lambda d: x_copy(d).start())
    each(1, 16, lambda d: g_copy(d).start())
    own16 = pl.ds(pl.multiple_of(e * 16, 16), 16)
    rx[own16, :] = sx[own16, :]
    rg[own16, :] = sg[own16, :]

    def kv_copy(slot, device, relay=False):
        return [remote(win.at[4] if relay else src, win.at[slot], kv_ss.at[slot, i], kv_rs.at[slot, i], device)
                for i, (src, win) in enumerate(((kh, k_win), (vh, v_win)))]

    def q_copy(slot, device, relay=False):
        return [remote(q_win.at[4] if relay else qh, q_win.at[slot], q_ss.at[slot], q_rs.at[slot], device)]

    def to_row(act):
        @pl.when(xl == 0)
        def _():
            act(kv_copy(4, (across, e)))

        @pl.when(xl == 1)
        def _():
            act(q_copy(4, (across, e)))
        for o in range(1, 4):
            yo = (y + o) % 4

            @pl.when(yo > y)
            def _():
                act(kv_copy(yo - y, (xl * 4 + yo, e)))

            @pl.when(yo < y)
            def _():
                act(q_copy(y - yo, (xl * 4 + yo, e)))

    def relay_row(act):
        for o in range(1, 4):
            yo = (y + o) % 4

            @pl.when((xl == 1) & (yo < y))
            def _():
                act(kv_copy(4 + yo - y, (xl * 4 + yo, e), True))

            @pl.when((xl == 0) & (yo > y))
            def _():
                act(q_copy(4 + y - yo, (xl * 4 + yo, e), True))

    def start(copies):
        for copy in copies:
            copy.start()

    def sent(copies):
        for copy in copies:
            copy.wait_send()

    def received(copies):
        for copy in copies:
            copy.wait_recv()

    to_row(start)

    mate = (c, exp_at(xh, z, 1 - k))
    facing = (across, exp_at(1 - xh, z, k))
    own_q, mate_q = xh * 2 + k, xh * 2 + 1 - k
    far_q, far_mate_q = (1 - xh) * 2 + k, (1 - xh) * 2 + 1 - k
    w_mate = remote(wo, w4.at[own_q], w_ss.at[0], w_rs.at[0], mate)
    w_facing = remote(wo, w4.at[own_q], w_ss.at[1], w_rs.at[1], facing)
    w_relay = remote(w4.at[far_q], w4.at[far_q], w_ss.at[2], w_rs.at[2], mate)
    w_mate.start()
    w_facing.start()
    each(1, 8, lambda o: c_copy(o).start())

    recv(rx, x_rs)
    for col in range(8):
        x_v[:, col * 256:(col + 1) * 256] = unpack(rx[...], col)
    loads[0].wait()
    loads[1].wait()

    def up(f0, n):
        cols = pl.ds(f0, n)
        a_v[:, cols] = mm(x_v[...], wg_v[:, cols])
        b_v[:, cols] = mm(x_v[...], wu_v[:, cols])

    def up_step(i, _):
        up(pl.multiple_of(i * FC, FC), FC)
        return 0

    ff = wg.shape[1]
    whole = ff // FC
    lax.fori_loop(0, whole, up_step, 0)
    if ff % FC:
        up(whole * FC, ff % FC)
    recv(rg, g_rs)
    for col in range(8):
        g_v[:, col * 256:(col + 1) * 256] = unpack(rg[...], col)
    loads[2].wait()

    def down(f0, n, acc):
        cols = pl.ds(f0, n)
        u = nt(g_v[...], wd_v[cols, :])
        a, b = a_v[:, cols], b_v[:, cols]
        sig = 1.0 / (1.0 + jnp.exp(-a))
        act = a * sig
        da_v[:, cols] = (u * b * sig * (1.0 + a * (1.0 - sig))).astype(BF)
        db_v[:, cols] = (u * act).astype(BF)
        return acc + fold(act * b * u, jnp.add)

    def down_step(i, acc):
        return down(pl.multiple_of(i * FC, FC), FC, acc)

    acc = lax.fori_loop(0, whole, down_step, jnp.zeros((96, 128), F32))
    if ff % FC:
        acc = down(whole * FC, ff % FC, acc)

    @pl.when(xl == 1)
    def _():
        received(kv_copy(4, (across, e)))

    @pl.when(xl == 0)
    def _():
        received(q_copy(4, (across, e)))
    relay_row(start)

    def back_step(i, _):
        cols = pl.ds(pl.multiple_of(i * FC, FC), FC)
        dx_v[:, cols] = (nt(da_v[...], wg_v[cols, :]) + nt(db_v[...], wu_v[cols, :])).astype(BF)
        return 0

    lax.fori_loop(0, wg.shape[0] // FC, back_step, 0)
    for j in range(3):
        px[:, j * 256:(j + 1) * 256] = mm(pack_weights(j, 96), stacked(dx_v[...], j)).astype(BF)
    each(1, 16, lambda d: r_copy(d).start())
    rr[own16, :] = px[own16, :]
    d_gate = jnp.broadcast_to(jnp.sum(acc, axis=1, keepdims=True), (96, 128)).astype(BF)
    row = iota((256, 96), 0)
    pack6 = ((iota((256, 96), 1) == (row // 16) * 6 + row % 16) & (row % 16 < 6)).astype(BF)
    dgs[...] = mm(pack6, d_gate).astype(BF)
    each(1, 16, lambda d: t_copy(d).start())
    dgr[own16, :] = dgs[own16, :]

    w_facing.wait_recv()
    w_relay.start()

    each(1, 8, lambda o: c_recv(o))
    total = counts[0]
    for src in range(1, 8):
        total = total + counts[src]

    def doc_start(place):
        start_at = jnp.zeros_like(place)
        for d in range(1, 4):
            first_of = jnp.concatenate([total[d:d + 1]] * (place.shape[1] // 128), axis=1)
            start_at = jnp.maximum(start_at, jnp.where(first_of <= place, first_of, 0))
        return start_at

    for i in (4, 5, 6):
        loads[i].wait()

    def half(i):
        return slice(i * 512, (i + 1) * 512)

    starts = [doc_start(c * 1024 + t * 512 + iota((1, 512), 1)) for t in range(2)]

    def seen(t, d, h):
        key = (c - d) * 1024 + h * 512 + iota((512, 512), 0)
        allowed = key >= starts[t]
        if isinstance(d, int) and d == 0:
            allowed = allowed & (key <= c * 1024 + t * 512 + iota((512, 512), 1))
        return allowed

    def key_halves(t, d):
        if isinstance(d, int):
            return range(t + 1) if d == 0 else range(t, 2)
        return range(2)

    top_v[...] = jnp.full((8, 1024), NEG, F32)
    sum_v[...] = jnp.zeros((8, 1024), F32)
    o_v[...] = jnp.zeros((128, 1024), F32)

    def statistics(d):
        for t in range(2):
            cols = half(t)
            halves = key_halves(t, d)
            q = q_win[0, cols, :]
            scores = [jnp.where(seen(t, d, h), nt(k_win[d, half(h), :], q) * SCALE2, NEG) for h in halves]
            most = functools.reduce(jnp.maximum, [over_rows(s, jnp.maximum) for s in scores])
            old = top_v[:, cols]
            new = jnp.maximum(old, jnp.max(most, axis=0, keepdims=True))
            fade = jnp.exp2(old - new)
            probs = [jnp.exp2(s - new[0:1]) for s in scores]
            top_v[:, cols] = new
            sum_v[:, cols] = sum_v[:, cols] * fade + sum(over_rows(p, jnp.add) for p in probs)
            o_v[:, cols] = o_v[:, cols] * fade[0:1] + sum(
                mm(jnp.transpose(v_win[d, half(h), :]), p.astype(BF)) for h, p in zip(halves, probs))

    def statistics_step(d, _):
        received(kv_copy(d, (c, e)))
        statistics(d)
        return 0

    last_before = jnp.minimum(c, 3)
    direct = jnp.minimum(y, 1)
    statistics(0)

    @pl.when(xl == 1)
    def _():
        statistics(4)
    lax.fori_loop(1, direct + 1, statistics_step, 0)

    recv(rr, r_rs)
    sums = [mm(selw[j], rr[:, j * 256:(j + 1) * 256]) for j in range(3)]
    parts = [sums[c_ % 3][(c_ // 3) * 64:(c_ // 3) * 64 + 64] for c_ in range(6)]
    parts.append(sums[0][128:192] + sums[1][128:192])
    parts.append(sums[1][192:256] + sums[2][128:192])
    for col in range(8):
        cols = slice(col * 256, (col + 1) * 256)
        low = (grad[:, cols].astype(F32) + parts[col]).astype(BF)
        ag[z, :, cols] = low
        d_hidden[:, cols] = low

    above, under = (c, exp_at(xh, (z + 1) % 4, k)), (c, exp_at(xh, (z + 3) % 4, k))
    z_up, z_down = (z + 1) % 4, (z + 3) % 4
    first, second = pl.ds(0, 32), pl.ds(32, 32)
    g_up = remote(ag.at[z], ag.at[z], ag_ss.at[0], ag_rs.at[0], above)
    g_down = remote(ag.at[z], ag.at[z], ag_ss.at[1], ag_rs.at[1], under)
    g_up2 = remote(ag.at[z_down, first], ag.at[z_down, first], ag_ss.at[2], ag_rs.at[2], above)
    g_down2 = remote(ag.at[z_up, second], ag.at[z_up, second], ag_ss.at[3], ag_rs.at[3], under)
    g_up.start()
    g_down.start()

    middle = jnp.minimum(direct + 3, last_before + 1)
    lax.fori_loop(direct + 1, middle, statistics_step, 0)
    g_up.wait_recv()
    g_up2.start()
    g_down.wait_recv()
    g_down2.start()
    lax.fori_loop(middle, last_before + 1, statistics_step, 0)
    norm = jnp.sum(sum_v[...], axis=0, keepdims=True)
    lse_win[0] = top_v[...] + jnp.log(norm) * math.log2(math.e)

    def row_copy(win, ss, rs, d):
        return remote(win.at[0], win.at[d], ss.at[d], rs.at[d], ((c + 8 - d) % 8, e))

    def before(act):
        for d in range(1, 5):
            @pl.when(c >= d)
            def _():
                act(d)

    def later(act):
        for d in range(1, 5):
            @pl.when(c + d <= 7)
            def _():
                act(d)

    before(lambda d: row_copy(lse_win, lse_ss, lse_rs, d).start())
    loads[3].wait()
    w_mate.wait_recv()
    w_relay.wait_recv()
    g_up2.wait_recv()
    g_down2.wait_recv()

    tokens = ag[...].reshape(256, ag.shape[2])
    for q_ in range(4):
        d4[q_] = nt(tokens, w4[q_]).astype(BF).reshape(4, 64, 128)
    pieces = [
        (own_q, e, (xh, k)),
        (mate_q, exp_at(xh, z, 1 - k), (xh, 1 - k)),
        (far_q, exp_at(1 - xh, z, k), (1 - xh, k)),
        (far_mate_q, exp_at(1 - xh, z, 1 - k), (1 - xh, 1 - k)),
    ]

    def piece_copy(i):
        q_, head, _ = pieces[i]
        return remote(d4.at[q_], do_win.at[0, xh, :, k], ex_ss.at[i], ex_rs.at[i], (c, head))

    def piece_across(i):
        q_, head, _ = pieces[i]
        return remote(d4.at[q_], do_win.at[4, xh, :, k], xs_ss.at[i], do_rs.at[4, i], (across, head))

    def piece_along(i, slot, yo, src):
        _, _, (xs, ks) = pieces[i]
        return remote(do_win.at[src, xs, :, ks], do_win.at[slot, xs, :, ks], do_ss.at[slot, i], do_rs.at[slot, i],
                      (xl * 4 + yo, e))

    def along(i, act):
        for o in range(1, 4):
            yo = (y + o) % 4

            @pl.when(yo < y)
            def _():
                act(piece_along(i, y - yo, yo, 0))

    def along_relay(i, act):
        for o in range(1, 4):
            yo = (y + o) % 4

            @pl.when((xl == 0) & (yo > y))
            def _():
                act(piece_along(i, 4 + y - yo, yo, 4))

    for i in (2, 3, 1):
        piece_copy(i).start()

    @pl.when(xl == 1)
    def _():
        for i in (2, 3, 1, 0):
            piece_across(i).start()
    do_win[0, xh, :, k] = d4[own_q]
    along(0, lambda copy: copy.start())

    def key_probs(t, d, halves, masked):
        key = c * 1024 + t * 512 + iota((512, 512), 0)
        for h in halves:
            cols = half(h)
            place = (c + d) * 1024 + h * 512 + iota((1, 512), 1)
            allowed = key >= doc_start(place)
            if masked:
                allowed = allowed & (key <= place)
            s = nt(k_win[0, half(t), :], q_win[d, cols, :]) * SCALE2
            p = jnp.where(allowed, jnp.exp2(s - lse_win[d, 0:1, cols]), 0.0)
            pt_v[t, d, :, cols] = p.astype(BF)

    def query_tiles(d, act):
        if d == 0:
            act(0, 0, range(2))
            act(1, 0, range(1, 2))
        elif d == 4:
            act(0, 4, range(1))
            act(1, 4, range(2))
        else:
            act(0, d, range(2))
            act(1, d, range(2))

    def probs_step(d, _):
        received(q_copy(d, (c, e)))
        row_copy(lse_win, lse_ss, lse_rs, d).wait_recv()
        query_tiles(1, lambda t, _, halves: key_probs(t, d, halves, False))
        return 0

    last_after = jnp.minimum(7 - c, 3)
    query_tiles(0, lambda t, d, halves: key_probs(t, d, halves, True))
    piece_copy(1).wait_recv()
    along(1, lambda copy: copy.start())
    lax.fori_loop(1, jnp.minimum(last_after, 1) + 1, probs_step, 0)
    for i in (2, 3):
        piece_copy(i).wait_recv()
        along(i, lambda copy: copy.start())

    @pl.when(xl == 0)
    def _():
        for i in range(4):
            piece_across(i).wait_recv()
    for i in range(4):
        along_relay(i, lambda copy: copy.start())

    d_own = do_win[0].reshape(1024, 128)
    prod = d_own.astype(F32) * jnp.transpose(o_v[...] / norm)
    high = prod.astype(BF)
    low_part = (prod - high.astype(F32)).astype(BF)
    ones = jnp.ones((8, 128), BF)
    delta_win[0] = nt(ones, high) + nt(ones, low_part)
    before(lambda d: row_copy(delta_win, dl_ss, dl_rs, d).start())
    lax.fori_loop(2, last_after + 1, probs_step, 0)

    @pl.when(xl == 0)
    def _():
        row_copy(lse_win, lse_ss, lse_rs, 4).wait_recv()
        query_tiles(4, lambda t, d, halves: key_probs(t, d, halves, False))

    dq_v[...] = jnp.zeros((128, 1024), F32)

    def query_grads(d):
        for t in range(2):
            cols = half(t)
            q = q_win[0, cols, :]
            do = d_own[cols, :]
            acc = dq_v[:, cols]
            for h in key_halves(t, d):
                keys = k_win[d, half(h), :]
                p = jnp.exp2(nt(keys, q) * SCALE2 - lse_win[0, 0:1, cols])
                p = jnp.where(seen(t, d, h), p, 0.0)
                ds = p * (nt(v_win[d, half(h), :], do) - delta_win[0, 0:1, cols])
                acc = acc + mm(jnp.transpose(keys), ds.astype(BF))
            dq_v[:, cols] = acc

    def query_step(d, _):
        query_grads(d)
        return 0

    query_grads(0)
    lax.fori_loop(1, last_before + 1, query_step, 0)

    @pl.when(xl == 1)
    def _():
        query_grads(4)
    dq_out[...] = (jnp.transpose(dq_v[...]) * SCALE).astype(BF)

    dk_v[...] = jnp.zeros((1024, 128), F32)
    dv_v[...] = jnp.zeros((1024, 128), F32)

    def key_grads(t, d, halves):
        rows = half(t)
        do_all = do_win[d].reshape(1024, 128)
        cols = slice(halves[0] * 512, halves[-1] * 512 + 512)
        do = do_all[cols, :]
        p = pt_v[t, d, :, cols]
        dv_v[rows, :] += mm(p, do)
        ds = p.astype(F32) * (nt(v_win[0, rows, :], do) - delta_win[d, 0:1, cols])
        dk_v[rows, :] += mm(ds.astype(BF), q_win[d, cols, :])

    query_tiles(0, key_grads)

    def grads_step(d, _):
        for i in range(4):
            piece_along(i, d, y, 0).wait_recv()
        row_copy(delta_win, dl_ss, dl_rs, d).wait_recv()
        query_tiles(1, lambda t, _, halves: key_grads(t, d, halves))
        return 0

    lax.fori_loop(1, last_after + 1, grads_step, 0)

    @pl.when(xl == 0)
    def _():
        row_copy(delta_win, dl_ss, dl_rs, 4).wait_recv()
        query_tiles(4, key_grads)
    dk_out[...] = (dk_v[...] * SCALE).astype(BF)
    dv_out[...] = dv_v[...].astype(BF)

    recv(dgr, t_rs)
    row, lane = iota((256, 128), 0), iota((256, 128), 1)
    diag = jnp.where(row % 16 == lane, dgr[...].astype(F32), 0.0).astype(BF)
    gather = (iota((16, 256), 1) // 16 == iota((16, 256), 0)).astype(BF)
    d_gates[0] = jnp.transpose(mm(gather, diag))[0:6].astype(BF)

    each(1, 16, lambda d: x_copy(d).wait_send())
    each(1, 16, lambda d: g_copy(d).wait_send())
    each(1, 16, lambda d: r_copy(d).wait_send())
    each(1, 16, lambda d: t_copy(d).wait_send())
    each(1, 8, lambda o: c_copy(o).wait_send())
    for copy in [w_mate, w_facing, w_relay, g_up, g_down, g_up2, g_down2]:
        copy.wait_send()
    to_row(sent)
    relay_row(sent)
    before(lambda d: row_copy(lse_win, lse_ss, lse_rs, d).wait_send())
    before(lambda d: row_copy(delta_win, dl_ss, dl_rs, d).wait_send())
    for i in range(1, 4):
        piece_copy(i).wait_send()

    @pl.when(xl == 1)
    def _():
        for i in range(4):
            piece_across(i).wait_send()
    for i in range(4):
        along(i, lambda copy: copy.wait_send())
        along_relay(i, lambda copy: copy.wait_send())


def hand_over(*refs):
    n = len(refs) // 3
    held, sems = refs[2 * n:3 * n], refs[-1]
    reads = [pltpu.make_async_copy(refs[i], held[i], sems.at[i]) for i in range(n)]
    writes = [pltpu.make_async_copy(held[i], refs[n + i], sems.at[n + i]) for i in range(n)]
    for read in reads:
        read.start()
    for read, write in zip(reads, writes):
        read.wait()
        write.start()
    for write in writes:
        write.wait()


def per_device(q_heads, k_heads, v_heads, doc_ids, w_out, hidden_rows, out_grad, picks, gates, w_gate, w_up, w_down):
    vm, hbm = pl.BlockSpec(memory_space=pltpu.VMEM), pl.BlockSpec(memory_space=pl.ANY)
    tok, width = q_heads.shape
    rows, model = hidden_rows.shape
    ff = w_gate.shape[2]
    dma = pltpu.SemaphoreType.DMA

    def low(*shape):
        return pltpu.VMEM(shape, BF)

    def full(*shape):
        return pltpu.VMEM(shape, F32)

    def out(*shape):
        return jax.ShapeDtypeStruct(shape, BF)

    shapes = (out(rows, model), out(1, 6, 16), out(tok, width), out(tok, width), out(tok, width))
    results = pl.pallas_call(
        kernel,
        out_shape=shapes,
        in_specs=[vm] * 5 + [hbm] * 7,
        out_specs=[vm] * 5,
        scratch_shapes=[
            low(model, ff), low(model, ff), low(ff, model), low(4, 128, model),
            low(256, 768), low(256, 768), low(256, 768), low(256, 768),
            low(96, model), low(96, model), full(96, ff), full(96, ff),
            low(96, ff), low(96, ff), low(96, model),
            low(256, 768), low(256, 768), low(256, 128), low(256, 128),
            low(3, 256, 256), low(4, rows, model), low(4, 4, rows, width),
            pltpu.VMEM((8, 128), jnp.int32), pltpu.VMEM((8, 8, 128), jnp.int32),
            low(5, tok, width), low(5, tok, width), low(5, tok, width), low(5, 2, 4, 2, rows, width),
            full(5, 8, tok), full(5, 8, tok), full(8, tok), full(8, tok), full(128, tok),
            low(2, 5, 512, tok), full(128, tok), full(tok, 128), full(tok, 128),
            dma((8,)), dma((16,)), dma((16,)), dma((16,)), dma((16,)), dma((16,)), dma((16,)), dma((16,)), dma((16,)),
            dma((8,)), dma((8,)), dma((3,)), dma((3,)), dma((4,)), dma((4,)), dma((4,)), dma((4,)), dma((4,)),
            dma((5, 2)), dma((5, 2)), dma((5,)), dma((5,)), dma((5, 4)), dma((5, 4)),
            dma((5,)), dma((5,)), dma((5,)), dma((5,)),
        ],
        compiler_params=pltpu.CompilerParams(
            collective_id=0, has_side_effects=True, vmem_limit_bytes=60 * 2**20),
        name="backward",
    )(hidden_rows, out_grad, jnp.transpose(picks, (2, 0, 1)), jnp.transpose(gates, (0, 2, 1)), doc_ids.reshape(8, 128),
      w_gate[0], w_up[0], w_down[0], w_out, q_heads, k_heads, v_heads)
    d_hidden, d_gates, d_queries, d_keys, d_values = pl.pallas_call(
        hand_over,
        out_shape=shapes,
        in_specs=[hbm] * 5,
        out_specs=[hbm] * 5,
        scratch_shapes=[pltpu.VMEM(shape.shape, BF) for shape in shapes] + [dma((10,))],
        compiler_params=pltpu.CompilerParams(vmem_limit_bytes=60 * 2**20),
        name="results",
    )(*results)
    return (d_queries, d_keys, d_values, d_hidden, jnp.transpose(d_gates, (0, 2, 1)))


def solution(mesh):
    return jax.shard_map(
        per_device,
        mesh=mesh,
        in_specs=(
            P("ctx", "exp"),
            P("ctx", "exp"),
            P("ctx", "exp"),
            P("ctx"),
            P("exp", None),
            P(("ctx", "exp"), None),
            P(("ctx", "exp"), None),
            P(("ctx", "exp"), None, None),
            P(("ctx", "exp"), None, None),
            P("exp", None, None),
            P("exp", None, None),
            P("exp", None, None),
        ),
        out_specs=(
            P("ctx", "exp"),
            P("ctx", "exp"),
            P("ctx", "exp"),
            P(("ctx", "exp"), None),
            P(("ctx", "exp"), None, None),
        ),
        check_vma=False,
    )
```

```python
import functools
import math

import jax
import jax.numpy as jnp
from jax import lax
from jax.experimental import pallas as pl
from jax.experimental.pallas import tpu as pltpu
from jax.sharding import PartitionSpec as P

NEG = -1e30
SCALE = 1.0 / math.sqrt(128)
SCALE2 = SCALE * math.log2(math.e)


def nt(a, b):
    return lax.dot_general(a, b, (((1,), (1,)), ((), ())), preferred_element_type=jnp.float32)


def fold(x, op):
    parts = [x[:, i * 128:(i + 1) * 128] for i in range(x.shape[1] // 128)]
    while len(parts) > 1:
        parts = [op(parts[i], parts[i + 1]) for i in range(0, len(parts), 2)]
    return parts[0]


BF = jnp.bfloat16
F32 = jnp.float32
MESH = pl.DeviceIdType.MESH
FC = 256


def iota(shape, dim):
    return lax.broadcasted_iota(jnp.int32, shape, dim)


def mm(a, b):
    return jnp.dot(a, b, preferred_element_type=F32)


def place_in_message(r, j):
    tail = (r - 12, jnp.where(r < 14, r - 8, r - 14), r - 10)[j]
    slot = jnp.where(r < 6, r, jnp.where(r < 12, r - 6, tail))
    block = jnp.where(r < 6, 0, jnp.where(r < 12, 1, 2))
    if j == 1:
        block = jnp.where(r >= 14, 3, block)
    return slot, block


BLOCKS = ((0, 3, 6), (1, 4, 6, 7), (2, 5, 7))


def stacked(array, j, width=256):
    return jnp.concatenate([array[:, c * width:(c + 1) * width] for c in BLOCKS[j]], axis=0)


def pack_weights(j, rows_in_block):
    wide = len(BLOCKS[j]) * rows_in_block
    row = iota((256, wide), 0)
    slot, block = place_in_message(row % 16, j)
    return (iota((256, wide), 1) == block * rows_in_block + (row // 16) * 6 + slot).astype(BF)


def unpack(buf, c):
    lane, i = iota((96, 256), 1), iota((96, 256), 0)
    r, src = lane % 16, lane // 16
    out = None
    for j in range(3):
        if c not in BLOCKS[j]:
            continue
        slot, block = place_in_message(r, j)
        pick = ((i == src * 6 + slot) & (block == BLOCKS[j].index(c))).astype(BF)
        part = mm(pick, buf[:, j * 256:(j + 1) * 256])
        out = part if out is None else out + part
    return out.astype(BF)


def remote(src, dst, ss, rs, device):
    return pltpu.make_async_remote_copy(
        src_ref=src, dst_ref=dst, send_sem=ss, recv_sem=rs, device_id=device, device_id_type=MESH)


def over_rows(x, op):
    parts = [x[i * 8:(i + 1) * 8] for i in range(x.shape[0] // 8)]
    while len(parts) > 1:
        parts = [op(parts[i], parts[i + 1]) for i in range(0, len(parts), 2)]
    return parts[0]


def rows16(ref, i):
    return ref.at[pl.ds(pl.multiple_of(i * 16, 16), 16), :]


def kernel(hidden, grad, picks, gates, docs, wg, wu, wd, wo, qh, kh, vh,
           d_hidden, d_gates, dq_out, dk_out, dv_out,
           wgu_v, wd_v, w4, sx, sg, rx, rg, x_v, g_v, a_v, b_v, da_v, db_v, dx_v,
           px, rr, dgs, dgr, selw, ag, d4, cnt, counts,
           q_win, k_win, v_win, do_win, lse_win, delta_win, top_v, sum_v, o_v,
           pt_v, tops_v, dq_v, dk_v, dv_v,
           local_sem, x_ss, x_rs, g_ss, g_rs, r_ss, r_rs, t_ss, t_rs, c_ss, c_rs,
           w_ss, w_rs, ag_ss, ag_rs, ex_ss, ex_rs, xs_ss, kv_ss, kv_rs, q_ss, q_rs, do_ss, do_rs,
           lse_ss, lse_rs, dl_ss, dl_rs):
    c = lax.axis_index("ctx")
    e = lax.axis_index("exp")
    xl, y = c // 4, c % 4
    xh, z, k = e // 8, (e // 2) % 4, e % 2
    across = (c + 4) % 8

    def exp_at(xh_, z_, k_):
        return (xh_ * 4 + z_) * 2 + k_

    def peer(d):
        p = (e + d) % 16
        return p, ((c + 4 * ((p // 8 + xh) % 2)) % 8, p)

    wg_v, wu_v = wgu_v.at[0], wgu_v.at[1]

    loads = [
        pltpu.make_async_copy(wg, wg_v, local_sem.at[0]),
        pltpu.make_async_copy(wu, wu_v, local_sem.at[1]),
        pltpu.make_async_copy(wd, wd_v, local_sem.at[2]),
        pltpu.make_async_copy(wo, w4.at[xh * 2 + k], local_sem.at[3]),
        pltpu.make_async_copy(qh, q_win.at[0], local_sem.at[4]),
        pltpu.make_async_copy(kh, k_win.at[0], local_sem.at[5]),
        pltpu.make_async_copy(vh, v_win.at[0], local_sem.at[6]),
    ]
    for load in loads:
        load.start()

    barrier = pltpu.get_barrier_semaphore()

    def greet(d, _):
        pl.semaphore_signal(barrier, inc=1, device_id=peer(d)[1], device_id_type=MESH)
        return 0

    lax.fori_loop(1, 16, greet, 0)
    for k_ in range(2):
        pl.semaphore_signal(barrier, inc=1, device_id=(c, exp_at(1 - xh, z, k_)), device_id_type=MESH)

    pl.semaphore_signal(barrier, inc=1, device_id=(across, exp_at(xh, z, 1 - k)), device_id_type=MESH)

    def greet_ctx(o, _):
        pl.semaphore_signal(barrier, inc=1, device_id=((c + o) % 8, e), device_id_type=MESH)
        return 0

    lax.fori_loop(1, 8, greet_ctx, 0)

    row = iota((256, 16), 0)
    spread = (row // 16 == iota((256, 16), 1)).astype(BF)
    pick_rows = nt(spread, jnp.concatenate([picks[i] for i in range(6)], axis=0).astype(F32).astype(BF))
    gate_rows = nt(spread, gates[0])
    r = iota((256, 6), 0) % 16
    lane6 = iota((256, 6), 1)
    hid, gra = hidden[...], grad[...]
    sels = []
    for j in range(3):
        slot, block = place_in_message(r, j)
        mine = lane6 == slot
        pick = jnp.sum(jnp.where(mine, pick_rows, 0.0), axis=1, keepdims=True)
        gate = jnp.sum(jnp.where(mine, gate_rows, 0.0), axis=1, keepdims=True)
        wide = 64 * len(BLOCKS[j])
        target = block[:, 0:1].astype(F32) * 64.0 + pick
        hit = iota((256, wide), 1).astype(F32) == target
        sel = hit.astype(BF)
        sels.append((sel, target, gate, hit))
        sx[:, j * 256:(j + 1) * 256] = mm(sel, stacked(hid, j)).astype(BF)
    pl.semaphore_wait(barrier, 15 + 3 + 7)

    def x_copy(d):
        p, device = peer(d)
        return remote(rows16(sx, p), rows16(rx, e), x_ss.at[p], x_rs.at[e], device)

    def g_copy(d):
        p, device = peer(d)
        return remote(rows16(sg, p), rows16(rg, e), g_ss.at[p], g_rs.at[e], device)

    def r_copy(d):
        p, device = peer(d)
        return remote(rows16(px, p), rows16(rr, e), r_ss.at[p], r_rs.at[e], device)

    def t_copy(d):
        p, device = peer(d)
        return remote(rows16(dgs, p), rows16(dgr, e), t_ss.at[p], t_rs.at[e], device)

    def c_copy(o):
        return remote(cnt, counts.at[c], c_ss.at[o], c_rs.at[c], ((c + o) % 8, e))

    def c_recv(o):
        src = (c + o) % 8
        remote(cnt, counts.at[src], c_ss.at[o], c_rs.at[src], (src, e)).wait_recv()

    def recv(buf, rs):
        def one(d, _):
            p, device = peer(d)
            remote(rows16(buf, p), rows16(buf, p), rs.at[p], rs.at[p], device).wait_recv()
            return 0
        lax.fori_loop(1, 16, one, 0)

    def each(n0, n1, act):
        def one(d, _):
            act(d)
            return 0
        lax.fori_loop(n0, n1, one, 0)

    def kv_copy(slot, device, relay=False, which=(0, 1)):
        pairs = ((kh, k_win), (vh, v_win))
        return [remote(pairs[i][1].at[4] if relay else pairs[i][0], pairs[i][1].at[slot], kv_ss.at[slot, i],
                       kv_rs.at[slot, i], device) for i in which]

    def q_copy(slot, device, relay=False):
        return [remote(q_win.at[4] if relay else qh, q_win.at[slot], q_ss.at[slot], q_rs.at[slot], device)]

    def to_half(act):
        @pl.when(xl == 0)
        def _():
            act(kv_copy(4, (across, e)))

        @pl.when(xl == 1)
        def _():
            act(q_copy(4, (across, e)))

    def to_row(act):
        for o in range(1, 4):
            yo = (y + o) % 4

            @pl.when(yo > y)
            def _():
                act(kv_copy(yo - y, (xl * 4 + yo, e)))

            @pl.when(yo < y)
            def _():
                act(q_copy(y - yo, (xl * 4 + yo, e)))

    def relay_row(act, which):
        for o in range(1, 4):
            yo = (y + o) % 4

            @pl.when((xl == 1) & (yo < y))
            def _():
                act(kv_copy(4 + yo - y, (xl * 4 + yo, e), True, (which,)))

            if which == 0:
                @pl.when((xl == 0) & (yo > y))
                def _():
                    act(q_copy(4 + y - yo, (xl * 4 + yo, e), True))

    def start(copies):
        for copy in copies:
            copy.start()

    def sent(copies):
        for copy in copies:
            copy.wait_send()

    def received(copies):
        for copy in copies:
            copy.wait_recv()

    each(1, 16, lambda d: x_copy(d).start())
    to_half(start)
    for j in range(3):
        sg[:, j * 256:(j + 1) * 256] = mm(sels[j][0], stacked(gra, j)).astype(BF)
    each(1, 16, lambda d: g_copy(d).start())
    to_row(start)
    own16 = pl.ds(pl.multiple_of(e * 16, 16), 16)
    rx[own16, :] = sx[own16, :]
    rg[own16, :] = sg[own16, :]

    mate = (c, exp_at(xh, z, 1 - k))
    facing = (across, exp_at(1 - xh, z, k))
    own_q, mate_q = xh * 2 + k, xh * 2 + 1 - k
    far_q, far_mate_q = (1 - xh) * 2 + k, (1 - xh) * 2 + 1 - k
    w_mate = remote(wo, w4.at[own_q], w_ss.at[0], w_rs.at[0], mate)
    w_facing = remote(wo, w4.at[own_q], w_ss.at[1], w_rs.at[1], facing)
    w_relay = remote(w4.at[far_q], w4.at[far_q], w_ss.at[2], w_rs.at[2], mate)
    w_mate.start()

    sizes = []
    for d in range(8):
        under_d = jnp.sum((docs[...] < d).astype(F32), axis=1, keepdims=True)
        sizes.append(jnp.broadcast_to(jnp.sum(under_d, axis=0, keepdims=True), (1, 128)))
    below = jnp.concatenate(sizes, axis=0).astype(jnp.int32)
    cnt[...] = below
    counts[c] = below
    each(1, 8, lambda o: c_copy(o).start())
    for j in range(3):
        _, target, gate, hit = sels[j]
        if hit.shape[1] < 256:
            hit = iota((256, 256), 1).astype(F32) == target
        selw[j] = jnp.transpose(jnp.where(hit, gate, 0.0)).astype(BF)

    @pl.when(xl == 1)
    def _():
        received(kv_copy(4, (across, e), which=(0,)))

    @pl.when(xl == 0)
    def _():
        received(q_copy(4, (across, e)))
    relay_row(start, 0)

    recv(rx, x_rs)
    for col in range(8):
        x_v[:, col * 256:(col + 1) * 256] = unpack(rx[...], col)
    loads[0].wait()
    loads[1].wait()

    def up(f0, n):
        cols = pl.ds(f0, n)
        a_v[:, cols] = mm(x_v[...], wg_v[:, cols])
        b_v[:, cols] = mm(x_v[...], wu_v[:, cols])

    def up_step(i, _):
        up(pl.multiple_of(i * FC, FC), FC)
        return 0

    ff = wg.shape[1]
    whole = ff // FC
    lax.fori_loop(0, whole, up_step, 0)
    if ff % FC:
        up(whole * FC, ff % FC)

    @pl.when(xl == 1)
    def _():
        received(kv_copy(4, (across, e), which=(1,)))
    relay_row(start, 1)
    recv(rg, g_rs)
    w_facing.start()
    for col in range(8):
        g_v[:, col * 256:(col + 1) * 256] = unpack(rg[...], col)
    loads[2].wait()

    def down(f0, n, acc):
        cols = pl.ds(f0, n)
        u = nt(g_v[...], wd_v[cols, :])
        a, b = a_v[:, cols], b_v[:, cols]
        sig = 1.0 / (1.0 + jnp.exp(-a))
        act = a * sig
        da_v[:, cols] = (u * b * sig * (1.0 + a * (1.0 - sig))).astype(BF)
        db_v[:, cols] = (u * act).astype(BF)
        return acc + fold(act * b * u, jnp.add)

    def down_step(i, acc):
        return down(pl.multiple_of(i * FC, FC), FC, acc)

    acc = lax.fori_loop(0, whole, down_step, jnp.zeros((96, 128), F32))
    if ff % FC:
        acc = down(whole * FC, ff % FC, acc)

    def back_step(i, _):
        cols = pl.ds(pl.multiple_of(i * FC, FC), FC)
        dx_v[:, cols] = (nt(da_v[...], wg_v[cols, :]) + nt(db_v[...], wu_v[cols, :])).astype(BF)
        return 0

    lax.fori_loop(0, wg.shape[0] // FC, back_step, 0)
    for j in range(3):
        px[:, j * 256:(j + 1) * 256] = mm(pack_weights(j, 96), stacked(dx_v[...], j)).astype(BF)
    each(1, 16, lambda d: r_copy(d).start())
    rr[own16, :] = px[own16, :]
    d_gate = jnp.broadcast_to(jnp.sum(acc, axis=1, keepdims=True), (96, 128)).astype(BF)
    row = iota((256, 96), 0)
    pack6 = ((iota((256, 96), 1) == (row // 16) * 6 + row % 16) & (row % 16 < 6)).astype(BF)
    dgs[...] = mm(pack6, d_gate).astype(BF)
    each(1, 16, lambda d: t_copy(d).start())
    dgr[own16, :] = dgs[own16, :]

    w_facing.wait_recv()
    w_relay.start()

    each(1, 8, lambda o: c_recv(o))
    total = counts[0]
    for src in range(1, 8):
        total = total + counts[src]

    def doc_start(place):
        start_at = jnp.zeros_like(place)
        for d in range(1, 4):
            first_of = jnp.concatenate([total[d:d + 1]] * (place.shape[1] // 128), axis=1)
            start_at = jnp.maximum(start_at, jnp.where(first_of <= place, first_of, 0))
        return start_at

    for i in (4, 5, 6):
        loads[i].wait()

    def half(i):
        return slice(i * 512, (i + 1) * 512)

    starts = [doc_start(c * 1024 + t * 512 + iota((1, 512), 1)) for t in range(2)]

    def seen(t, d, h):
        key = (c - d) * 1024 + h * 512 + iota((512, 512), 0)
        allowed = key >= starts[t]
        if isinstance(d, int) and d == 0:
            allowed = allowed & (key <= c * 1024 + t * 512 + iota((512, 512), 1))
        return allowed

    def key_halves(t, d):
        if isinstance(d, int):
            return range(t + 1) if d == 0 else range(t, 2)
        return range(2)

    def kept_probs(d, first, n, cols):
        if isinstance(d, int) and d == 0:
            return wd_v.at[first:first + n, cols]
        return wgu_v.at[(d - 1) // 2, pl.ds(pl.multiple_of((d - 1) % 2 * 1024 + first, 512), n), cols]

    top_v[...] = jnp.full((8, 1024), NEG, F32)
    sum_v[...] = jnp.zeros((8, 1024), F32)
    o_v[...] = jnp.zeros((128, 1024), F32)

    def statistics(d):
        for t in range(2):
            cols = half(t)
            halves = key_halves(t, d)
            q = q_win[0, cols, :]
            scores = [jnp.where(seen(t, d, h), nt(k_win[d, half(h), :], q) * SCALE2, NEG) for h in halves]
            most = functools.reduce(jnp.maximum, [over_rows(s, jnp.maximum) for s in scores])
            old = top_v[:, cols]
            new = jnp.maximum(old, jnp.max(most, axis=0, keepdims=True))
            fade = jnp.exp2(old - new)
            probs = [jnp.exp2(s - new[0:1]) for s in scores]
            top_v[:, cols] = new
            tops_v[d, :, cols] = new
            for h, p in zip(halves, probs):
                kept_probs(d, h * 512, 512, cols)[...] = p.astype(BF)
            sum_v[:, cols] = sum_v[:, cols] * fade + sum(over_rows(p, jnp.add) for p in probs)
            o_v[:, cols] = o_v[:, cols] * fade[0:1] + sum(
                mm(jnp.transpose(v_win[d, half(h), :]), p.astype(BF)) for h, p in zip(halves, probs))

    def statistics_step(d, _):
        received(kv_copy(d, (c, e)))
        statistics(d)
        return 0

    last_before = jnp.minimum(c, 3)
    direct = jnp.minimum(y, 1)
    statistics(0)

    @pl.when(xl == 1)
    def _():
        statistics(4)
    lax.fori_loop(1, direct + 1, statistics_step, 0)

    recv(rr, r_rs)
    sums = [mm(selw[j], rr[:, j * 256:(j + 1) * 256]) for j in range(3)]
    parts = [sums[c_ % 3][(c_ // 3) * 64:(c_ // 3) * 64 + 64] for c_ in range(6)]
    parts.append(sums[0][128:192] + sums[1][128:192])
    parts.append(sums[1][192:256] + sums[2][128:192])
    for col in range(8):
        cols = slice(col * 256, (col + 1) * 256)
        low = (grad[:, cols].astype(F32) + parts[col]).astype(BF)
        ag[z, :, cols] = low
        d_hidden[:, cols] = low

    above, under = (c, exp_at(xh, (z + 1) % 4, k)), (c, exp_at(xh, (z + 3) % 4, k))
    z_up, z_down = (z + 1) % 4, (z + 3) % 4
    first, second = pl.ds(0, 32), pl.ds(32, 32)
    g_up = remote(ag.at[z], ag.at[z], ag_ss.at[0], ag_rs.at[0], above)
    g_down = remote(ag.at[z], ag.at[z], ag_ss.at[1], ag_rs.at[1], under)
    g_up2 = remote(ag.at[z_down, first], ag.at[z_down, first], ag_ss.at[2], ag_rs.at[2], above)
    g_down2 = remote(ag.at[z_up, second], ag.at[z_up, second], ag_ss.at[3], ag_rs.at[3], under)
    g_up.start()
    g_down.start()

    middle = jnp.minimum(direct + 3, last_before + 1)
    lax.fori_loop(direct + 1, middle, statistics_step, 0)
    g_up.wait_recv()
    g_up2.start()
    g_down.wait_recv()
    g_down2.start()
    lax.fori_loop(middle, last_before + 1, statistics_step, 0)
    norm = jnp.sum(sum_v[...], axis=0, keepdims=True)
    lse_win[0] = top_v[...] + jnp.log(norm) * math.log2(math.e)

    def row_copy(win, ss, rs, d):
        return remote(win.at[0], win.at[d], ss.at[d], rs.at[d], ((c + 8 - d) % 8, e))

    def before(act):
        for d in range(1, 5):
            @pl.when(c >= d)
            def _():
                act(d)

    def later(act):
        for d in range(1, 5):
            @pl.when(c + d <= 7)
            def _():
                act(d)

    before(lambda d: row_copy(lse_win, lse_ss, lse_rs, d).start())
    loads[3].wait()
    w_mate.wait_recv()
    w_relay.wait_recv()
    g_up2.wait_recv()
    g_down2.wait_recv()

    tokens = ag[...].reshape(256, ag.shape[2])
    for q_ in range(4):
        d4[q_] = nt(tokens, w4[q_]).astype(BF).reshape(4, 64, 128)
    pieces = [
        (own_q, e, (xh, k)),
        (mate_q, exp_at(xh, z, 1 - k), (xh, 1 - k)),
        (far_q, exp_at(1 - xh, z, k), (1 - xh, k)),
        (far_mate_q, exp_at(1 - xh, z, 1 - k), (1 - xh, 1 - k)),
    ]

    def piece_copy(i):
        q_, head, _ = pieces[i]
        return remote(d4.at[q_], do_win.at[0, xh, :, k], ex_ss.at[i], ex_rs.at[i], (c, head))

    def piece_across(i):
        q_, head, _ = pieces[i]
        return remote(d4.at[q_], do_win.at[4, xh, :, k], xs_ss.at[i], do_rs.at[4, i], (across, head))

    def piece_along(i, slot, yo, src):
        _, _, (xs, ks) = pieces[i]
        return remote(do_win.at[src, xs, :, ks], do_win.at[slot, xs, :, ks], do_ss.at[slot, i], do_rs.at[slot, i],
                      (xl * 4 + yo, e))

    def along(i, act):
        for o in range(1, 4):
            yo = (y + o) % 4

            @pl.when(yo < y)
            def _():
                act(piece_along(i, y - yo, yo, 0))

    def along_relay(i, act):
        for o in range(1, 4):
            yo = (y + o) % 4

            @pl.when((xl == 0) & (yo > y))
            def _():
                act(piece_along(i, 4 + y - yo, yo, 4))

    for i in (2, 3, 1):
        piece_copy(i).start()

    @pl.when(xl == 1)
    def _():
        for i in (2, 3, 1, 0):
            piece_across(i).start()
    do_win[0, xh, :, k] = d4[own_q]
    along(0, lambda copy: copy.start())

    def key_probs(t, d, halves, masked):
        key = c * 1024 + t * 512 + iota((512, 512), 0)
        for h in halves:
            cols = half(h)
            place = (c + d) * 1024 + h * 512 + iota((1, 512), 1)
            allowed = key >= doc_start(place)
            if masked:
                allowed = allowed & (key <= place)
            s = nt(k_win[0, half(t), :], q_win[d, cols, :]) * SCALE2
            p = jnp.where(allowed, jnp.exp2(s - lse_win[d, 0:1, cols]), 0.0)
            pt_v[t, d, :, cols] = p.astype(BF)

    def query_tiles(d, act):
        if d == 0:
            act(0, 0, range(2))
            act(1, 0, range(1, 2))
        elif d == 4:
            act(0, 4, range(1))
            act(1, 4, range(2))
        else:
            act(0, d, range(2))
            act(1, d, range(2))

    def probs_step(d, _):
        received(q_copy(d, (c, e)))
        row_copy(lse_win, lse_ss, lse_rs, d).wait_recv()
        query_tiles(1, lambda t, _, halves: key_probs(t, d, halves, False))
        return 0

    last_after = jnp.minimum(7 - c, 3)
    query_tiles(0, lambda t, d, halves: key_probs(t, d, halves, True))
    piece_copy(1).wait_recv()
    along(1, lambda copy: copy.start())
    lax.fori_loop(1, jnp.minimum(last_after, 1) + 1, probs_step, 0)
    for i in (2, 3):
        piece_copy(i).wait_recv()
        along(i, lambda copy: copy.start())

    for i in range(4):
        @pl.when(xl == 0)
        def _():
            piece_across(i).wait_recv()
        along_relay(i, lambda copy: copy.start())

    d_own = do_win[0].reshape(1024, 128)
    prod = d_own.astype(F32) * jnp.transpose(o_v[...] / norm)
    high = prod.astype(BF)
    low_part = (prod - high.astype(F32)).astype(BF)
    ones = jnp.ones((8, 128), BF)
    delta_win[0] = nt(ones, high) + nt(ones, low_part)
    before(lambda d: row_copy(delta_win, dl_ss, dl_rs, d).start())
    lax.fori_loop(2, last_after + 1, probs_step, 0)

    @pl.when(xl == 0)
    def _():
        row_copy(lse_win, lse_ss, lse_rs, 4).wait_recv()
        query_tiles(4, lambda t, d, halves: key_probs(t, d, halves, False))

    dq_v[...] = jnp.zeros((128, 1024), F32)

    def query_grads(d):
        for t in range(2):
            cols = half(t)
            do = d_own[cols, :]
            acc = dq_v[:, cols]
            fade = jnp.exp2(tops_v[d, 0:1, cols] - lse_win[0, 0:1, cols])
            faded_delta = delta_win[0, 0:1, cols] * fade
            halves = key_halves(t, d)
            rows = slice(halves[0] * 512, halves[-1] * 512 + 512)
            dp = nt(v_win[d, rows, :], do)
            kept = kept_probs(d, rows.start, rows.stop - rows.start, cols)[...]
            ds = kept.astype(F32) * (dp * fade - faded_delta)
            acc = acc + mm(jnp.transpose(k_win[d, rows, :]), ds.astype(BF))
            dq_v[:, cols] = acc

    def query_step(d, _):
        query_grads(d)
        return 0

    query_grads(0)
    lax.fori_loop(1, last_before + 1, query_step, 0)

    @pl.when(xl == 1)
    def _():
        query_grads(4)
    dq_out[...] = (jnp.transpose(dq_v[...]) * SCALE).astype(BF)

    dk_v[...] = jnp.zeros((1024, 128), F32)
    dv_v[...] = jnp.zeros((1024, 128), F32)

    def key_grads(t, d, halves):
        rows = half(t)
        do_all = do_win[d].reshape(1024, 128)
        cols = slice(halves[0] * 512, halves[-1] * 512 + 512)
        do = do_all[cols, :]
        p = pt_v[t, d, :, cols]
        dv_v[rows, :] += mm(p, do)
        ds = p.astype(F32) * (nt(v_win[0, rows, :], do) - delta_win[d, 0:1, cols])
        dk_v[rows, :] += mm(ds.astype(BF), q_win[d, cols, :])

    query_tiles(0, key_grads)

    def grads_step(d, _):
        for i in range(4):
            piece_along(i, d, y, 0).wait_recv()
        row_copy(delta_win, dl_ss, dl_rs, d).wait_recv()
        query_tiles(1, lambda t, _, halves: key_grads(t, d, halves))
        return 0

    lax.fori_loop(1, last_after + 1, grads_step, 0)

    @pl.when(xl == 0)
    def _():
        row_copy(delta_win, dl_ss, dl_rs, 4).wait_recv()
        query_tiles(4, key_grads)
    dk_out[...] = (dk_v[...] * SCALE).astype(BF)
    dv_out[...] = dv_v[...].astype(BF)

    recv(dgr, t_rs)
    row, lane = iota((256, 128), 0), iota((256, 128), 1)
    diag = jnp.where(row % 16 == lane, dgr[...].astype(F32), 0.0).astype(BF)
    gather = (iota((16, 256), 1) // 16 == iota((16, 256), 0)).astype(BF)
    d_gates[0] = jnp.transpose(mm(gather, diag))[0:6].astype(BF)

    each(1, 16, lambda d: x_copy(d).wait_send())
    each(1, 16, lambda d: g_copy(d).wait_send())
    each(1, 16, lambda d: r_copy(d).wait_send())
    each(1, 16, lambda d: t_copy(d).wait_send())
    each(1, 8, lambda o: c_copy(o).wait_send())
    for copy in [w_mate, w_facing, w_relay, g_up, g_down, g_up2, g_down2]:
        copy.wait_send()
    to_half(sent)
    to_row(sent)
    relay_row(sent, 0)
    relay_row(sent, 1)
    before(lambda d: row_copy(lse_win, lse_ss, lse_rs, d).wait_send())
    before(lambda d: row_copy(delta_win, dl_ss, dl_rs, d).wait_send())
    for i in range(1, 4):
        piece_copy(i).wait_send()

    @pl.when(xl == 1)
    def _():
        for i in range(4):
            piece_across(i).wait_send()
    for i in range(4):
        along(i, lambda copy: copy.wait_send())
        along_relay(i, lambda copy: copy.wait_send())


def hand_over(*refs):
    n = len(refs) // 3
    held, sems = refs[2 * n:3 * n], refs[-1]
    reads = [pltpu.make_async_copy(refs[i], held[i], sems.at[i]) for i in range(n)]
    writes = [pltpu.make_async_copy(held[i], refs[n + i], sems.at[n + i]) for i in range(n)]
    for read in reads:
        read.start()
    for read, write in zip(reads, writes):
        read.wait()
        write.start()
    for write in writes:
        write.wait()


def per_device(q_heads, k_heads, v_heads, doc_ids, w_out, hidden_rows, out_grad, picks, gates, w_gate, w_up, w_down):
    vm, hbm = pl.BlockSpec(memory_space=pltpu.VMEM), pl.BlockSpec(memory_space=pl.ANY)
    tok, width = q_heads.shape
    rows, model = hidden_rows.shape
    ff = w_gate.shape[2]
    dma = pltpu.SemaphoreType.DMA

    def low(*shape):
        return pltpu.VMEM(shape, BF)

    def full(*shape):
        return pltpu.VMEM(shape, F32)

    def out(*shape):
        return jax.ShapeDtypeStruct(shape, BF)

    shapes = (out(rows, model), out(1, 6, 16), out(tok, width), out(tok, width), out(tok, width))
    results = pl.pallas_call(
        kernel,
        out_shape=shapes,
        in_specs=[vm] * 5 + [hbm] * 7,
        out_specs=[vm] * 5,
        scratch_shapes=[
            low(2, model, ff), low(ff, model), low(4, 128, model),
            low(256, 768), low(256, 768), low(256, 768), low(256, 768),
            low(96, model), low(96, model), full(96, ff), full(96, ff),
            low(96, ff), low(96, ff), low(96, model),
            low(256, 768), low(256, 768), low(256, 128), low(256, 128),
            low(3, 256, 256), low(4, rows, model), low(4, 4, rows, width),
            pltpu.VMEM((8, 128), jnp.int32), pltpu.VMEM((8, 8, 128), jnp.int32),
            low(5, tok, width), low(5, tok, width), low(5, tok, width), low(5, 2, 4, 2, rows, width),
            full(5, 8, tok), full(5, 8, tok), full(8, tok), full(8, tok), full(128, tok),
            low(2, 5, 512, tok), full(5, 8, tok), full(128, tok), full(tok, 128), full(tok, 128),
            dma((8,)), dma((16,)), dma((16,)), dma((16,)), dma((16,)), dma((16,)), dma((16,)), dma((16,)), dma((16,)),
            dma((8,)), dma((8,)), dma((3,)), dma((3,)), dma((4,)), dma((4,)), dma((4,)), dma((4,)), dma((4,)),
            dma((5, 2)), dma((5, 2)), dma((5,)), dma((5,)), dma((5, 4)), dma((5, 4)),
            dma((5,)), dma((5,)), dma((5,)), dma((5,)),
        ],
        compiler_params=pltpu.CompilerParams(
            collective_id=0, has_side_effects=True, vmem_limit_bytes=60 * 2**20),
        name="backward",
    )(hidden_rows, out_grad, jnp.transpose(picks, (2, 0, 1)), jnp.transpose(gates, (0, 2, 1)), doc_ids.reshape(8, 128),
      w_gate[0], w_up[0], w_down[0], w_out, q_heads, k_heads, v_heads)
    d_hidden, d_gates, d_queries, d_keys, d_values = pl.pallas_call(
        hand_over,
        out_shape=shapes,
        in_specs=[hbm] * 5,
        out_specs=[hbm] * 5,
        scratch_shapes=[pltpu.VMEM(shape.shape, BF) for shape in shapes] + [dma((10,))],
        compiler_params=pltpu.CompilerParams(vmem_limit_bytes=60 * 2**20),
        name="results",
    )(*results)
    return (d_queries, d_keys, d_values, d_hidden, jnp.transpose(d_gates, (0, 2, 1)))


def solution(mesh):
    return jax.shard_map(
        per_device,
        mesh=mesh,
        in_specs=(
            P("ctx", "exp"),
            P("ctx", "exp"),
            P("ctx", "exp"),
            P("ctx"),
            P("exp", None),
            P(("ctx", "exp"), None),
            P(("ctx", "exp"), None),
            P(("ctx", "exp"), None, None),
            P(("ctx", "exp"), None, None),
            P("exp", None, None),
            P("exp", None, None),
            P("exp", None, None),
        ),
        out_specs=(
            P("ctx", "exp"),
            P("ctx", "exp"),
            P("ctx", "exp"),
            P(("ctx", "exp"), None),
            P(("ctx", "exp"), None, None),
        ),
        check_vma=False,
    )
```

```python
import functools
import math

import jax
import jax.numpy as jnp
from jax import lax
from jax.experimental import pallas as pl
from jax.experimental.pallas import tpu as pltpu
from jax.sharding import PartitionSpec as P

NEG = -1e30
SCALE = 1.0 / math.sqrt(128)
SCALE2 = SCALE * math.log2(math.e)


def nt(a, b):
    return lax.dot_general(a, b, (((1,), (1,)), ((), ())), preferred_element_type=jnp.float32)


def fold(x, op):
    parts = [x[:, i * 128:(i + 1) * 128] for i in range(x.shape[1] // 128)]
    while len(parts) > 1:
        parts = [op(parts[i], parts[i + 1]) for i in range(0, len(parts), 2)]
    return parts[0]


BF = jnp.bfloat16
F32 = jnp.float32
MESH = pl.DeviceIdType.MESH
FC = 256


def iota(shape, dim):
    return lax.broadcasted_iota(jnp.int32, shape, dim)


def mm(a, b):
    return jnp.dot(a, b, preferred_element_type=F32)


def place_in_message(r, j):
    tail = (r - 12, jnp.where(r < 14, r - 8, r - 14), r - 10)[j]
    slot = jnp.where(r < 6, r, jnp.where(r < 12, r - 6, tail))
    block = jnp.where(r < 6, 0, jnp.where(r < 12, 1, 2))
    if j == 1:
        block = jnp.where(r >= 14, 3, block)
    return slot, block


BLOCKS = ((0, 3, 6), (1, 4, 6, 7), (2, 5, 7))


def stacked(array, j, width=256):
    return jnp.concatenate([array[:, c * width:(c + 1) * width] for c in BLOCKS[j]], axis=0)


def pack_weights(j, rows_in_block):
    wide = len(BLOCKS[j]) * rows_in_block
    row = iota((256, wide), 0)
    slot, block = place_in_message(row % 16, j)
    return (iota((256, wide), 1) == block * rows_in_block + (row // 16) * 6 + slot).astype(BF)


def unpack(buf, c):
    lane, i = iota((96, 256), 1), iota((96, 256), 0)
    r, src = lane % 16, lane // 16
    out = None
    for j in range(3):
        if c not in BLOCKS[j]:
            continue
        slot, block = place_in_message(r, j)
        pick = ((i == src * 6 + slot) & (block == BLOCKS[j].index(c))).astype(BF)
        part = mm(pick, buf[:, j * 256:(j + 1) * 256])
        out = part if out is None else out + part
    return out.astype(BF)


def remote(src, dst, ss, rs, device):
    return pltpu.make_async_remote_copy(
        src_ref=src, dst_ref=dst, send_sem=ss, recv_sem=rs, device_id=device, device_id_type=MESH)


def over_rows(x, op):
    parts = [x[i * 8:(i + 1) * 8] for i in range(x.shape[0] // 8)]
    while len(parts) > 1:
        parts = [op(parts[i], parts[i + 1]) for i in range(0, len(parts), 2)]
    return parts[0]


def rows16(ref, i):
    return ref.at[pl.ds(pl.multiple_of(i * 16, 16), 16), :]


def kernel(hidden, grad, picks, gates, docs, wg, wu, wd, wo, qh, kh, vh,
           d_hidden, d_gates, dq_out, dk_out, dv_out,
           wgu_v, wd_v, w4, sx, sg, rx, rg, x_v, g_v, a_v, b_v, da_v, db_v, dx_v,
           px, rr, dgs, dgr, selw, ag, d4, cnt, counts,
           q_win, k_win, v_win, do_win, lse_win, delta_win, top_v, sum_v, o_v,
           pt_v, tops_v, dq_v, dk_v, dv_v,
           local_sem, x_ss, x_rs, g_ss, g_rs, r_ss, r_rs, t_ss, t_rs, c_ss, c_rs,
           w_ss, w_rs, ag_ss, ag_rs, ex_ss, ex_rs, xs_ss, kv_ss, kv_rs, q_ss, q_rs, do_ss, do_rs,
           lse_ss, lse_rs, dl_ss, dl_rs):
    c = lax.axis_index("ctx")
    e = lax.axis_index("exp")
    xl, y = c // 4, c % 4
    xh, z, k = e // 8, (e // 2) % 4, e % 2
    across = (c + 4) % 8

    def exp_at(xh_, z_, k_):
        return (xh_ * 4 + z_) * 2 + k_

    def peer(d):
        p = (e + d) % 16
        return p, ((c + 4 * ((p // 8 + xh) % 2)) % 8, p)

    wg_v, wu_v = wgu_v.at[0], wgu_v.at[1]

    loads = [
        pltpu.make_async_copy(wg, wg_v, local_sem.at[0]),
        pltpu.make_async_copy(wu, wu_v, local_sem.at[1]),
        pltpu.make_async_copy(wd, wd_v, local_sem.at[2]),
        pltpu.make_async_copy(wo, w4.at[xh * 2 + k], local_sem.at[3]),
        pltpu.make_async_copy(qh, q_win.at[0], local_sem.at[4]),
        pltpu.make_async_copy(kh, k_win.at[0], local_sem.at[5]),
        pltpu.make_async_copy(vh, v_win.at[0], local_sem.at[6]),
    ]
    for load in loads:
        load.start()

    barrier = pltpu.get_barrier_semaphore()

    def greet(d, _):
        pl.semaphore_signal(barrier, inc=1, device_id=peer(d)[1], device_id_type=MESH)
        return 0

    lax.fori_loop(1, 16, greet, 0)
    for k_ in range(2):
        pl.semaphore_signal(barrier, inc=1, device_id=(c, exp_at(1 - xh, z, k_)), device_id_type=MESH)

    pl.semaphore_signal(barrier, inc=1, device_id=(across, exp_at(xh, z, 1 - k)), device_id_type=MESH)

    def greet_ctx(o, _):
        pl.semaphore_signal(barrier, inc=1, device_id=((c + o) % 8, e), device_id_type=MESH)
        return 0

    lax.fori_loop(1, 8, greet_ctx, 0)

    row = iota((256, 16), 0)
    spread = (row // 16 == iota((256, 16), 1)).astype(BF)
    pick_rows = nt(spread, jnp.concatenate([picks[i] for i in range(6)], axis=0).astype(F32).astype(BF))
    gate_rows = nt(spread, gates[0])
    r = iota((256, 6), 0) % 16
    lane6 = iota((256, 6), 1)
    hid, gra = hidden[...], grad[...]
    sels = []
    for j in range(3):
        slot, block = place_in_message(r, j)
        mine = lane6 == slot
        pick = jnp.sum(jnp.where(mine, pick_rows, 0.0), axis=1, keepdims=True)
        gate = jnp.sum(jnp.where(mine, gate_rows, 0.0), axis=1, keepdims=True)
        wide = 64 * len(BLOCKS[j])
        target = block[:, 0:1].astype(F32) * 64.0 + pick
        hit = iota((256, wide), 1).astype(F32) == target
        sel = hit.astype(BF)
        sels.append((sel, target, gate, hit))
        sx[:, j * 256:(j + 1) * 256] = mm(sel, stacked(hid, j)).astype(BF)
    pl.semaphore_wait(barrier, 15 + 3 + 7)

    def x_copy(d):
        p, device = peer(d)
        return remote(rows16(sx, p), rows16(rx, e), x_ss.at[p], x_rs.at[e], device)

    def g_copy(d):
        p, device = peer(d)
        return remote(rows16(sg, p), rows16(rg, e), g_ss.at[p], g_rs.at[e], device)

    def r_copy(d):
        p, device = peer(d)
        return remote(rows16(px, p), rows16(rr, e), r_ss.at[p], r_rs.at[e], device)

    def t_copy(d):
        p, device = peer(d)
        return remote(rows16(dgs, p), rows16(dgr, e), t_ss.at[p], t_rs.at[e], device)

    def c_copy(o):
        return remote(cnt, counts.at[c], c_ss.at[o], c_rs.at[c], ((c + o) % 8, e))

    def c_recv(o):
        src = (c + o) % 8
        remote(cnt, counts.at[src], c_ss.at[o], c_rs.at[src], (src, e)).wait_recv()

    def recv(buf, rs):
        def one(d, _):
            p, device = peer(d)
            remote(rows16(buf, p), rows16(buf, p), rs.at[p], rs.at[p], device).wait_recv()
            return 0
        lax.fori_loop(1, 16, one, 0)

    def each(n0, n1, act):
        def one(d, _):
            act(d)
            return 0
        lax.fori_loop(n0, n1, one, 0)

    def kv_copy(slot, device, relay=False, which=(0, 1)):
        pairs = ((kh, k_win), (vh, v_win))
        return [remote(pairs[i][1].at[4] if relay else pairs[i][0], pairs[i][1].at[slot], kv_ss.at[slot, i],
                       kv_rs.at[slot, i], device) for i in which]

    def q_copy(slot, device, relay=False):
        return [remote(q_win.at[4] if relay else qh, q_win.at[slot], q_ss.at[slot], q_rs.at[slot], device)]

    def to_half(act):
        @pl.when(xl == 0)
        def _():
            act(kv_copy(4, (across, e)))

        @pl.when(xl == 1)
        def _():
            act(q_copy(4, (across, e)))

    def to_row(act):
        for o in range(1, 4):
            yo = (y + o) % 4

            @pl.when(yo > y)
            def _():
                act(kv_copy(yo - y, (xl * 4 + yo, e)))

            @pl.when(yo < y)
            def _():
                act(q_copy(y - yo, (xl * 4 + yo, e)))

    def relay_row(act, which):
        for o in range(1, 4):
            yo = (y + o) % 4

            @pl.when((xl == 1) & (yo < y))
            def _():
                act(kv_copy(4 + yo - y, (xl * 4 + yo, e), True, (which,)))

            if which == 0:
                @pl.when((xl == 0) & (yo > y))
                def _():
                    act(q_copy(4 + y - yo, (xl * 4 + yo, e), True))

    def start(copies):
        for copy in copies:
            copy.start()

    def sent(copies):
        for copy in copies:
            copy.wait_send()

    def received(copies):
        for copy in copies:
            copy.wait_recv()

    each(1, 16, lambda d: x_copy(d).start())
    to_half(start)
    for j in range(3):
        sg[:, j * 256:(j + 1) * 256] = mm(sels[j][0], stacked(gra, j)).astype(BF)
    each(1, 16, lambda d: g_copy(d).start())
    to_row(start)
    own16 = pl.ds(pl.multiple_of(e * 16, 16), 16)
    rx[own16, :] = sx[own16, :]
    rg[own16, :] = sg[own16, :]

    mate = (c, exp_at(xh, z, 1 - k))
    facing = (across, exp_at(1 - xh, z, k))
    own_q, mate_q = xh * 2 + k, xh * 2 + 1 - k
    far_q, far_mate_q = (1 - xh) * 2 + k, (1 - xh) * 2 + 1 - k
    w_mate = remote(wo, w4.at[own_q], w_ss.at[0], w_rs.at[0], mate)
    w_facing = remote(wo, w4.at[own_q], w_ss.at[1], w_rs.at[1], facing)
    w_relay = remote(w4.at[far_q], w4.at[far_q], w_ss.at[2], w_rs.at[2], mate)
    w_mate.start()

    sizes = []
    for d in range(8):
        under_d = jnp.sum((docs[...] < d).astype(F32), axis=1, keepdims=True)
        sizes.append(jnp.broadcast_to(jnp.sum(under_d, axis=0, keepdims=True), (1, 128)))
    below = jnp.concatenate(sizes, axis=0).astype(jnp.int32)
    cnt[...] = below
    counts[c] = below
    each(1, 8, lambda o: c_copy(o).start())
    for j in range(3):
        _, target, gate, hit = sels[j]
        if hit.shape[1] < 256:
            hit = iota((256, 256), 1).astype(F32) == target
        selw[j] = jnp.transpose(jnp.where(hit, gate, 0.0)).astype(BF)

    @pl.when(xl == 1)
    def _():
        received(kv_copy(4, (across, e), which=(0,)))

    @pl.when(xl == 0)
    def _():
        received(q_copy(4, (across, e)))
    relay_row(start, 0)

    recv(rx, x_rs)
    for col in range(8):
        x_v[:, col * 256:(col + 1) * 256] = unpack(rx[...], col)
    loads[0].wait()
    loads[1].wait()

    def up(f0, n):
        cols = pl.ds(f0, n)
        a_v[:, cols] = mm(x_v[...], wg_v[:, cols])
        b_v[:, cols] = mm(x_v[...], wu_v[:, cols])

    ff = wg.shape[1]
    chunks = [(f0, min(FC, ff - f0)) for f0 in range(0, ff, FC)]
    for f0, n in chunks:
        up(f0, n)

    @pl.when(xl == 1)
    def _():
        received(kv_copy(4, (across, e), which=(1,)))
    relay_row(start, 1)
    recv(rg, g_rs)
    w_facing.start()
    for col in range(8):
        g_v[:, col * 256:(col + 1) * 256] = unpack(rg[...], col)
    loads[2].wait()

    def down(f0, n, acc):
        cols = pl.ds(f0, n)
        u = nt(g_v[...], wd_v[cols, :])
        a, b = a_v[:, cols], b_v[:, cols]
        sig = 1.0 / (1.0 + jnp.exp(-a))
        act = a * sig
        da_v[:, cols] = (u * b * sig * (1.0 + a * (1.0 - sig))).astype(BF)
        db_v[:, cols] = (u * act).astype(BF)
        return acc + fold(act * b * u, jnp.add)

    acc = jnp.zeros((96, 128), F32)
    for f0, n in chunks:
        acc = down(f0, n, acc)

    for d0 in range(0, wg.shape[0], FC):
        cols = pl.ds(d0, FC)
        dx_v[:, cols] = (nt(da_v[...], wg_v[cols, :]) + nt(db_v[...], wu_v[cols, :])).astype(BF)
    for j in range(3):
        px[:, j * 256:(j + 1) * 256] = mm(pack_weights(j, 96), stacked(dx_v[...], j)).astype(BF)
    each(1, 16, lambda d: r_copy(d).start())
    rr[own16, :] = px[own16, :]
    d_gate = jnp.broadcast_to(jnp.sum(acc, axis=1, keepdims=True), (96, 128)).astype(BF)
    row = iota((256, 96), 0)
    pack6 = ((iota((256, 96), 1) == (row // 16) * 6 + row % 16) & (row % 16 < 6)).astype(BF)
    dgs[...] = mm(pack6, d_gate).astype(BF)
    each(1, 16, lambda d: t_copy(d).start())
    dgr[own16, :] = dgs[own16, :]

    w_facing.wait_recv()
    w_relay.start()

    each(1, 8, lambda o: c_recv(o))
    total = counts[0]
    for src in range(1, 8):
        total = total + counts[src]

    def doc_start(place):
        start_at = jnp.zeros_like(place)
        for d in range(1, 4):
            first_of = jnp.concatenate([total[d:d + 1]] * (place.shape[1] // 128), axis=1)
            start_at = jnp.maximum(start_at, jnp.where(first_of <= place, first_of, 0))
        return start_at

    for i in (4, 5, 6):
        loads[i].wait()

    def half(i):
        return slice(i * 512, (i + 1) * 512)

    starts = [doc_start(c * 1024 + t * 512 + iota((1, 512), 1)) for t in range(2)]

    def seen(t, d, h):
        key = (c - d) * 1024 + h * 512 + iota((512, 512), 0)
        allowed = key >= starts[t]
        if isinstance(d, int) and d == 0:
            allowed = allowed & (key <= c * 1024 + t * 512 + iota((512, 512), 1))
        return allowed

    def key_halves(t, d):
        if isinstance(d, int):
            return range(t + 1) if d == 0 else range(t, 2)
        return range(2)

    def kept_probs(d, first, n, cols):
        if isinstance(d, int) and d == 0:
            return wd_v.at[first:first + n, cols]
        return wgu_v.at[(d - 1) // 2, pl.ds(pl.multiple_of((d - 1) % 2 * 1024 + first, 512), n), cols]

    top_v[...] = jnp.full((8, 1024), NEG, F32)
    sum_v[...] = jnp.zeros((8, 1024), F32)
    o_v[...] = jnp.zeros((128, 1024), F32)

    def statistics(d):
        for t in range(2):
            cols = half(t)
            halves = key_halves(t, d)
            q = q_win[0, cols, :]
            scores = [jnp.where(seen(t, d, h), nt(k_win[d, half(h), :], q) * SCALE2, NEG) for h in halves]
            most = functools.reduce(jnp.maximum, [over_rows(s, jnp.maximum) for s in scores])
            old = top_v[:, cols]
            new = jnp.maximum(old, jnp.max(most, axis=0, keepdims=True))
            fade = jnp.exp2(old - new)
            probs = [jnp.exp2(s - new[0:1]) for s in scores]
            top_v[:, cols] = new
            tops_v[d, :, cols] = new
            for h, p in zip(halves, probs):
                kept_probs(d, h * 512, 512, cols)[...] = p.astype(BF)
            sum_v[:, cols] = sum_v[:, cols] * fade + sum(over_rows(p, jnp.add) for p in probs)
            o_v[:, cols] = o_v[:, cols] * fade[0:1] + sum(
                mm(jnp.transpose(v_win[d, half(h), :]), p.astype(BF)) for h, p in zip(halves, probs))

    def statistics_step(d, _):
        received(kv_copy(d, (c, e)))
        statistics(d)
        return 0

    last_before = jnp.minimum(c, 3)
    direct = jnp.minimum(y, 1)
    statistics(0)

    @pl.when(xl == 1)
    def _():
        statistics(4)
    lax.fori_loop(1, direct + 1, statistics_step, 0)

    recv(rr, r_rs)
    sums = [mm(selw[j], rr[:, j * 256:(j + 1) * 256]) for j in range(3)]
    parts = [sums[c_ % 3][(c_ // 3) * 64:(c_ // 3) * 64 + 64] for c_ in range(6)]
    parts.append(sums[0][128:192] + sums[1][128:192])
    parts.append(sums[1][192:256] + sums[2][128:192])
    for col in range(8):
        cols = slice(col * 256, (col + 1) * 256)
        low = (grad[:, cols].astype(F32) + parts[col]).astype(BF)
        ag[z, :, cols] = low
        d_hidden[:, cols] = low

    above, under = (c, exp_at(xh, (z + 1) % 4, k)), (c, exp_at(xh, (z + 3) % 4, k))
    z_up, z_down = (z + 1) % 4, (z + 3) % 4
    first, second = pl.ds(0, 32), pl.ds(32, 32)
    g_up = remote(ag.at[z], ag.at[z], ag_ss.at[0], ag_rs.at[0], above)
    g_down = remote(ag.at[z], ag.at[z], ag_ss.at[1], ag_rs.at[1], under)
    g_up2 = remote(ag.at[z_down, first], ag.at[z_down, first], ag_ss.at[2], ag_rs.at[2], above)
    g_down2 = remote(ag.at[z_up, second], ag.at[z_up, second], ag_ss.at[3], ag_rs.at[3], under)
    g_up.start()
    g_down.start()

    loads[3].wait()
    w_mate.wait_recv()
    w_relay.wait_recv()
    sets = ((0, 1), (1, 2), (3, 1))
    order = (z, z_up, z_down, (z + 2) % 4)
    pieces = [
        (own_q, e, (xh, k)),
        (mate_q, exp_at(xh, z, 1 - k), (xh, 1 - k)),
        (far_q, exp_at(1 - xh, z, k), (1 - xh, k)),
        (far_mate_q, exp_at(1 - xh, z, 1 - k), (1 - xh, 1 - k)),
    ]

    def piece_copy(g, i):
        q_, head, _ = pieces[i]
        part = pl.ds(*sets[g])
        return remote(d4.at[q_, part], do_win.at[0, xh, part, k], ex_ss.at[g, i], ex_rs.at[g, i], (c, head))

    def piece_across(g, i):
        q_, head, _ = pieces[i]
        part = pl.ds(*sets[g])
        return remote(d4.at[q_, part], do_win.at[4, xh, part, k], xs_ss.at[g, i], do_rs.at[g, 4, i], (across, head))

    def piece_along(g, i, slot, yo, src):
        _, _, (xs, ks) = pieces[i]
        part = pl.ds(*sets[g])
        return remote(do_win.at[src, xs, part, ks], do_win.at[slot, xs, part, ks], do_ss.at[g, slot, i],
                      do_rs.at[g, slot, i], (xl * 4 + yo, e))

    def along(g, i, act):
        for o in (1, 3, 2):
            yo = (y + o) % 4

            @pl.when(yo < y)
            def _():
                act(piece_along(g, i, y - yo, yo, 0))

    def along_relay(g, i, act):
        for o in (1, 3, 2):
            yo = (y + o) % 4

            @pl.when((xl == 0) & (yo > y))
            def _():
                act(piece_along(g, i, 4 + y - yo, yo, 4))

    def begin(copy):
        copy.start()

    def project(g):
        first_of, n = sets[g]
        tokens = jnp.concatenate([ag[order[first_of + i]] for i in range(n)], axis=0)
        flat = nt(tokens, w4[...].reshape(512, ag.shape[2])).astype(BF)
        part = slice(first_of, first_of + n)
        for q_ in range(4):
            d4[q_, part] = flat[:, q_ * 128:(q_ + 1) * 128].reshape(n, 64, 128)
        for i in (2, 3, 1):
            piece_copy(g, i).start()

        @pl.when(xl == 1)
        def _():
            for i in (2, 3, 1, 0):
                piece_across(g, i).start()
        do_win[0, xh, part, k] = d4[own_q, part]
        along(g, 0, begin)

    def pass_on(g):
        for i in (1, 2, 3):
            piece_copy(g, i).wait_recv()
            along(g, i, begin)

    def pass_across(g):
        for i in range(4):
            @pl.when(xl == 0)
            def _():
                piece_across(g, i).wait_recv()
            along_relay(g, i, begin)

    def gradient_rows(d):
        halves = []
        for xs in range(2):
            for z_ in range(4):
                away = (z_ + 4 - z) % 4
                halves.append(do_win[d, xs, away + away // 2 - 2 * (away // 3)].reshape(128, 128))
        return jnp.concatenate(halves, axis=0)

    def row_copy(win, ss, rs, d):
        return remote(win.at[0], win.at[d], ss.at[d], rs.at[d], ((c + 8 - d) % 8, e))

    def before(act):
        for d in range(1, 5):
            @pl.when(c >= d)
            def _():
                act(d)

    def later(act):
        for d in range(1, 5):
            @pl.when(c + d <= 7)
            def _():
                act(d)

    project(0)
    middle = jnp.minimum(direct + 3, last_before + 1)
    lax.fori_loop(direct + 1, middle, statistics_step, 0)
    pass_on(0)
    g_up.wait_recv()
    g_up2.start()
    g_down.wait_recv()
    g_down2.start()
    project(1)
    pass_across(0)
    lax.fori_loop(middle, last_before + 1, statistics_step, 0)
    norm = jnp.sum(sum_v[...], axis=0, keepdims=True)
    lse_win[0] = top_v[...] + jnp.log(norm) * math.log2(math.e)
    before(lambda d: row_copy(lse_win, lse_ss, lse_rs, d).start())

    def key_probs(t, d, halves, masked):
        key = c * 1024 + t * 512 + iota((512, 512), 0)
        for h in halves:
            cols = half(h)
            place = (c + d) * 1024 + h * 512 + iota((1, 512), 1)
            allowed = key >= doc_start(place)
            if masked:
                allowed = allowed & (key <= place)
            s = nt(k_win[0, half(t), :], q_win[d, cols, :]) * SCALE2
            p = jnp.where(allowed, jnp.exp2(s - lse_win[d, 0:1, cols]), 0.0)
            pt_v[t, d, :, cols] = p.astype(BF)

    def query_tiles(d, act):
        if d == 0:
            act(0, 0, range(2))
            act(1, 0, range(1, 2))
        elif d == 4:
            act(0, 4, range(1))
            act(1, 4, range(2))
        else:
            act(0, d, range(2))
            act(1, d, range(2))

    def probs_step(d, _):
        received(q_copy(d, (c, e)))
        row_copy(lse_win, lse_ss, lse_rs, d).wait_recv()
        query_tiles(1, lambda t, _, halves: key_probs(t, d, halves, False))
        return 0

    last_after = jnp.minimum(7 - c, 3)
    query_tiles(0, lambda t, d, halves: key_probs(t, d, halves, True))
    pass_on(1)
    g_up2.wait_recv()
    g_down2.wait_recv()
    project(2)
    pass_across(1)
    lax.fori_loop(1, jnp.minimum(last_after, 1) + 1, probs_step, 0)
    pass_on(2)
    pass_across(2)

    d_own = gradient_rows(0)
    prod = d_own.astype(F32) * jnp.transpose(o_v[...] / norm)
    high = prod.astype(BF)
    low_part = (prod - high.astype(F32)).astype(BF)
    ones = jnp.ones((8, 128), BF)
    delta_win[0] = nt(ones, high) + nt(ones, low_part)
    before(lambda d: row_copy(delta_win, dl_ss, dl_rs, d).start())
    lax.fori_loop(2, last_after + 1, probs_step, 0)

    @pl.when(xl == 0)
    def _():
        row_copy(lse_win, lse_ss, lse_rs, 4).wait_recv()
        query_tiles(4, lambda t, d, halves: key_probs(t, d, halves, False))

    dq_v[...] = jnp.zeros((128, 1024), F32)

    def query_grads(d):
        for t in range(2):
            cols = half(t)
            do = d_own[cols, :]
            acc = dq_v[:, cols]
            fade = jnp.exp2(tops_v[d, 0:1, cols] - lse_win[0, 0:1, cols])
            faded_delta = delta_win[0, 0:1, cols] * fade
            halves = key_halves(t, d)
            rows = slice(halves[0] * 512, halves[-1] * 512 + 512)
            dp = nt(v_win[d, rows, :], do)
            kept = kept_probs(d, rows.start, rows.stop - rows.start, cols)[...]
            ds = kept.astype(F32) * (dp * fade - faded_delta)
            acc = acc + mm(jnp.transpose(k_win[d, rows, :]), ds.astype(BF))
            dq_v[:, cols] = acc

    def query_step(d, _):
        query_grads(d)
        return 0

    query_grads(0)
    lax.fori_loop(1, last_before + 1, query_step, 0)

    @pl.when(xl == 1)
    def _():
        query_grads(4)
    dq_out[...] = (jnp.transpose(dq_v[...]) * SCALE).astype(BF)

    dk_v[...] = jnp.zeros((1024, 128), F32)
    dv_v[...] = jnp.zeros((1024, 128), F32)

    def key_grads(t, d, halves):
        rows = half(t)
        do_all = gradient_rows(d)
        cols = slice(halves[0] * 512, halves[-1] * 512 + 512)
        do = do_all[cols, :]
        p = pt_v[t, d, :, cols]
        dv_v[rows, :] += mm(p, do)
        ds = p.astype(F32) * (nt(v_win[0, rows, :], do) - delta_win[d, 0:1, cols])
        dk_v[rows, :] += mm(ds.astype(BF), q_win[d, cols, :])

    query_tiles(0, key_grads)

    def grads_step(n, _):
        d = 1 + 2 * n - 3 * (n // 2)

        @pl.when(d <= last_after)
        def _():
            for g in range(3):
                for i in range(4):
                    piece_along(g, i, d, y, 0).wait_recv()
            row_copy(delta_win, dl_ss, dl_rs, d).wait_recv()
            query_tiles(1, lambda t, _, halves: key_grads(t, d, halves))
        return 0

    @pl.when(xl == 0)
    def _():
        row_copy(delta_win, dl_ss, dl_rs, 4).wait_recv()
        query_tiles(4, key_grads)

    lax.fori_loop(0, 3, grads_step, 0)

    dk_out[...] = (dk_v[...] * SCALE).astype(BF)
    dv_out[...] = dv_v[...].astype(BF)

    recv(dgr, t_rs)
    row, lane = iota((256, 128), 0), iota((256, 128), 1)
    diag = jnp.where(row % 16 == lane, dgr[...].astype(F32), 0.0).astype(BF)
    gather = (iota((16, 256), 1) // 16 == iota((16, 256), 0)).astype(BF)
    d_gates[0] = jnp.transpose(mm(gather, diag))[0:6].astype(BF)

    each(1, 16, lambda d: x_copy(d).wait_send())
    each(1, 16, lambda d: g_copy(d).wait_send())
    each(1, 16, lambda d: r_copy(d).wait_send())
    each(1, 16, lambda d: t_copy(d).wait_send())
    each(1, 8, lambda o: c_copy(o).wait_send())
    for copy in [w_mate, w_facing, w_relay, g_up, g_down, g_up2, g_down2]:
        copy.wait_send()
    to_half(sent)
    to_row(sent)
    relay_row(sent, 0)
    relay_row(sent, 1)
    before(lambda d: row_copy(lse_win, lse_ss, lse_rs, d).wait_send())
    before(lambda d: row_copy(delta_win, dl_ss, dl_rs, d).wait_send())
    for g in range(3):
        for i in range(1, 4):
            piece_copy(g, i).wait_send()

        @pl.when(xl == 1)
        def _():
            for i in range(4):
                piece_across(g, i).wait_send()
        for i in range(4):
            along(g, i, lambda copy: copy.wait_send())
            along_relay(g, i, lambda copy: copy.wait_send())


def hand_over(*refs):
    n = len(refs) // 3
    held, sems = refs[2 * n:3 * n], refs[-1]
    reads = [pltpu.make_async_copy(refs[i], held[i], sems.at[i]) for i in range(n)]
    writes = [pltpu.make_async_copy(held[i], refs[n + i], sems.at[n + i]) for i in range(n)]
    for read in reads:
        read.start()
    for read, write in zip(reads, writes):
        read.wait()
        write.start()
    for write in writes:
        write.wait()


def per_device(q_heads, k_heads, v_heads, doc_ids, w_out, hidden_rows, out_grad, picks, gates, w_gate, w_up, w_down):
    vm, hbm = pl.BlockSpec(memory_space=pltpu.VMEM), pl.BlockSpec(memory_space=pl.ANY)
    tok, width = q_heads.shape
    rows, model = hidden_rows.shape
    ff = w_gate.shape[2]
    dma = pltpu.SemaphoreType.DMA

    def low(*shape):
        return pltpu.VMEM(shape, BF)

    def full(*shape):
        return pltpu.VMEM(shape, F32)

    def out(*shape):
        return jax.ShapeDtypeStruct(shape, BF)

    shapes = (out(rows, model), out(1, 6, 16), out(tok, width), out(tok, width), out(tok, width))
    results = pl.pallas_call(
        kernel,
        out_shape=shapes,
        in_specs=[vm] * 5 + [hbm] * 7,
        out_specs=[vm] * 5,
        scratch_shapes=[
            low(2, model, ff), low(ff, model), low(4, 128, model),
            low(256, 768), low(256, 768), low(256, 768), low(256, 768),
            low(96, model), low(96, model), full(96, ff), full(96, ff),
            low(96, ff), low(96, ff), low(96, model),
            low(256, 768), low(256, 768), low(256, 128), low(256, 128),
            low(3, 256, 256), low(4, rows, model), low(4, 4, rows, width),
            pltpu.VMEM((8, 128), jnp.int32), pltpu.VMEM((8, 8, 128), jnp.int32),
            low(5, tok, width), low(5, tok, width), low(5, tok, width), low(5, 2, 4, 2, rows, width),
            full(5, 8, tok), full(5, 8, tok), full(8, tok), full(8, tok), full(128, tok),
            low(2, 5, 512, tok), full(5, 8, tok), full(128, tok), full(tok, 128), full(tok, 128),
            dma((8,)), dma((16,)), dma((16,)), dma((16,)), dma((16,)), dma((16,)), dma((16,)), dma((16,)), dma((16,)),
            dma((8,)), dma((8,)), dma((3,)), dma((3,)), dma((4,)), dma((4,)), dma((3, 4)), dma((3, 4)), dma((3, 4)),
            dma((5, 2)), dma((5, 2)), dma((5,)), dma((5,)), dma((3, 5, 4)), dma((3, 5, 4)),
            dma((5,)), dma((5,)), dma((5,)), dma((5,)),
        ],
        compiler_params=pltpu.CompilerParams(
            collective_id=0, has_side_effects=True, vmem_limit_bytes=60 * 2**20),
        name="backward",
    )(hidden_rows, out_grad, jnp.transpose(picks, (2, 0, 1)), jnp.transpose(gates, (0, 2, 1)), doc_ids.reshape(8, 128),
      w_gate[0], w_up[0], w_down[0], w_out, q_heads, k_heads, v_heads)
    d_hidden, d_gates, d_queries, d_keys, d_values = pl.pallas_call(
        hand_over,
        out_shape=shapes,
        in_specs=[hbm] * 5,
        out_specs=[hbm] * 5,
        scratch_shapes=[pltpu.VMEM(shape.shape, BF) for shape in shapes] + [dma((10,))],
        compiler_params=pltpu.CompilerParams(vmem_limit_bytes=60 * 2**20),
        name="results",
    )(*results)
    return (d_queries, d_keys, d_values, d_hidden, jnp.transpose(d_gates, (0, 2, 1)))


def solution(mesh):
    return jax.shard_map(
        per_device,
        mesh=mesh,
        in_specs=(
            P("ctx", "exp"),
            P("ctx", "exp"),
            P("ctx", "exp"),
            P("ctx"),
            P("exp", None),
            P(("ctx", "exp"), None),
            P(("ctx", "exp"), None),
            P(("ctx", "exp"), None, None),
            P(("ctx", "exp"), None, None),
            P("exp", None, None),
            P("exp", None, None),
            P("exp", None, None),
        ),
        out_specs=(
            P("ctx", "exp"),
            P("ctx", "exp"),
            P("ctx", "exp"),
            P(("ctx", "exp"), None),
            P(("ctx", "exp"), None, None),
        ),
        check_vma=False,
    )
```

```python
import functools
import math

import jax
import jax.numpy as jnp
from jax import lax
from jax.experimental import pallas as pl
from jax.experimental.pallas import tpu as pltpu
from jax.sharding import PartitionSpec as P

NEG = -1e30
SCALE = 1.0 / math.sqrt(128)
SCALE2 = SCALE * math.log2(math.e)


def nt(a, b):
    return lax.dot_general(a, b, (((1,), (1,)), ((), ())), preferred_element_type=jnp.float32)


def fold(x, op):
    parts = [x[:, i * 128:(i + 1) * 128] for i in range(x.shape[1] // 128)]
    while len(parts) > 1:
        parts = [op(parts[i], parts[i + 1]) for i in range(0, len(parts), 2)]
    return parts[0]


BF = jnp.bfloat16
F32 = jnp.float32
MESH = pl.DeviceIdType.MESH
FC = 256


def iota(shape, dim):
    return lax.broadcasted_iota(jnp.int32, shape, dim)


def mm(a, b):
    return jnp.dot(a, b, preferred_element_type=F32)


def place_in_message(r, j):
    tail = (r - 12, jnp.where(r < 14, r - 8, r - 14), r - 10)[j]
    slot = jnp.where(r < 6, r, jnp.where(r < 12, r - 6, tail))
    block = jnp.where(r < 6, 0, jnp.where(r < 12, 1, 2))
    if j == 1:
        block = jnp.where(r >= 14, 3, block)
    return slot, block


BLOCKS = ((0, 3, 6), (1, 4, 6, 7), (2, 5, 7))


def stacked(array, j, width=256):
    return jnp.concatenate([array[:, c * width:(c + 1) * width] for c in BLOCKS[j]], axis=0)


def pack_weights(j, rows_in_block):
    wide = len(BLOCKS[j]) * rows_in_block
    row = iota((256, wide), 0)
    slot, block = place_in_message(row % 16, j)
    return (iota((256, wide), 1) == block * rows_in_block + (row // 16) * 6 + slot).astype(BF)


def unpack(buf, c):
    lane, i = iota((96, 256), 1), iota((96, 256), 0)
    r, src = lane % 16, lane // 16
    out = None
    for j in range(3):
        if c not in BLOCKS[j]:
            continue
        slot, block = place_in_message(r, j)
        pick = ((i == src * 6 + slot) & (block == BLOCKS[j].index(c))).astype(BF)
        part = mm(pick, buf[:, j * 256:(j + 1) * 256])
        out = part if out is None else out + part
    return out.astype(BF)


def remote(src, dst, ss, rs, device):
    return pltpu.make_async_remote_copy(
        src_ref=src, dst_ref=dst, send_sem=ss, recv_sem=rs, device_id=device, device_id_type=MESH)


def over_rows(x, op):
    parts = [x[i * 8:(i + 1) * 8] for i in range(x.shape[0] // 8)]
    while len(parts) > 1:
        parts = [op(parts[i], parts[i + 1]) for i in range(0, len(parts), 2)]
    return parts[0]


def rows16(ref, i):
    return ref.at[pl.ds(pl.multiple_of(i * 16, 16), 16), :]


def kernel(hidden, grad, picks, gates, docs, wg, wu, wd, wo, qh, kh, vh,
           d_hidden, d_gates, dq_out, dk_out, dv_out,
           wgu_v, wd_v, w4, sx, sg, rx, rg, x_v, g_v, a_v, b_v, da_v, db_v, dx_v,
           px, rr, dgs, dgr, selw, ag, d4, cnt, counts,
           q_win, k_win, v_win, do_win, lse_win, delta_win, top_v, sum_v, o_v,
           pt_v, tops_v, dq_v, dk_v, dv_v,
           local_sem, x_ss, x_rs, g_ss, g_rs, r_ss, r_rs, t_ss, t_rs, c_ss, c_rs,
           w_ss, w_rs, ag_ss, ag_rs, ex_ss, ex_rs, xs_ss, kv_ss, kv_rs, q_ss, q_rs, do_ss, do_rs,
           lse_ss, lse_rs, dl_ss, dl_rs):
    c = lax.axis_index("ctx")
    e = lax.axis_index("exp")
    xl, y = c // 4, c % 4
    xh, z, k = e // 8, (e // 2) % 4, e % 2
    across = (c + 4) % 8

    def exp_at(xh_, z_, k_):
        return (xh_ * 4 + z_) * 2 + k_

    def peer(d):
        p = (e + d) % 16
        return p, ((c + 4 * ((p // 8 + xh) % 2)) % 8, p)

    wg_v, wu_v = wgu_v.at[0], wgu_v.at[1]

    loads = [
        pltpu.make_async_copy(wg, wg_v, local_sem.at[0]),
        pltpu.make_async_copy(wu, wu_v, local_sem.at[1]),
        pltpu.make_async_copy(wd, wd_v, local_sem.at[2]),
        pltpu.make_async_copy(wo, w4.at[xh * 2 + k], local_sem.at[3]),
        pltpu.make_async_copy(qh, q_win.at[0], local_sem.at[4]),
        pltpu.make_async_copy(kh, k_win.at[0], local_sem.at[5]),
        pltpu.make_async_copy(vh, v_win.at[0], local_sem.at[6]),
    ]
    for load in loads:
        load.start()

    barrier = pltpu.get_barrier_semaphore()

    def greet(d, _):
        pl.semaphore_signal(barrier, inc=1, device_id=peer(d)[1], device_id_type=MESH)
        return 0

    lax.fori_loop(1, 16, greet, 0)
    for k_ in range(2):
        pl.semaphore_signal(barrier, inc=1, device_id=(c, exp_at(1 - xh, z, k_)), device_id_type=MESH)

    pl.semaphore_signal(barrier, inc=1, device_id=(across, exp_at(xh, z, 1 - k)), device_id_type=MESH)

    def greet_ctx(o, _):
        pl.semaphore_signal(barrier, inc=1, device_id=((c + o) % 8, e), device_id_type=MESH)
        return 0

    lax.fori_loop(1, 8, greet_ctx, 0)

    row = iota((256, 16), 0)
    spread = (row // 16 == iota((256, 16), 1)).astype(BF)
    pick_rows = nt(spread, jnp.concatenate([picks[i] for i in range(6)], axis=0).astype(F32).astype(BF))
    gate_rows = nt(spread, gates[0])
    r = iota((256, 6), 0) % 16
    lane6 = iota((256, 6), 1)
    hid, gra = hidden[...], grad[...]
    sels = []
    for j in range(3):
        slot, block = place_in_message(r, j)
        mine = lane6 == slot
        pick = jnp.sum(jnp.where(mine, pick_rows, 0.0), axis=1, keepdims=True)
        gate = jnp.sum(jnp.where(mine, gate_rows, 0.0), axis=1, keepdims=True)
        wide = 64 * len(BLOCKS[j])
        target = block[:, 0:1].astype(F32) * 64.0 + pick
        hit = iota((256, wide), 1).astype(F32) == target
        sel = hit.astype(BF)
        sels.append((sel, target, gate, hit))
        sx[:, j * 256:(j + 1) * 256] = mm(sel, stacked(hid, j)).astype(BF)
    pl.semaphore_wait(barrier, 15 + 3 + 7)

    def x_copy(d):
        p, device = peer(d)
        return remote(rows16(sx, p), rows16(rx, e), x_ss.at[p], x_rs.at[e], device)

    def g_copy(d):
        p, device = peer(d)
        return remote(rows16(sg, p), rows16(rg, e), g_ss.at[p], g_rs.at[e], device)

    def r_copy(d):
        p, device = peer(d)
        return remote(rows16(px, p), rows16(rr, e), r_ss.at[p], r_rs.at[e], device)

    def t_copy(d):
        p, device = peer(d)
        return remote(rows16(dgs, p), rows16(dgr, e), t_ss.at[p], t_rs.at[e], device)

    def c_copy(o):
        return remote(cnt, counts.at[c], c_ss.at[o], c_rs.at[c], ((c + o) % 8, e))

    def c_recv(o):
        src = (c + o) % 8
        remote(cnt, counts.at[src], c_ss.at[o], c_rs.at[src], (src, e)).wait_recv()

    def recv(buf, rs):
        def one(d, _):
            p, device = peer(d)
            remote(rows16(buf, p), rows16(buf, p), rs.at[p], rs.at[p], device).wait_recv()
            return 0
        lax.fori_loop(1, 16, one, 0)

    def each(n0, n1, act):
        def one(d, _):
            act(d)
            return 0
        lax.fori_loop(n0, n1, one, 0)

    def kv_copy(slot, device, relay=False, which=(0, 1)):
        pairs = ((kh, k_win), (vh, v_win))
        return [remote(pairs[i][1].at[4] if relay else pairs[i][0], pairs[i][1].at[slot], kv_ss.at[slot, i],
                       kv_rs.at[slot, i], device) for i in which]

    def q_copy(slot, device, relay=False):
        return [remote(q_win.at[4] if relay else qh, q_win.at[slot], q_ss.at[slot], q_rs.at[slot], device)]

    def to_half(act):
        @pl.when(xl == 0)
        def _():
            act(kv_copy(4, (across, e)))

        @pl.when(xl == 1)
        def _():
            act(q_copy(4, (across, e)))

    def to_row(act):
        for o in range(1, 4):
            yo = (y + o) % 4

            @pl.when(yo > y)
            def _():
                act(kv_copy(yo - y, (xl * 4 + yo, e)))

            @pl.when(yo < y)
            def _():
                act(q_copy(y - yo, (xl * 4 + yo, e)))

    def relay_row(act, which):
        for o in range(1, 4):
            yo = (y + o) % 4

            @pl.when((xl == 1) & (yo < y))
            def _():
                act(kv_copy(4 + yo - y, (xl * 4 + yo, e), True, (which,)))

            if which == 0:
                @pl.when((xl == 0) & (yo > y))
                def _():
                    act(q_copy(4 + y - yo, (xl * 4 + yo, e), True))

    def start(copies):
        for copy in copies:
            copy.start()

    def sent(copies):
        for copy in copies:
            copy.wait_send()

    def received(copies):
        for copy in copies:
            copy.wait_recv()

    each(1, 16, lambda d: x_copy(d).start())
    to_half(start)
    for j in range(3):
        sg[:, j * 256:(j + 1) * 256] = mm(sels[j][0], stacked(gra, j)).astype(BF)
    each(1, 16, lambda d: g_copy(d).start())
    to_row(start)
    own16 = pl.ds(pl.multiple_of(e * 16, 16), 16)
    rx[own16, :] = sx[own16, :]
    rg[own16, :] = sg[own16, :]

    mate = (c, exp_at(xh, z, 1 - k))
    facing = (across, exp_at(1 - xh, z, k))
    own_q, mate_q = xh * 2 + k, xh * 2 + 1 - k
    far_q, far_mate_q = (1 - xh) * 2 + k, (1 - xh) * 2 + 1 - k
    w_mate = remote(wo, w4.at[own_q], w_ss.at[0], w_rs.at[0], mate)
    w_facing = remote(wo, w4.at[own_q], w_ss.at[1], w_rs.at[1], facing)
    w_relay = remote(w4.at[far_q], w4.at[far_q], w_ss.at[2], w_rs.at[2], mate)
    w_mate.start()

    sizes = []
    for d in range(8):
        under_d = jnp.sum((docs[...] < d).astype(F32), axis=1, keepdims=True)
        sizes.append(jnp.broadcast_to(jnp.sum(under_d, axis=0, keepdims=True), (1, 128)))
    below = jnp.concatenate(sizes, axis=0).astype(jnp.int32)
    cnt[...] = below
    counts[c] = below
    each(1, 8, lambda o: c_copy(o).start())
    for j in range(3):
        _, target, gate, hit = sels[j]
        if hit.shape[1] < 256:
            hit = iota((256, 256), 1).astype(F32) == target
        selw[j] = jnp.transpose(jnp.where(hit, gate, 0.0)).astype(BF)

    @pl.when(xl == 1)
    def _():
        received(kv_copy(4, (across, e), which=(0,)))

    @pl.when(xl == 0)
    def _():
        received(q_copy(4, (across, e)))
    relay_row(start, 0)

    recv(rx, x_rs)
    for col in range(8):
        x_v[:, col * 256:(col + 1) * 256] = unpack(rx[...], col)
    loads[0].wait()
    loads[1].wait()

    def up(f0, n):
        cols = pl.ds(f0, n)
        a_v[:, cols] = mm(x_v[...], wg_v[:, cols])
        b_v[:, cols] = mm(x_v[...], wu_v[:, cols])

    ff = wg.shape[1]
    chunks = [(f0, min(FC, ff - f0)) for f0 in range(0, ff, FC)]
    for f0, n in chunks:
        up(f0, n)

    @pl.when(xl == 1)
    def _():
        received(kv_copy(4, (across, e), which=(1,)))
    relay_row(start, 1)
    recv(rg, g_rs)
    w_facing.start()
    for col in range(8):
        g_v[:, col * 256:(col + 1) * 256] = unpack(rg[...], col)
    loads[2].wait()

    def down(f0, n, acc):
        cols = pl.ds(f0, n)
        u = nt(g_v[...], wd_v[cols, :])
        a, b = a_v[:, cols], b_v[:, cols]
        sig = 1.0 / (1.0 + jnp.exp(-a))
        act = a * sig
        da_v[:, cols] = (u * b * sig * (1.0 + a * (1.0 - sig))).astype(BF)
        db_v[:, cols] = (u * act).astype(BF)
        return acc + fold(act * b * u, jnp.add)

    acc = jnp.zeros((96, 128), F32)
    for f0, n in chunks:
        acc = down(f0, n, acc)

    for d0 in range(0, wg.shape[0], FC):
        cols = pl.ds(d0, FC)
        dx_v[:, cols] = (nt(da_v[...], wg_v[cols, :]) + nt(db_v[...], wu_v[cols, :])).astype(BF)
    for j in range(3):
        px[:, j * 256:(j + 1) * 256] = mm(pack_weights(j, 96), stacked(dx_v[...], j)).astype(BF)
    each(1, 16, lambda d: r_copy(d).start())
    rr[own16, :] = px[own16, :]
    d_gate = jnp.broadcast_to(jnp.sum(acc, axis=1, keepdims=True), (96, 128)).astype(BF)
    row = iota((256, 96), 0)
    pack6 = ((iota((256, 96), 1) == (row // 16) * 6 + row % 16) & (row % 16 < 6)).astype(BF)
    dgs[...] = mm(pack6, d_gate).astype(BF)
    each(1, 16, lambda d: t_copy(d).start())
    dgr[own16, :] = dgs[own16, :]

    w_facing.wait_recv()
    w_relay.start()

    each(1, 8, lambda o: c_recv(o))
    total = counts[0]
    for src in range(1, 8):
        total = total + counts[src]

    def doc_start(place):
        start_at = jnp.zeros_like(place)
        for d in range(1, 4):
            first_of = jnp.concatenate([total[d:d + 1]] * (place.shape[1] // 128), axis=1)
            start_at = jnp.maximum(start_at, jnp.where(first_of <= place, first_of, 0))
        return start_at

    for i in (4, 5, 6):
        loads[i].wait()

    def half(i):
        return slice(i * 512, (i + 1) * 512)

    starts = [doc_start(c * 1024 + t * 512 + iota((1, 512), 1)) for t in range(2)]

    def seen(t, d, h):
        key = (c - d) * 1024 + h * 512 + iota((512, 512), 0)
        allowed = key >= starts[t]
        if isinstance(d, int) and d == 0:
            allowed = allowed & (key <= c * 1024 + t * 512 + iota((512, 512), 1))
        return allowed

    def key_halves(t, d):
        if isinstance(d, int):
            return range(t + 1) if d == 0 else range(t, 2)
        return range(2)

    def kept_probs(d, first, n, cols):
        if isinstance(d, int) and d == 0:
            return wd_v.at[first:first + n, cols]
        return wgu_v.at[(d - 1) // 2, pl.ds(pl.multiple_of((d - 1) % 2 * 1024 + first, 512), n), cols]

    top_v[...] = jnp.full((8, 1024), NEG, F32)
    sum_v[...] = jnp.zeros((8, 1024), F32)
    o_v[...] = jnp.zeros((128, 1024), F32)

    def statistics(d):
        flipped = [jnp.transpose(v_win[d, half(h), :]) for h in range(2)]
        for t in range(2):
            cols = half(t)
            halves = key_halves(t, d)
            q = q_win[0, cols, :]
            scores = [jnp.where(seen(t, d, h), nt(k_win[d, half(h), :], q) * SCALE2, NEG) for h in halves]
            most = functools.reduce(jnp.maximum, [over_rows(s, jnp.maximum) for s in scores])
            old = top_v[:, cols]
            new = jnp.maximum(old, jnp.max(most, axis=0, keepdims=True))
            fade = jnp.exp2(old - new)
            probs = [jnp.exp2(s - new[0:1]) for s in scores]
            top_v[:, cols] = new
            tops_v[d, :, cols] = new
            for h, p in zip(halves, probs):
                kept_probs(d, h * 512, 512, cols)[...] = p.astype(BF)
            sum_v[:, cols] = sum_v[:, cols] * fade + sum(over_rows(p, jnp.add) for p in probs)
            o_v[:, cols] = o_v[:, cols] * fade[0:1] + sum(
                mm(flipped[h], p.astype(BF)) for h, p in zip(halves, probs))

    def statistics_step(d, _):
        received(kv_copy(d, (c, e)))
        statistics(d)
        return 0

    last_before = jnp.minimum(c, 3)
    direct = jnp.minimum(y, 1)
    statistics(0)

    @pl.when(xl == 1)
    def _():
        statistics(4)
    lax.fori_loop(1, direct + 1, statistics_step, 0)

    recv(rr, r_rs)
    sums = [mm(selw[j], rr[:, j * 256:(j + 1) * 256]) for j in range(3)]
    parts = [sums[c_ % 3][(c_ // 3) * 64:(c_ // 3) * 64 + 64] for c_ in range(6)]
    parts.append(sums[0][128:192] + sums[1][128:192])
    parts.append(sums[1][192:256] + sums[2][128:192])
    for col in range(8):
        cols = slice(col * 256, (col + 1) * 256)
        low = (grad[:, cols].astype(F32) + parts[col]).astype(BF)
        ag[z, :, cols] = low
        d_hidden[:, cols] = low

    above, under = (c, exp_at(xh, (z + 1) % 4, k)), (c, exp_at(xh, (z + 3) % 4, k))
    z_up, z_down = (z + 1) % 4, (z + 3) % 4
    first, second = pl.ds(0, 32), pl.ds(32, 32)
    g_up = remote(ag.at[z], ag.at[z], ag_ss.at[0], ag_rs.at[0], above)
    g_down = remote(ag.at[z], ag.at[z], ag_ss.at[1], ag_rs.at[1], under)
    g_up2 = remote(ag.at[z_down, first], ag.at[z_down, first], ag_ss.at[2], ag_rs.at[2], above)
    g_down2 = remote(ag.at[z_up, second], ag.at[z_up, second], ag_ss.at[3], ag_rs.at[3], under)
    g_up.start()
    g_down.start()

    loads[3].wait()
    w_mate.wait_recv()
    w_relay.wait_recv()
    sets = ((0, 1), (1, 2), (3, 1))
    order = (z, z_up, z_down, (z + 2) % 4)
    pieces = [
        (own_q, e, (xh, k)),
        (mate_q, exp_at(xh, z, 1 - k), (xh, 1 - k)),
        (far_q, exp_at(1 - xh, z, k), (1 - xh, k)),
        (far_mate_q, exp_at(1 - xh, z, 1 - k), (1 - xh, 1 - k)),
    ]

    def piece_copy(g, i):
        q_, head, _ = pieces[i]
        part = pl.ds(*sets[g])
        return remote(d4.at[q_, part], do_win.at[0, xh, part, k], ex_ss.at[g, i], ex_rs.at[g, i], (c, head))

    def piece_across(g, i):
        q_, head, _ = pieces[i]
        part = pl.ds(*sets[g])
        return remote(d4.at[q_, part], do_win.at[4, xh, part, k], xs_ss.at[g, i], do_rs.at[g, 4, i], (across, head))

    def piece_along(g, i, slot, yo, src):
        _, _, (xs, ks) = pieces[i]
        part = pl.ds(*sets[g])
        return remote(do_win.at[src, xs, part, ks], do_win.at[slot, xs, part, ks], do_ss.at[g, slot, i],
                      do_rs.at[g, slot, i], (xl * 4 + yo, e))

    def along(g, i, act):
        for o in (1, 3, 2):
            yo = (y + o) % 4

            @pl.when(yo < y)
            def _():
                act(piece_along(g, i, y - yo, yo, 0))

    def along_relay(g, i, act):
        for o in (1, 3, 2):
            yo = (y + o) % 4

            @pl.when((xl == 0) & (yo > y))
            def _():
                act(piece_along(g, i, 4 + y - yo, yo, 4))

    def begin(copy):
        copy.start()

    def project(g):
        first_of, n = sets[g]
        tokens = jnp.concatenate([ag[order[first_of + i]] for i in range(n)], axis=0)
        flat = nt(tokens, w4[...].reshape(512, ag.shape[2])).astype(BF)
        part = slice(first_of, first_of + n)
        for q_ in range(4):
            d4[q_, part] = flat[:, q_ * 128:(q_ + 1) * 128].reshape(n, 64, 128)
        for i in (2, 3, 1):
            piece_copy(g, i).start()

        @pl.when(xl == 1)
        def _():
            for i in (2, 3, 1, 0):
                piece_across(g, i).start()
        do_win[0, xh, part, k] = d4[own_q, part]
        along(g, 0, begin)

    def pass_on(g):
        for i in (1, 2, 3):
            piece_copy(g, i).wait_recv()
            along(g, i, begin)

    def pass_across(g):
        for i in range(4):
            @pl.when(xl == 0)
            def _():
                piece_across(g, i).wait_recv()
            along_relay(g, i, begin)

    def gradient_rows(d):
        halves = []
        for xs in range(2):
            for z_ in range(4):
                away = (z_ + 4 - z) % 4
                halves.append(do_win[d, xs, away + away // 2 - 2 * (away // 3)].reshape(128, 128))
        return jnp.concatenate(halves, axis=0)

    def row_copy(win, ss, rs, d):
        return remote(win.at[0], win.at[d], ss.at[d], rs.at[d], ((c + 8 - d) % 8, e))

    def before(act):
        for d in range(1, 5):
            @pl.when(c >= d)
            def _():
                act(d)

    def later(act):
        for d in range(1, 5):
            @pl.when(c + d <= 7)
            def _():
                act(d)

    project(0)
    middle = jnp.minimum(direct + 3, last_before + 1)
    lax.fori_loop(direct + 1, middle, statistics_step, 0)
    pass_on(0)
    g_up.wait_recv()
    g_up2.start()
    g_down.wait_recv()
    g_down2.start()
    project(1)
    pass_across(0)
    lax.fori_loop(middle, last_before + 1, statistics_step, 0)
    norm = jnp.sum(sum_v[...], axis=0, keepdims=True)
    lse_win[0] = top_v[...] + jnp.log(norm) * math.log2(math.e)
    before(lambda d: row_copy(lse_win, lse_ss, lse_rs, d).start())

    def key_probs(t, d, halves, masked):
        key = c * 1024 + t * 512 + iota((512, 512), 0)
        for h in halves:
            cols = half(h)
            place = (c + d) * 1024 + h * 512 + iota((1, 512), 1)
            allowed = key >= doc_start(place)
            if masked:
                allowed = allowed & (key <= place)
            s = nt(k_win[0, half(t), :], q_win[d, cols, :]) * SCALE2
            p = jnp.where(allowed, jnp.exp2(s - lse_win[d, 0:1, cols]), 0.0)
            pt_v[t, d, :, cols] = p.astype(BF)

    def query_tiles(d, act):
        if d == 0:
            act(0, 0, range(2))
            act(1, 0, range(1, 2))
        elif d == 4:
            act(0, 4, range(1))
            act(1, 4, range(2))
        else:
            act(0, d, range(2))
            act(1, d, range(2))

    def nth(n):
        return jnp.where(n < 3 - y, n + 1, 7 - y - n)

    def probs_step(n, _):
        d = nth(n)

        @pl.when(d <= last_after)
        def _():
            received(q_copy(d, (c, e)))
            row_copy(lse_win, lse_ss, lse_rs, d).wait_recv()
            query_tiles(1, lambda t, _, halves: key_probs(t, d, halves, False))

        @pl.when((d == 4) & (xl == 0))
        def _():
            row_copy(lse_win, lse_ss, lse_rs, 4).wait_recv()
            query_tiles(4, lambda t, d, halves: key_probs(t, d, halves, False))
        return 0

    last_after = jnp.minimum(7 - c, 3)
    query_tiles(0, lambda t, d, halves: key_probs(t, d, halves, True))
    pass_on(1)
    g_up2.wait_recv()
    g_down2.wait_recv()
    project(2)
    pass_across(1)
    lax.fori_loop(0, 1, probs_step, 0)
    pass_on(2)
    pass_across(2)

    d_own = gradient_rows(0)
    prod = d_own.astype(F32) * jnp.transpose(o_v[...] / norm)
    high = prod.astype(BF)
    low_part = (prod - high.astype(F32)).astype(BF)
    ones = jnp.ones((8, 128), BF)
    delta_win[0] = nt(ones, high) + nt(ones, low_part)
    before(lambda d: row_copy(delta_win, dl_ss, dl_rs, d).start())
    lax.fori_loop(1, 4, probs_step, 0)

    dq_v[...] = jnp.zeros((128, 1024), F32)

    def query_grads(d):
        flipped = jnp.transpose(k_win[d])
        for t in range(2):
            cols = half(t)
            do = d_own[cols, :]
            acc = dq_v[:, cols]
            fade = jnp.exp2(tops_v[d, 0:1, cols] - lse_win[0, 0:1, cols])
            faded_delta = delta_win[0, 0:1, cols] * fade
            halves = key_halves(t, d)
            rows = slice(halves[0] * 512, halves[-1] * 512 + 512)
            dp = nt(v_win[d, rows, :], do)
            kept = kept_probs(d, rows.start, rows.stop - rows.start, cols)[...]
            ds = kept.astype(F32) * (dp * fade - faded_delta)
            acc = acc + mm(flipped[:, rows], ds.astype(BF))
            dq_v[:, cols] = acc

    def query_step(d, _):
        query_grads(d)
        return 0

    query_grads(0)
    lax.fori_loop(1, last_before + 1, query_step, 0)

    @pl.when(xl == 1)
    def _():
        query_grads(4)
    dq_out[...] = (jnp.transpose(dq_v[...]) * SCALE).astype(BF)

    dk_v[...] = jnp.zeros((1024, 128), F32)
    dv_v[...] = jnp.zeros((1024, 128), F32)

    def key_grads(t, d, halves, do_all):
        rows = half(t)
        cols = slice(halves[0] * 512, halves[-1] * 512 + 512)
        do = do_all[cols, :]
        p = pt_v[t, d, :, cols]
        dv_v[rows, :] += mm(p, do)
        ds = p.astype(F32) * (nt(v_win[0, rows, :], do) - delta_win[d, 0:1, cols])
        dk_v[rows, :] += mm(ds.astype(BF), q_win[d, cols, :])

    query_tiles(0, functools.partial(key_grads, do_all=d_own))

    def grads_step(n, _):
        d = nth(n)

        @pl.when(d <= last_after)
        def _():
            for g in range(3):
                for i in range(4):
                    piece_along(g, i, d, y, 0).wait_recv()
            row_copy(delta_win, dl_ss, dl_rs, d).wait_recv()
            do_all = gradient_rows(d)
            query_tiles(1, lambda t, _, halves: key_grads(t, d, halves, do_all))

        @pl.when((d == 4) & (xl == 0))
        def _():
            row_copy(delta_win, dl_ss, dl_rs, 4).wait_recv()
            query_tiles(4, functools.partial(key_grads, do_all=gradient_rows(4)))
        return 0

    lax.fori_loop(0, 4, grads_step, 0)
    dk_out[...] = (dk_v[...] * SCALE).astype(BF)
    dv_out[...] = dv_v[...].astype(BF)

    recv(dgr, t_rs)
    row, lane = iota((256, 128), 0), iota((256, 128), 1)
    diag = jnp.where(row % 16 == lane, dgr[...].astype(F32), 0.0).astype(BF)
    gather = (iota((16, 256), 1) // 16 == iota((16, 256), 0)).astype(BF)
    d_gates[0] = jnp.transpose(mm(gather, diag))[0:6].astype(BF)

    each(1, 16, lambda d: x_copy(d).wait_send())
    each(1, 16, lambda d: g_copy(d).wait_send())
    each(1, 16, lambda d: r_copy(d).wait_send())
    each(1, 16, lambda d: t_copy(d).wait_send())
    each(1, 8, lambda o: c_copy(o).wait_send())
    for copy in [w_mate, w_facing, w_relay, g_up, g_down, g_up2, g_down2]:
        copy.wait_send()
    to_half(sent)
    to_row(sent)
    relay_row(sent, 0)
    relay_row(sent, 1)
    before(lambda d: row_copy(lse_win, lse_ss, lse_rs, d).wait_send())
    before(lambda d: row_copy(delta_win, dl_ss, dl_rs, d).wait_send())
    for g in range(3):
        for i in range(1, 4):
            piece_copy(g, i).wait_send()

        @pl.when(xl == 1)
        def _():
            for i in range(4):
                piece_across(g, i).wait_send()
        for i in range(4):
            along(g, i, lambda copy: copy.wait_send())
            along_relay(g, i, lambda copy: copy.wait_send())


def hand_over(*refs):
    n = len(refs) // 3
    held, sems = refs[2 * n:3 * n], refs[-1]
    reads = [pltpu.make_async_copy(refs[i], held[i], sems.at[i]) for i in range(n)]
    writes = [pltpu.make_async_copy(held[i], refs[n + i], sems.at[n + i]) for i in range(n)]
    for read in reads:
        read.start()
    for read, write in zip(reads, writes):
        read.wait()
        write.start()
    for write in writes:
        write.wait()


def per_device(q_heads, k_heads, v_heads, doc_ids, w_out, hidden_rows, out_grad, picks, gates, w_gate, w_up, w_down):
    vm, hbm = pl.BlockSpec(memory_space=pltpu.VMEM), pl.BlockSpec(memory_space=pl.ANY)
    tok, width = q_heads.shape
    rows, model = hidden_rows.shape
    ff = w_gate.shape[2]
    dma = pltpu.SemaphoreType.DMA

    def low(*shape):
        return pltpu.VMEM(shape, BF)

    def full(*shape):
        return pltpu.VMEM(shape, F32)

    def out(*shape):
        return jax.ShapeDtypeStruct(shape, BF)

    shapes = (out(rows, model), out(1, 6, 16), out(tok, width), out(tok, width), out(tok, width))
    results = pl.pallas_call(
        kernel,
        out_shape=shapes,
        in_specs=[vm] * 5 + [hbm] * 7,
        out_specs=[vm] * 5,
        scratch_shapes=[
            low(2, model, ff), low(ff, model), low(4, 128, model),
            low(256, 768), low(256, 768), low(256, 768), low(256, 768),
            low(96, model), low(96, model), full(96, ff), full(96, ff),
            low(96, ff), low(96, ff), low(96, model),
            low(256, 768), low(256, 768), low(256, 128), low(256, 128),
            low(3, 256, 256), low(4, rows, model), low(4, 4, rows, width),
            pltpu.VMEM((8, 128), jnp.int32), pltpu.VMEM((8, 8, 128), jnp.int32),
            low(5, tok, width), low(5, tok, width), low(5, tok, width), low(5, 2, 4, 2, rows, width),
            full(5, 8, tok), full(5, 8, tok), full(8, tok), full(8, tok), full(128, tok),
            low(2, 5, 512, tok), full(5, 8, tok), full(128, tok), full(tok, 128), full(tok, 128),
            dma((8,)), dma((16,)), dma((16,)), dma((16,)), dma((16,)), dma((16,)), dma((16,)), dma((16,)), dma((16,)),
            dma((8,)), dma((8,)), dma((3,)), dma((3,)), dma((4,)), dma((4,)), dma((3, 4)), dma((3, 4)), dma((3, 4)),
            dma((5, 2)), dma((5, 2)), dma((5,)), dma((5,)), dma((3, 5, 4)), dma((3, 5, 4)),
            dma((5,)), dma((5,)), dma((5,)), dma((5,)),
        ],
        compiler_params=pltpu.CompilerParams(
            collective_id=0, has_side_effects=True, vmem_limit_bytes=60 * 2**20),
        name="backward",
    )(hidden_rows, out_grad, jnp.transpose(picks, (2, 0, 1)), jnp.transpose(gates, (0, 2, 1)), doc_ids.reshape(8, 128),
      w_gate[0], w_up[0], w_down[0], w_out, q_heads, k_heads, v_heads)
    d_hidden, d_gates, d_queries, d_keys, d_values = pl.pallas_call(
        hand_over,
        out_shape=shapes,
        in_specs=[hbm] * 5,
        out_specs=[hbm] * 5,
        scratch_shapes=[pltpu.VMEM(shape.shape, BF) for shape in shapes] + [dma((10,))],
        compiler_params=pltpu.CompilerParams(vmem_limit_bytes=60 * 2**20),
        name="results",
    )(*results)
    return (d_queries, d_keys, d_values, d_hidden, jnp.transpose(d_gates, (0, 2, 1)))


def solution(mesh):
    return jax.shard_map(
        per_device,
        mesh=mesh,
        in_specs=(
            P("ctx", "exp"),
            P("ctx", "exp"),
            P("ctx", "exp"),
            P("ctx"),
            P("exp", None),
            P(("ctx", "exp"), None),
            P(("ctx", "exp"), None),
            P(("ctx", "exp"), None, None),
            P(("ctx", "exp"), None, None),
            P("exp", None, None),
            P("exp", None, None),
            P("exp", None, None),
        ),
        out_specs=(
            P("ctx", "exp"),
            P("ctx", "exp"),
            P("ctx", "exp"),
            P(("ctx", "exp"), None),
            P(("ctx", "exp"), None, None),
        ),
        check_vma=False,
    )
```
